32 devices in a mesh: groups: 2 (over x), tm: 16 (over z, y, core).
Axes of the slice: x: 2, y: 2, z: 4, core: 2. Of those that a mesh axis runs over, the one named last changes fastest.
Arguments:
- sharded_latents: bfloat16 [32, 6144], P('groups', 'tm'), parts along dimension 0, may hold values from -6 to 6
- sample_frame_count: int32 [16], P('groups'), parts along dimension 0, may hold values from 5 to 8, as said below
- entry_kernel: bfloat16 [27, 16, 384], replicated, may hold values from -0.3125 to 0.3125
- entry_bias: float32 [384], replicated, may hold values from -3 to 3
- norm_scale_gain: float32 [384], replicated, may hold values from 0.25 to 1.75
- residual_kernel: bfloat16 [27, 384, 384], P(None, 'tm'), may hold values from -0.0625 to 0.0625
- residual_bias: float32 [384], replicated, may hold values from -3 to 3
Outputs:
- decoded: bfloat16 [128, 6, 16, 384], P(('groups', 'tm')), parts along dimension 0
The draws below stay inside these ranges and needn't reach their ends.
There are 2 independent parts, one for each index of `groups`. The reference program is written for one: setup_inputs(seed, part) draws one part's arguments, and reference() takes and returns one part's arrays. A program takes and returns all parts, laid end to end along the dimension named above; an argument that names none is the same for every part. Nothing has to cross between parts.
Inputs may be any that keep to these rules, and one draw needn't show every extreme that they name: `sample_frame_count`: every sample has more than half of its 8 frames valid; some sample has all of them valid.
All inputs are finite; a program needn't handle non-finite values.
Results may differ from the reference program's by a relative error of at most 0.009.
Values may be sent and summed in bfloat16 or wider, within the bound.
A program may use at most 64 MiB of HBM per device.

```python
import jax
import jax.numpy as jnp
from jax import lax

LATENT_CHANNELS = 16
C = 384
PROMPT_SAMPLES = 8
BLOCK_FRAMES = 4
LATENT_ROWS = 6
LATENT_COLUMNS = 16
FRAME_BLOCKS = 2
FRAMES = 8


def draw_sample_frame_count(key, part):
    first, second = jax.random.split(jax.random.fold_in(key, 7))
    counts = jax.random.randint(first, (PROMPT_SAMPLES,), FRAMES // 2 + 1, FRAMES + 1)
    chosen = jax.random.randint(second, (), 0, PROMPT_SAMPLES)
    return jnp.where(jnp.arange(PROMPT_SAMPLES) == chosen, FRAMES, counts).astype(jnp.int32)


def steps_of(own_key, dims, pieces, least, high):
    loudness = 1.0
    for axis_at, shards_of in pieces:
        draws = jax.random.uniform(jax.random.fold_in(jax.random.fold_in(own_key, 6), axis_at), (shards_of,), jnp.float32, least / len(pieces), high / len(pieces))
        loudness = loudness * jnp.repeat(jnp.exp(draws), dims[axis_at] // shards_of).reshape((-1,) + (1,) * (len(dims) - 1 - axis_at))
    return loudness


def scatter_about(key, dims, deviation, most, shards=(), kind=jnp.bfloat16):
    values = deviation * jax.random.normal(key, dims, jnp.float32)
    if shards:
        values = values * steps_of(key, dims, shards, -0.22, 0.18)
    return jnp.clip(values, -most, most).astype(kind)


def setup_inputs(seed: int = 0, part: int = 0) -> dict:
    seeds = jax.random.split(jax.random.key(seed), 8)
    part_splits = jax.random.split(jax.random.fold_in(seeds[7], part), 8)
    sharded_latents = scatter_about(part_splits[0], (FRAME_BLOCKS * PROMPT_SAMPLES, BLOCK_FRAMES * LATENT_CHANNELS * LATENT_ROWS * LATENT_COLUMNS), 1.0, 6.0, ((1, 16),))
    sample_frame_count = draw_sample_frame_count(jax.random.fold_in(jax.random.fold_in(seeds[7], part), 71), part)
    entry_kernel = scatter_about(seeds[2], (27, LATENT_CHANNELS, C), (27 * LATENT_CHANNELS) ** -0.5, 0.3125)
    entry_bias = scatter_about(seeds[3], (C,), 0.5, 3.0, (), jnp.float32)
    norm_scale_gain = jnp.clip(1.0 + 0.15 * jax.random.normal(seeds[4], (C,), jnp.float32), 0.25, 1.75)
    residual_kernel = scatter_about(seeds[5], (27, C, C), (27 * C) ** -0.5, 0.0625, ((1, 16),))
    residual_bias = scatter_about(seeds[6], (C,), 0.5, 3.0, (), jnp.float32)
    return {"sharded_latents": sharded_latents, "sample_frame_count": sample_frame_count, "entry_kernel": entry_kernel, "entry_bias": entry_bias, "norm_scale_gain": norm_scale_gain, "residual_kernel": residual_kernel, "residual_bias": residual_bias}


def causal_conv(frames, weight):
    frames_out = frames.shape[0] - 2
    inputs = frames.shape[3]
    padded = jnp.pad(frames, ((0, 0), (1, 1), (1, 1), (0, 0)))
    total = jnp.zeros((frames_out * LATENT_ROWS * LATENT_COLUMNS, weight.shape[2]), jnp.float32)
    for time_tap in range(3):
        for row_tap in range(3):
            for col_tap in range(3):
                window = padded[time_tap:time_tap + frames_out, row_tap:row_tap + LATENT_ROWS, col_tap:col_tap + LATENT_COLUMNS, :]
                window = window.reshape(frames_out * LATENT_ROWS * LATENT_COLUMNS, inputs)
                tap = 9 * time_tap + 3 * row_tap + col_tap
                total = total + jnp.dot(window, weight[tap], preferred_element_type=jnp.float32)
    return total

def activate(stream, norm_scale_gain):
    values = stream.astype(jnp.float32)
    scale = lax.rsqrt(lax.optimization_barrier(jnp.mean(values * values, axis=-1, keepdims=True)) + 1e-06)
    return jax.nn.silu(values * scale * norm_scale_gain).astype(jnp.bfloat16)

def reference(sharded_latents, sample_frame_count, entry_kernel, entry_bias, norm_scale_gain, residual_kernel, residual_bias):
    latent_volume = sharded_latents.reshape(FRAME_BLOCKS, PROMPT_SAMPLES, BLOCK_FRAMES, LATENT_CHANNELS, LATENT_ROWS, LATENT_COLUMNS)
    latent_volume = jnp.transpose(latent_volume, (1, 0, 2, 4, 5, 3)).reshape(PROMPT_SAMPLES, FRAMES, LATENT_ROWS, LATENT_COLUMNS, LATENT_CHANNELS)

    def decode(inputs):
        sample, count = inputs
        frames = jnp.concatenate([jnp.zeros((2, LATENT_ROWS, LATENT_COLUMNS, LATENT_CHANNELS), sample.dtype), sample], axis=0)
        stream = (causal_conv(frames, entry_kernel) + entry_bias).astype(jnp.bfloat16)
        active = activate(stream, norm_scale_gain).reshape(FRAMES, LATENT_ROWS, LATENT_COLUMNS, C)
        extended = jnp.concatenate([jnp.zeros((2, LATENT_ROWS, LATENT_COLUMNS, C), active.dtype), active], axis=0)
        branch = causal_conv(extended, residual_kernel) + residual_bias
        total = (stream.astype(jnp.float32) + branch).reshape(FRAMES, LATENT_ROWS, LATENT_COLUMNS, C)
        valid = (jnp.arange(FRAMES) < count)[:, None, None, None]
        return jnp.where(valid, total, jnp.zeros_like(total)).astype(jnp.bfloat16)
    result = lax.map(decode, (latent_volume, sample_frame_count))
    result = result.reshape(PROMPT_SAMPLES, FRAME_BLOCKS, BLOCK_FRAMES, LATENT_ROWS, LATENT_COLUMNS, C)
    result = jnp.transpose(result, (1, 0, 2, 3, 4, 5))
    return result.reshape(PROMPT_SAMPLES * FRAMES, LATENT_ROWS, LATENT_COLUMNS, C)
```

```python
import jax
import jax.numpy as jnp
from jax import lax
from jax.experimental import pallas as pl
from jax.experimental.pallas import tpu as pltpu
from jax.sharding import PartitionSpec as P

LATENT_CHANNELS = 16
C = 384
PROMPT_SAMPLES = 8
BLOCK_FRAMES = 4
LATENT_ROWS = 6
LATENT_COLUMNS = 16


def from_behind(block, axis, distance):
    devices = range(lax.axis_size(axis))
    route = [(i - distance, i) for i in devices if i - distance in devices]
    return lax.ppermute(block, axis, route)


def causal_conv(frames, weight):
    frames_out = frames.shape[0] - 2
    inputs = frames.shape[3]
    padded = jnp.pad(frames, ((0, 0), (1, 1), (1, 1), (0, 0)))
    total = jnp.zeros((frames_out * LATENT_ROWS * LATENT_COLUMNS, weight.shape[2]), jnp.float32)
    for time_tap in range(3):
        for row_tap in range(3):
            for col_tap in range(3):
                window = padded[
                    time_tap : time_tap + frames_out,
                    row_tap : row_tap + LATENT_ROWS,
                    col_tap : col_tap + LATENT_COLUMNS,
                    :,
                ]
                window = window.reshape(frames_out * LATENT_ROWS * LATENT_COLUMNS, inputs)
                tap = 9 * time_tap + 3 * row_tap + col_tap
                total = total + jnp.dot(window, weight[tap], preferred_element_type=jnp.float32)
    return total


def activate(stream, norm_scale_gain):
    values = stream.astype(jnp.float32)
    scale = lax.rsqrt(jnp.mean(values * values, axis=-1, keepdims=True) + 1e-06)
    return jax.nn.silu(values * scale * norm_scale_gain).astype(jnp.bfloat16)


def to_cells(planes):
    return jnp.transpose(
        planes.reshape(planes.shape[0], LATENT_CHANNELS, LATENT_ROWS, LATENT_COLUMNS), (0, 2, 3, 1)
    )


def shards(
    sharded_latents,
    sample_frame_count,
    entry_kernel,
    entry_bias,
    norm_scale_gain,
    residual_kernel,
    residual_bias,
):
    gathered_latents = lax.all_to_all(
        sharded_latents, "tm", split_axis=0, concat_axis=1, tiled=True
    )
    latent_volume = gathered_latents.reshape(
        BLOCK_FRAMES, LATENT_CHANNELS, LATENT_ROWS * LATENT_COLUMNS
    )
    position = lax.axis_index("tm")
    block = position // PROMPT_SAMPLES
    sample = position % PROMPT_SAMPLES
    keep = block > 0
    earlier = from_behind(latent_volume, "tm", PROMPT_SAMPLES)
    earlier = jnp.where(keep, earlier, jnp.zeros_like(earlier))
    frames = to_cells(jnp.concatenate([earlier, latent_volume], axis=0))
    widened = (causal_conv(frames, entry_kernel) + entry_bias).astype(jnp.bfloat16)
    active_all = activate(widened, norm_scale_gain).reshape(
        BLOCK_FRAMES + 2, LATENT_ROWS, LATENT_COLUMNS, C
    )
    behind = jnp.where(keep, active_all[:2], jnp.zeros_like(active_all[:2]))
    extended = jnp.concatenate([behind, active_all[2:]], axis=0)
    stream = widened[2 * LATENT_ROWS * LATENT_COLUMNS :]
    kernel_all = lax.all_gather(residual_kernel, "tm", axis=1, tiled=True)
    branch = causal_conv(extended, kernel_all)
    total = (stream.astype(jnp.float32) + (branch + residual_bias)).reshape(
        BLOCK_FRAMES, LATENT_ROWS, LATENT_COLUMNS, C
    )
    limit = jnp.sum(jnp.where(jnp.arange(PROMPT_SAMPLES) == sample, sample_frame_count, 0))
    frame_index = block * BLOCK_FRAMES + jnp.arange(BLOCK_FRAMES)
    valid = (frame_index < limit)[:, None, None, None]
    return jnp.where(valid, total, jnp.zeros_like(total)).astype(jnp.bfloat16)


MESH = pl.DeviceIdType.MESH
F32, BF16 = jnp.float32, jnp.bfloat16
CELLS = LATENT_ROWS * LATENT_COLUMNS
PLANE = 128
SLICES = 3
CHUNKS = ((0, 8, 12, 7), (8, 3, 6, 3), (11, 3, 0, 3))
LOCAL_TAPS = 14


def place_of(tap):
    if tap >= 12:
        return (0, tap - 12) if tap < 20 else (1, tap - 19)
    if tap >= 6:
        return (tap - 6) // 3, 8 + tap % 3
    return tap // 3, 11 + tap % 3


def section_kernel(
    latq, counts, entry_far, entry_bias_far, gain_far, residual_bias_far, taps_far,
    out,
    entry, entry_bias, gain, residual_bias, lat, at, act, kept, blocks, right, acc, done,
    lat_send, lat_recv, z_send, z_recv, y_send, y_recv, x_send, x_recv, r_send, r_recv,
    d_send, d_recv, c_send, c_recv, o_send, o_recv, own,
):
    x = lax.axis_index("groups")
    me = lax.axis_index("tm")
    z, y, c = me // 4, (me // 2) % 2, me % 2

    def where_(zz, yy, cc):
        return {"tm": zz * 4 + yy * 2 + cc}

    row_peer = {"groups": x, "tm": z * 4 + (1 - y) * 2 + c}
    col_peer = {"groups": 1 - x, "tm": me}
    far_peer = {"groups": 1 - x, "tm": z * 4 + (1 - y) * 2 + c}
    sibling = {"tm": z * 4 + y * 2 + (1 - c)}

    barrier = pltpu.get_barrier_semaphore()
    for step in range(1, 16):
        pl.semaphore_signal(barrier, inc=1, device_id={"tm": lax.rem(me + step, 16)}, device_id_type=MESH)
    for peer in (col_peer, far_peer):
        pl.semaphore_signal(barrier, inc=1, device_id=peer, device_id_type=MESH)
    pl.semaphore_wait(barrier, 17)

    def remote(src, dst, send, recv, device):
        return pltpu.make_async_remote_copy(
            src_ref=src, dst_ref=dst, send_sem=send, recv_sem=recv, device_id=device, device_id_type=MESH
        )

    def columns(n):
        return pl.ds(pl.multiple_of(128 * n, 128), 128)

    def raw(part, ch, n):
        _, count, first, step = CHUNKS[ch]
        return taps_far.at[pl.ds(first + step * part, count), :, columns(n)]

    def block(part, ch, zz, yy, cc):
        low, count, _, _ = CHUNKS[ch]
        return blocks.at[part, pl.ds(low, count), zz * 4 + yy * 2 + cc]

    def lat_copy(to):
        return remote(latq.at[to % 4], lat.at[me], lat_send.at[to], lat_recv.at[me], {"tm": to})

    def z_copy(ch, n):
        return remote(raw(x, ch, n), block(x, ch, z, y, c), z_send.at[ch, n], z_recv.at[ch, z], where_(n, y, c))

    def z_arrival(ch, zz):
        b = block(x, ch, zz, y, c)
        return remote(b, b, z_send.at[ch, 0], z_recv.at[ch, zz], where_(zz, y, c))

    def y_copy(ch, zz, part=None, source=None):
        at_ = zz if part is None else 4
        b = block(x if part is None else part, ch, zz, y, c)
        return remote(b if source is None else source, b, y_send.at[ch, at_], y_recv.at[ch, at_], row_peer)

    def y_arrival(ch, zz, part=None):
        at_ = zz if part is None else 4
        b = block(x if part is None else part, ch, zz, 1 - y, c)
        return remote(b, b, y_send.at[ch, at_], y_recv.at[ch, at_], row_peer)

    def x_copy(ch, zz):
        b = block(x, ch, zz, y, c)
        return remote(b, b, x_send.at[ch, zz], x_recv.at[ch, zz], col_peer)

    def x_arrival(ch, zz):
        b = block(1 - x, ch, zz, y, c)
        return remote(b, b, x_send.at[ch, zz], x_recv.at[ch, zz], col_peer)

    def r_copy(zz):
        b = block(x, 0, zz, 1 - y, c)
        return remote(b, b, r_send.at[zz], r_recv.at[zz], col_peer)

    def r_arrival(zz):
        b = block(1 - x, 0, zz, 1 - y, c)
        return remote(b, b, r_send.at[zz], r_recv.at[zz], col_peer)

    def d_copy(ch, zz):
        b = block(x, ch, zz, y, c)
        return remote(b, b, d_send.at[ch - 1, zz], d_recv.at[ch - 1, zz], far_peer)

    def d_arrival(ch, zz):
        b = block(1 - x, ch, zz, 1 - y, c)
        return remote(b, b, d_send.at[ch - 1, zz], d_recv.at[ch - 1, zz], far_peer)

    def c_copy(ch, part, zz, yy, source=None):
        b = block(part, ch, zz, yy, c)
        return remote(
            b if source is None else source, b, c_send.at[ch, part, zz, yy], c_recv.at[ch, part, zz, yy], sibling
        )

    def c_arrival(ch, part, zz, yy):
        b = block(part, ch, zz, yy, 1 - c)
        return remote(b, b, c_send.at[ch, part, zz, yy], c_recv.at[ch, part, zz, yy], sibling)

    def o_copy(d):
        return remote(done.at[d], out.at[:, columns(z)], o_send.at[d], o_recv.at[z], where_(d, y, c))

    def o_arrival(n):
        return remote(done.at[0], out.at[:, columns(n)], o_send.at[0], o_recv.at[n], where_(n, y, c))

    for to in range(12):
        @pl.when(to != me)
        def _():
            lat_copy(to).start()

    for ch in range(3):
        for n in range(SLICES):
            @pl.when(n != z)
            def _():
                z_copy(ch, n).start()

    @pl.when(z < SLICES)
    def _():
        for ch in range(3):
            y_copy(ch, z, None, raw(x, ch, z)).start()
            y_copy(ch, z, 1 - x, raw(1 - x, ch, z)).start()
        for ch in range(3):
            for part in range(2):
                c_copy(ch, part, z, y, raw(part, ch, z)).start()
        mine = [
            pltpu.make_async_copy(latq.at[me % 4], lat.at[me], own.at[0]),
            pltpu.make_async_copy(entry_far, entry, own.at[1]),
            pltpu.make_async_copy(entry_bias_far, entry_bias, own.at[2]),
            pltpu.make_async_copy(gain_far, gain, own.at[3]),
            pltpu.make_async_copy(residual_bias_far, residual_bias, own.at[4]),
        ]
        for ch in range(3):
            for part in range(2):
                mine.append(
                    pltpu.make_async_copy(raw(part, ch, z), block(part, ch, z, y, c), own.at[5 + 2 * ch + part])
                )
        for copy in mine:
            copy.start()

        def near(step):
            at_ = jnp.where(z == 2, 3 - step, step + jnp.where(step >= z, 1, 0))
            at_ = jnp.where((z == 2) & (step == 0), 3, at_)
            return jnp.where((z == 2) & (step > 0), 2 - step, at_)

        def forward(ch, step):
            zz = near(step)
            z_arrival(ch, zz).wait_recv()
            y_copy(ch, zz).start()
            x_copy(ch, zz).start()
            if ch:
                d_copy(ch, zz).start()
            c_copy(ch, x, zz, y).start()

        def from_row_peer(ch):
            y_arrival(ch, z).wait_recv()
            c_copy(ch, x, z, 1 - y).start()
            y_arrival(ch, z, 1 - x).wait_recv()
            c_copy(ch, 1 - x, z, 1 - y).start()
            for step in range(3):
                zz = near(step)
                y_arrival(ch, zz).wait_recv()
                if ch == 0:
                    r_copy(zz).start()
                c_copy(ch, x, zz, 1 - y).start()

        def from_col_peer(ch):
            for step in range(3):
                zz = near(step)
                x_arrival(ch, zz).wait_recv()
                c_copy(ch, 1 - x, zz, y).start()
            for step in range(3):
                zz = near(step)
                if ch == 0:
                    r_arrival(zz).wait_recv()
                else:
                    d_arrival(ch, zz).wait_recv()
                c_copy(ch, 1 - x, zz, 1 - y).start()

        def from_sibling(ch):
            for part in range(2):
                for yy in range(2):
                    for zz in range(4):
                        c_arrival(ch, part, zz, yy).wait_recv()

        at[:, 0:2] = jnp.zeros((2, 2, 144, PLANE), BF16)
        acc[...] = jnp.zeros((2, 10, PLANE, 128), F32)
        for copy in mine[:5]:
            copy.wait()
        for source in range(16):
            @pl.when(source != me)
            def _():
                remote(latq.at[0], lat.at[source], lat_send.at[0], lat_recv.at[source], {"tm": source}).wait_recv()
        forward(0, 0)
        target = lax.broadcasted_iota(jnp.int32, (256, 256), 0)
        origin = lax.broadcasted_iota(jnp.int32, (256, 256), 1)
        h_, b_, g_, ch_ = target // 128, (target // 64) % 2, (target // 16) % 4, target % 16
        perm = (origin == (g_ * 4 + ch_ // 4) * 16 + (b_ * 2 + h_) * 4 + ch_ % 4).astype(F32).astype(BF16)
        cells = jnp.dot(perm, lat[...].reshape(256, PLANE), preferred_element_type=F32)
        lane = lax.broadcasted_iota(jnp.int32, (256, PLANE), 1)
        row, column = lane // LATENT_COLUMNS, lane % LATENT_COLUMNS
        for j in range(3):
            for k in range(3):
                offset = (j - 1) * LATENT_COLUMNS + (k - 1)
                moved = pltpu.roll(cells, (-offset) % PLANE, 1) if offset else cells
                good = (
                    (row + (j - 1) >= 0)
                    & (row + (j - 1) < LATENT_ROWS)
                    & (column + (k - 1) >= 0)
                    & (column + (k - 1) < LATENT_COLUMNS)
                )
                tap = 3 * j + k
                at[:, 2:, tap * 16 : tap * 16 + 16, :] = (
                    jnp.where(good, moved, 0.0).astype(BF16).reshape(2, 8, 16, PLANE)
                )

        def inlet(index):
            h, b = index // 2, index % 2
            left = jnp.concatenate([at[h, 4 * b + q : 4 * b + q + 3].reshape(432, PLANE) for q in range(4)], axis=1)
            wide = lax.dot_general(left, entry[...], (((0,), (0,)), ((), ())), preferred_element_type=F32)
            wide = wide.reshape(4, PLANE, C)[:, :CELLS].reshape(4 * CELLS, C)
            stream = (wide + entry_bias[...][None, :]).astype(BF16)
            kept[4 * index : 4 * index + 4] = stream.reshape(4, CELLS, C)
            values = stream.astype(F32)
            scale = lax.rsqrt(jnp.mean(values * values, axis=-1, keepdims=True) + 1e-06)
            u = values * scale * gain[...][None, :]
            active = (u / (1.0 + jnp.exp(-u))).astype(BF16).astype(F32)
            column = lax.broadcasted_iota(jnp.int32, (4 * CELLS, C), 0) % LATENT_COLUMNS
            rows = slice(4 * b, 4 * b + 4)
            before = jnp.where(column == 0, 0.0, pltpu.roll(active, 1, 0))
            behind = jnp.where(column == LATENT_COLUMNS - 1, 0.0, pltpu.roll(active, 4 * CELLS - 1, 0))
            for k, moved in enumerate((before, active, behind)):
                act[h, rows, :, k * C : k * C + C] = moved.astype(BF16).reshape(4, CELLS, C)

        def prepare(low, high):
            for tap in range(low, high):
                part, local = place_of(tap)
                slot, k = tap // 3, tap % 3
                index = 8 - slot + (1 if slot < 4 else 0)
                piece = blocks[part, local].astype(F32).reshape(C, 128).astype(BF16)
                right[index // 2, k * C : k * C + C, index % 2 * 128 : index % 2 * 128 + 128] = piece

        def sweep(h, tile, slots, frames):
            left = act[h, :frames].reshape(frames * CELLS, 3 * C)
            wide = jnp.dot(left, right[tile, :, : 128 * len(slots)], preferred_element_type=F32)
            for n, slot in enumerate(slots):
                i, j = slot // 3, slot % 3
                part = wide[:, 128 * n : 128 * n + 128].reshape(frames, CELLS, 128)
                acc[h, 2 - i : 2 - i + frames, 16 * (2 - j) : 16 * (2 - j) + CELLS] += part

        inlet(0)
        forward(0, 1)
        forward(0, 2)
        inlet(1)
        for step in range(3):
            forward(1, step)
        from_row_peer(0)
        inlet(2)
        for step in range(3):
            forward(2, step)
        inlet(3)
        from_col_peer(0)
        for copy in mine[5:]:
            copy.wait()
        from_row_peer(1)
        from_sibling(0)
        prepare(12, 27)

        def first(h, carry):
            sweep(h, 0, (8, 7), 8)
            sweep(h, 1, (6, 5), 8)
            sweep(h, 2, (4,), 7)
            return carry

        lax.fori_loop(0, 1, first, 0)
        from_col_peer(1)
        from_row_peer(2)
        lax.fori_loop(1, 2, first, 0)
        from_col_peer(2)
        from_sibling(1)
        prepare(6, 12)

        def second(h, carry):
            sweep(h, 3, (3, 2), 7)
            return carry

        lax.fori_loop(0, 2, second, 0)
        from_sibling(2)
        prepare(0, 6)

        def finish(step, carry):
            h = 1 - step
            sweep(h, 4, (1, 0), 6)
            for b in (1, 0):
                d = 2 * b + h
                stream = kept[pl.ds(h * 8 + b * 4, 4), :, columns(z)].astype(F32)
                total = acc[h, 4 * b : 4 * b + 4, 16 : 16 + CELLS] + residual_bias[columns(z)][None, None, :]
                total = stream + total
                limit = counts[me % 4 + 4 * h]
                valid = lax.broadcasted_iota(jnp.int32, (4, CELLS, 128), 0) + 4 * b < limit
                done[d] = jnp.where(valid, total, 0.0).astype(BF16).reshape(4 * CELLS, 128)

                @pl.when(d != z)
                def _():
                    o_copy(d).start()

            return carry

        lax.fori_loop(0, 2, finish, 0)
        out[:, columns(z)] = done[z]

    for n in range(SLICES):
        @pl.when(n != z)
        def _():
            o_arrival(n).wait_recv()
            for ch in range(3):
                z_copy(ch, n).wait_send()

    for to in range(12):
        @pl.when(to != me)
        def _():
            lat_copy(to).wait_send()

    @pl.when(z < SLICES)
    def _():
        for ch in range(3):
            y_copy(ch, z, 1 - x).wait_send()
            for zz in range(4):
                y_copy(ch, zz).wait_send()

                @pl.when(zz != z)
                def _():
                    x_copy(ch, zz).wait_send()
                    if ch == 0:
                        r_copy(zz).wait_send()
                    else:
                        d_copy(ch, zz).wait_send()

                for part in range(2):
                    for yy in range(2):
                        c_copy(ch, part, zz, yy).wait_send()
        for d in range(4):
            @pl.when(d != z)
            def _():
                o_copy(d).wait_send()


def sliced_shards(
    sharded_latents,
    sample_frame_count,
    entry_kernel,
    entry_bias,
    norm_scale_gain,
    residual_kernel,
    residual_bias,
):
    latq = jnp.transpose(sharded_latents.reshape(4, 4, 4, CELLS), (1, 0, 2, 3)).reshape(4, 16, CELLS)
    latq = jnp.pad(latq, ((0, 0), (0, 0), (0, PLANE - CELLS)))
    vmem = pl.BlockSpec(memory_space=pltpu.VMEM)
    far = pl.BlockSpec(memory_space=pltpu.HBM)
    dma = pltpu.SemaphoreType.DMA
    out = pl.pallas_call(
        section_kernel,
        out_shape=jax.ShapeDtypeStruct((4 * CELLS, C), BF16),
        in_specs=[vmem, pl.BlockSpec(memory_space=pltpu.SMEM)] + [far] * 5,
        out_specs=vmem,
        scratch_shapes=[
            pltpu.VMEM((27 * LATENT_CHANNELS, C), BF16),
            pltpu.VMEM((C,), F32), pltpu.VMEM((C,), F32), pltpu.VMEM((C,), F32),
            pltpu.VMEM((16, 16, PLANE), BF16),
            pltpu.VMEM((2, 10, 144, PLANE), BF16),
            pltpu.VMEM((2, 8, CELLS, 3 * C), BF16),
            pltpu.VMEM((16, CELLS, C), BF16),
            pltpu.VMEM((2, LOCAL_TAPS, 16, 24, 128), BF16),
            pltpu.VMEM((5, 3 * C, 256), BF16),
            pltpu.VMEM((2, 10, PLANE, 128), F32),
            pltpu.VMEM((4, 4 * CELLS, 128), BF16),
            dma((12,)), dma((16,)), dma((3, 3)), dma((3, 4)), dma((3, 5)), dma((3, 5)),
            dma((3, 4)), dma((3, 4)), dma((4,)), dma((4,)), dma((2, 4)), dma((2, 4)),
            dma((3, 2, 4, 2)), dma((3, 2, 4, 2)), dma((4,)), dma((3,)), dma((11,)),
        ],
        compiler_params=pltpu.CompilerParams(
            collective_id=0, has_side_effects=True, vmem_limit_bytes=56 * 1024 * 1024
        ),
        cost_estimate=pl.CostEstimate(flops=5_000_000_000, bytes_accessed=2_000_000, transcendentals=600_000),
    )(
        latq,
        sample_frame_count,
        entry_kernel.reshape(27 * LATENT_CHANNELS, C),
        entry_bias,
        norm_scale_gain,
        residual_bias,
        residual_kernel,
    )
    return out.reshape(4, LATENT_ROWS, LATENT_COLUMNS, C)


def solution(mesh):
    in_specs = (P("groups", "tm"), P("groups"), P(), P(), P(), P(None, "tm", None), P())
    out_specs = P(("groups", "tm"), None, None, None)
    sliced = mesh.shape["groups"] == 2 and mesh.shape["tm"] == 16
    body = sliced_shards if sliced else shards
    return jax.shard_map(body, mesh=mesh, in_specs=in_specs, out_specs=out_specs, check_vma=False)
```

```python
import jax
import jax.numpy as jnp
from jax import lax
from jax.experimental import pallas as pl
from jax.experimental.pallas import tpu as pltpu
from jax.sharding import PartitionSpec as P

LATENT_CHANNELS = 16
C = 384
PROMPT_SAMPLES = 8
BLOCK_FRAMES = 4
LATENT_ROWS = 6
LATENT_COLUMNS = 16


def from_behind(block, axis, distance):
    devices = range(lax.axis_size(axis))
    route = [(i - distance, i) for i in devices if i - distance in devices]
    return lax.ppermute(block, axis, route)


def causal_conv(frames, weight):
    frames_out = frames.shape[0] - 2
    inputs = frames.shape[3]
    padded = jnp.pad(frames, ((0, 0), (1, 1), (1, 1), (0, 0)))
    total = jnp.zeros((frames_out * LATENT_ROWS * LATENT_COLUMNS, weight.shape[2]), jnp.float32)
    for time_tap in range(3):
        for row_tap in range(3):
            for col_tap in range(3):
                window = padded[
                    time_tap : time_tap + frames_out,
                    row_tap : row_tap + LATENT_ROWS,
                    col_tap : col_tap + LATENT_COLUMNS,
                    :,
                ]
                window = window.reshape(frames_out * LATENT_ROWS * LATENT_COLUMNS, inputs)
                tap = 9 * time_tap + 3 * row_tap + col_tap
                total = total + jnp.dot(window, weight[tap], preferred_element_type=jnp.float32)
    return total


def activate(stream, norm_scale_gain):
    values = stream.astype(jnp.float32)
    scale = lax.rsqrt(jnp.mean(values * values, axis=-1, keepdims=True) + 1e-06)
    return jax.nn.silu(values * scale * norm_scale_gain).astype(jnp.bfloat16)


def to_cells(planes):
    return jnp.transpose(
        planes.reshape(planes.shape[0], LATENT_CHANNELS, LATENT_ROWS, LATENT_COLUMNS), (0, 2, 3, 1)
    )


def shards(
    sharded_latents,
    sample_frame_count,
    entry_kernel,
    entry_bias,
    norm_scale_gain,
    residual_kernel,
    residual_bias,
):
    gathered_latents = lax.all_to_all(
        sharded_latents, "tm", split_axis=0, concat_axis=1, tiled=True
    )
    latent_volume = gathered_latents.reshape(
        BLOCK_FRAMES, LATENT_CHANNELS, LATENT_ROWS * LATENT_COLUMNS
    )
    position = lax.axis_index("tm")
    block = position // PROMPT_SAMPLES
    sample = position % PROMPT_SAMPLES
    keep = block > 0
    earlier = from_behind(latent_volume, "tm", PROMPT_SAMPLES)
    earlier = jnp.where(keep, earlier, jnp.zeros_like(earlier))
    frames = to_cells(jnp.concatenate([earlier, latent_volume], axis=0))
    widened = (causal_conv(frames, entry_kernel) + entry_bias).astype(jnp.bfloat16)
    active_all = activate(widened, norm_scale_gain).reshape(
        BLOCK_FRAMES + 2, LATENT_ROWS, LATENT_COLUMNS, C
    )
    behind = jnp.where(keep, active_all[:2], jnp.zeros_like(active_all[:2]))
    extended = jnp.concatenate([behind, active_all[2:]], axis=0)
    stream = widened[2 * LATENT_ROWS * LATENT_COLUMNS :]
    kernel_all = lax.all_gather(residual_kernel, "tm", axis=1, tiled=True)
    branch = causal_conv(extended, kernel_all)
    total = (stream.astype(jnp.float32) + (branch + residual_bias)).reshape(
        BLOCK_FRAMES, LATENT_ROWS, LATENT_COLUMNS, C
    )
    limit = jnp.sum(jnp.where(jnp.arange(PROMPT_SAMPLES) == sample, sample_frame_count, 0))
    frame_index = block * BLOCK_FRAMES + jnp.arange(BLOCK_FRAMES)
    valid = (frame_index < limit)[:, None, None, None]
    return jnp.where(valid, total, jnp.zeros_like(total)).astype(jnp.bfloat16)


MESH = pl.DeviceIdType.MESH
F32, BF16 = jnp.float32, jnp.bfloat16
CELLS = LATENT_ROWS * LATENT_COLUMNS
PLANE = 128
HALF = 64
SLICES = 3
PAIRS = ((8, 7), (6, 5), (4, 3), (2, 1), (0, 0))
CHUNKS = ((0, 1), (2, 3), (4,))


def section_kernel(
    lat_far, counts, entry_far, entry_bias_far, gain_far, residual_bias_far, taps_far,
    out,
    entry, entry_bias, gain, residual_bias, lat_raw, taps, latq, lat, at, act, kept,
    piece_a, piece_b, piece_c, block_a, block_b, block_c, right, acc, done, got,
    lat_send, lat_recv, z_send, z_recv, y_send, y_recv, c_send, c_recv, o_send, o_recv, own,
):
    x = lax.axis_index("groups")
    me = lax.axis_index("tm")
    z, y, c = me // 4, (me // 2) % 2, me % 2
    pieces = (piece_a, piece_b, piece_c)
    blocks = (block_a, block_b, block_c)

    barrier = pltpu.get_barrier_semaphore()
    for step in range(1, 16):
        pl.semaphore_signal(barrier, inc=1, device_id={"tm": lax.rem(me + step, 16)}, device_id_type=MESH)
    for step in range(16):
        pl.semaphore_signal(
            barrier, inc=1, device_id={"groups": 1 - x, "tm": lax.rem(me + step, 16)}, device_id_type=MESH
        )

    first_copies = [
        pltpu.make_async_copy(lat_far, lat_raw, own.at[0]),
        pltpu.make_async_copy(taps_far, taps, own.at[1]),
        pltpu.make_async_copy(entry_far, entry, own.at[2]),
        pltpu.make_async_copy(entry_bias_far, entry_bias, own.at[3]),
        pltpu.make_async_copy(gain_far, gain, own.at[4]),
        pltpu.make_async_copy(residual_bias_far, residual_bias, own.at[5]),
    ]
    for copy in first_copies:
        copy.start()
    first_copies[0].wait()
    cell_rows = lat_raw[...].astype(F32)
    quads = [cell_rows[:, CELLS * q : CELLS * q + CELLS] for q in range(4)]
    quads = jnp.concatenate([jnp.concatenate([q, jnp.zeros((16, PLANE - CELLS), F32)], axis=1) for q in quads], axis=0)
    to_ = lax.broadcasted_iota(jnp.int32, (64, 64), 0)
    from_ = lax.broadcasted_iota(jnp.int32, (64, 64), 1)
    pick = from_ == (to_ % 4) * 16 + ((to_ % 16) // 8) * 8 + ((to_ // 4) % 2) * 4 + to_ // 16
    picked = jnp.dot(pick.astype(F32).astype(BF16), quads.astype(BF16), preferred_element_type=F32)
    latq[...] = picked.astype(BF16).reshape(4, 16, PLANE)
    first_copies[1].wait()
    keeps = (lax.broadcasted_iota(jnp.int32, (24, 128), 1) < HALF) == (x == 0)
    for ch, pairs in enumerate(CHUNKS):
        for n, p in enumerate(pairs):
            low, high = PAIRS[p]
            for k in range(3):
                for s in range(SLICES):
                    a = taps[3 * low + k, :, 128 * s : 128 * s + 128].astype(F32)
                    b = taps[3 * high + k, :, 128 * s : 128 * s + 128].astype(F32)
                    still = jnp.where(x == 0, a, b)
                    moved = pltpu.roll(jnp.where(x == 0, b, a), HALF, 1)
                    pieces[ch][s, 3 * n + k] = jnp.where(keeps, still, moved).astype(BF16)
    pl.semaphore_wait(barrier, 31)

    def remote(src, dst, send, recv, device):
        return pltpu.make_async_remote_copy(
            src_ref=src, dst_ref=dst, send_sem=send, recv_sem=recv, device_id=device, device_id_type=MESH
        )

    def columns(n):
        return pl.ds(pl.multiple_of(128 * n, 128), 128)

    def source_of(zz, yy, cc):
        return zz * 4 + yy * 2 + cc

    def lat_copy(g, to):
        return remote(
            latq.at[to % 4], lat.at[x, me], lat_send.at[g, to], lat_recv.at[x, me], {"groups": g, "tm": to}
        )

    def z_copy(ch, n):
        return remote(
            pieces[ch].at[n], blocks[ch].at[me], z_send.at[ch, n], z_recv.at[ch, z], {"tm": source_of(n, y, c)}
        )

    def z_arrival(ch, zz):
        b = blocks[ch].at[source_of(zz, y, c)]
        return remote(b, b, z_send.at[ch, 0], z_recv.at[ch, zz], {"tm": source_of(zz, y, c)})

    def y_copy(ch, zz, source=None):
        b = blocks[ch].at[source_of(zz, y, c)]
        return remote(
            b if source is None else source, b, y_send.at[ch, zz], y_recv.at[ch, zz], {"tm": source_of(z, 1 - y, c)}
        )

    def y_arrival(ch, zz):
        b = blocks[ch].at[source_of(zz, 1 - y, c)]
        return remote(b, b, y_send.at[ch, zz], y_recv.at[ch, zz], {"tm": source_of(z, 1 - y, c)})

    def c_copy(ch, zz, yy, source=None):
        b = blocks[ch].at[source_of(zz, yy, c)]
        return remote(
            b if source is None else source, b, c_send.at[ch, zz, yy], c_recv.at[ch, zz, yy],
            {"tm": source_of(z, y, 1 - c)},
        )

    def c_arrival(ch, zz, yy):
        b = blocks[ch].at[source_of(zz, yy, 1 - c)]
        return remote(b, b, c_send.at[ch, zz, yy], c_recv.at[ch, zz, yy], {"tm": source_of(z, y, 1 - c)})

    def o_copy(g, h, b):
        return remote(
            done.at[g, h, b], got.at[z, x], o_send.at[g, h, b], o_recv.at[z, x],
            {"groups": g, "tm": source_of(2 * b + h, y, c)},
        )

    def o_arrival(n, xx):
        return remote(
            done.at[0, 0, 0], got.at[n, xx], o_send.at[0, 0, 0], o_recv.at[n, xx],
            {"groups": xx, "tm": source_of(n, y, c)},
        )

    for to in range(12):
        for g in range(2):
            @pl.when((to != me) | (g != x))
            def _():
                lat_copy(g, to).start()

    for ch in range(3):
        for n in range(SLICES):
            @pl.when(n != z)
            def _():
                z_copy(ch, n).start()

    @pl.when(z < SLICES)
    def _():
        mine = [pltpu.make_async_copy(latq.at[me % 4], lat.at[x, me], own.at[6])]
        for ch in range(3):
            y_copy(ch, z, pieces[ch].at[z]).start()
            c_copy(ch, z, y, pieces[ch].at[z]).start()
            mine.append(pltpu.make_async_copy(pieces[ch].at[z], blocks[ch].at[me], own.at[7 + ch]))
        for copy in mine:
            copy.start()

        def near(step):
            at_ = jnp.where(z == 2, 3 - step, step + jnp.where(step >= z, 1, 0))
            at_ = jnp.where((z == 2) & (step == 0), 3, at_)
            return jnp.where((z == 2) & (step > 0), 2 - step, at_)

        def forward(ch, step):
            zz = near(step)
            z_arrival(ch, zz).wait_recv()
            y_copy(ch, zz).start()
            c_copy(ch, zz, y).start()

        def from_row_peer(ch):
            y_arrival(ch, z).wait_recv()
            c_copy(ch, z, 1 - y).start()
            for step in range(3):
                zz = near(step)
                y_arrival(ch, zz).wait_recv()
                c_copy(ch, zz, 1 - y).start()

        def from_sibling(ch):
            for yy in range(2):
                for zz in range(4):
                    c_arrival(ch, zz, yy).wait_recv()

        at[:, 0:2] = jnp.zeros((4, 2, 144, PLANE), BF16)

        def clear(n, carry):
            acc[n // 4, n % 4] = jnp.zeros((10, PLANE, 128), F32)
            return carry

        lax.fori_loop(0, 8, clear, 0)
        for copy in first_copies[2:]:
            copy.wait()
        for copy in mine:
            copy.wait()
        for g in range(2):
            for source in range(16):
                @pl.when((source != me) | (g != x))
                def _():
                    remote(
                        latq.at[0], lat.at[g, source], lat_send.at[0, 0], lat_recv.at[g, source],
                        {"groups": g, "tm": source},
                    ).wait_recv()
        forward(0, 0)
        target = lax.broadcasted_iota(jnp.int32, (256, 256), 0)
        origin = lax.broadcasted_iota(jnp.int32, (256, 256), 1)
        h_, b_, g_, ch_ = target // 128, (target // 64) % 2, (target // 16) % 4, target % 16
        perm = (origin == (g_ * 4 + ch_ // 4) * 16 + (b_ * 2 + h_) * 4 + ch_ % 4).astype(F32).astype(BF16)
        lane = lax.broadcasted_iota(jnp.int32, (256, PLANE), 1)
        row, column = lane // LATENT_COLUMNS, lane % LATENT_COLUMNS

        def spread(g, carry):
            cells = jnp.dot(perm, lat[g].reshape(256, PLANE), preferred_element_type=F32)
            for j in range(3):
                for k in range(3):
                    offset = (j - 1) * LATENT_COLUMNS + (k - 1)
                    moved = pltpu.roll(cells, (-offset) % PLANE, 1) if offset else cells
                    good = (
                        (row + (j - 1) >= 0)
                        & (row + (j - 1) < LATENT_ROWS)
                        & (column + (k - 1) >= 0)
                        & (column + (k - 1) < LATENT_COLUMNS)
                    )
                    tap = 3 * j + k
                    at[pl.ds(2 * g, 2), 2:, tap * 16 : tap * 16 + 16, :] = (
                        jnp.where(good, moved, 0.0).astype(BF16).reshape(2, 8, 16, PLANE)
                    )
            return carry

        def inlet(index, carry):
            h, b = index // 2, index % 2
            left = jnp.concatenate([at[h, pl.ds(4 * b + q, 3)].reshape(432, PLANE) for q in range(4)], axis=1)
            wide = lax.dot_general(left, entry[...], (((0,), (0,)), ((), ())), preferred_element_type=F32)
            wide = wide.reshape(4, PLANE, C)[:, :CELLS].reshape(4 * CELLS, C)
            stream = (wide + entry_bias[...][None, :]).astype(BF16)
            kept[index] = stream
            values = stream.astype(F32)
            scale = lax.rsqrt(jnp.mean(values * values, axis=-1, keepdims=True) + 1e-06)
            u = values * scale * gain[...][None, :]
            active = (u / (1.0 + jnp.exp(-u))).astype(BF16).astype(F32)
            column = lax.broadcasted_iota(jnp.int32, (4 * CELLS, C), 0) % LATENT_COLUMNS
            before = jnp.where(column == 0, 0.0, pltpu.roll(active, 1, 0))
            behind = jnp.where(column == LATENT_COLUMNS - 1, 0.0, pltpu.roll(active, 4 * CELLS - 1, 0))
            for k, moved in enumerate((before, active, behind)):
                act[h, pl.ds(4 * b, 4), :, k * C : k * C + C] = moved.astype(BF16).reshape(4, CELLS, C)
            return carry

        def prepare(ch):
            for n in range(len(CHUNKS[ch])):
                for k in range(3):
                    piece = blocks[ch][:, 3 * n + k].astype(F32).reshape(C, 128).astype(BF16)
                    right[ch, k * C : k * C + C, n * 128 : n * 128 + 128] = piece

        def sweep(h, ch, frames):
            pairs = CHUNKS[ch]
            left = act[h, :frames].reshape(frames * CELLS, 3 * C)
            wide = jnp.dot(left, right[ch, :, : 128 * len(pairs)], preferred_element_type=F32)
            for n, p in enumerate(pairs):
                part = wide[:, 128 * n : 128 * n + 128].reshape(frames, CELLS, 128)
                for side in range(1 if p == 4 else 2):
                    i, j = PAIRS[p][side] // 3, PAIRS[p][side] % 3
                    acc[side, h, 2 - i : 2 - i + frames, 16 * (2 - j) : 16 * (2 - j) + CELLS] += part

        lax.fori_loop(0, 2, spread, 0)
        lax.fori_loop(0, 2, inlet, 0)
        forward(0, 1)
        forward(0, 2)
        lax.fori_loop(2, 4, inlet, 0)
        for step in range(3):
            forward(1, step)
        from_row_peer(0)
        lax.fori_loop(4, 6, inlet, 0)
        for step in range(3):
            forward(2, step)
        lax.fori_loop(6, 8, inlet, 0)
        from_row_peer(1)
        from_sibling(0)
        prepare(0)

        def first(h, carry):
            sweep(h, 0, 8)
            return carry

        lax.fori_loop(0, 2, first, 0)
        from_row_peer(2)
        lax.fori_loop(2, 4, first, 0)
        from_sibling(1)
        prepare(1)
        from_sibling(2)
        prepare(2)
        edge = lax.broadcasted_iota(jnp.int32, (2, CELLS, 128), 2) < HALF
        bias = residual_bias[columns(z)][None, :]
        bias = jnp.where(x == 0, bias, pltpu.roll(jnp.broadcast_to(bias, (8, 128)), HALF, 1)[:1])

        def finish(step, carry):
            g, h = step % 2, 1 - step // 2
            gh = 2 * g + h
            sweep(gh, 1, 7)
            sweep(gh, 2, 6)
            for b in (1, 0):
                stream = kept[2 * gh + b, :, columns(z)].astype(F32)
                stream = jnp.where(x == 0, stream, pltpu.roll(stream, HALF, 1))
                even = acc[0, gh, 4 * b : 4 * b + 4, 16 : 16 + CELLS].reshape(4 * CELLS, 128)
                odd = acc[1, gh, 4 * b : 4 * b + 4, 16 : 16 + CELLS].reshape(4 * CELLS, 128)
                total = stream + (even + pltpu.roll(odd, HALF, 1) + bias)
                top = total[: 2 * CELLS].reshape(2, CELLS, 128)
                low = pltpu.roll(total[2 * CELLS :], HALF, 1).reshape(2, CELLS, 128)
                done[g, h, b] = jnp.where(edge, top, low).astype(BF16).reshape(2 * CELLS, 128)

                @pl.when((g != x) | (2 * b + h != z))
                def _():
                    o_copy(g, h, b).start()

            return carry

        lax.fori_loop(0, 4, finish, 0)
        got[z, x] = done[x, z % 2, z // 2]

    for n in range(SLICES):
        for xx in range(2):
            @pl.when((n != z) | (xx != x))
            def _():
                o_arrival(n, xx).wait_recv()
    limit = counts[me % PROMPT_SAMPLES]
    frame = lax.broadcasted_iota(jnp.int32, (2, CELLS, 128), 0) + BLOCK_FRAMES * (me // PROMPT_SAMPLES)
    half = lax.broadcasted_iota(jnp.int32, (2, CELLS, 128), 2) < HALF
    for n in range(SLICES):
        near_half = got[n, 0].astype(F32)
        far_half = got[n, 1].astype(F32)
        top = jnp.where(half, near_half.reshape(2, CELLS, 128), pltpu.roll(far_half, HALF, 1).reshape(2, CELLS, 128))
        low = jnp.where(half, pltpu.roll(near_half, HALF, 1).reshape(2, CELLS, 128), far_half.reshape(2, CELLS, 128))
        for first_frame, values in ((0, top), (2, low)):
            values = jnp.where(frame + first_frame < limit, values, 0.0).astype(BF16)
            out[CELLS * first_frame : CELLS * (first_frame + 2), 128 * n : 128 * n + 128] = values.reshape(2 * CELLS, 128)

    @pl.when(z == SLICES)
    def _():
        for copy in first_copies[2:]:
            copy.wait()

    for n in range(SLICES):
        @pl.when(n != z)
        def _():
            for ch in range(3):
                z_copy(ch, n).wait_send()

    for to in range(12):
        for g in range(2):
            @pl.when((to != me) | (g != x))
            def _():
                lat_copy(g, to).wait_send()

    @pl.when(z < SLICES)
    def _():
        for ch in range(3):
            for zz in range(4):
                y_copy(ch, zz).wait_send()
                for yy in range(2):
                    c_copy(ch, zz, yy).wait_send()
        for g in range(2):
            for h in range(2):
                for b in range(2):
                    @pl.when((g != x) | (2 * b + h != z))
                    def _():
                        o_copy(g, h, b).wait_send()


def sliced_shards(
    sharded_latents,
    sample_frame_count,
    entry_kernel,
    entry_bias,
    norm_scale_gain,
    residual_kernel,
    residual_bias,
):
    vmem = pl.BlockSpec(memory_space=pltpu.VMEM)
    far = pl.BlockSpec(memory_space=pltpu.HBM)
    dma = pltpu.SemaphoreType.DMA
    pairs = [3 * len(chunk) for chunk in CHUNKS]
    out = pl.pallas_call(
        section_kernel,
        out_shape=jax.ShapeDtypeStruct((4 * CELLS, C), BF16),
        in_specs=[far, pl.BlockSpec(memory_space=pltpu.SMEM)] + [far] * 5,
        out_specs=vmem,
        scratch_shapes=[
            pltpu.VMEM((27 * LATENT_CHANNELS, C), BF16),
            pltpu.VMEM((C,), F32), pltpu.VMEM((C,), F32), pltpu.VMEM((C,), F32),
            pltpu.VMEM((16, 4 * CELLS), BF16),
            pltpu.VMEM((27, 24, C), BF16),
            pltpu.VMEM((4, 16, PLANE), BF16),
            pltpu.VMEM((2, 16, 16, PLANE), BF16),
            pltpu.VMEM((4, 10, 144, PLANE), BF16),
            pltpu.VMEM((4, 8, CELLS, 3 * C), BF16),
            pltpu.VMEM((8, 4 * CELLS, C), BF16),
        ]
        + [pltpu.VMEM((SLICES, n, 24, 128), BF16) for n in pairs]
        + [pltpu.VMEM((16, n, 24, 128), BF16) for n in pairs]
        + [
            pltpu.VMEM((3, 3 * C, 256), BF16),
            pltpu.VMEM((2, 4, 10, PLANE, 128), F32),
            pltpu.VMEM((2, 2, 2, 2 * CELLS, 128), BF16),
            pltpu.VMEM((SLICES, 2, 2 * CELLS, 128), BF16),
            dma((2, 12)), dma((2, 16)), dma((3, 3)), dma((3, 4)), dma((3, 4)), dma((3, 4)),
            dma((3, 4, 2)), dma((3, 4, 2)), dma((2, 2, 2)), dma((3, 2)), dma((10,)),
        ],
        compiler_params=pltpu.CompilerParams(
            collective_id=0, has_side_effects=True, vmem_limit_bytes=56 * 1024 * 1024
        ),
        cost_estimate=pl.CostEstimate(flops=5_000_000_000, bytes_accessed=2_000_000, transcendentals=600_000),
    )(
        sharded_latents,
        sample_frame_count,
        entry_kernel.reshape(27 * LATENT_CHANNELS, C),
        entry_bias,
        norm_scale_gain,
        residual_bias,
        residual_kernel,
    )
    return out.reshape(4, LATENT_ROWS, LATENT_COLUMNS, C)


def solution(mesh):
    in_specs = (P("groups", "tm"), P("groups"), P(), P(), P(), P(None, "tm", None), P())
    out_specs = P(("groups", "tm"), None, None, None)
    sliced = mesh.shape["groups"] == 2 and mesh.shape["tm"] == 16
    body = sliced_shards if sliced else shards
    return jax.shard_map(body, mesh=mesh, in_specs=in_specs, out_specs=out_specs, check_vma=False)
```

```python
import jax
import jax.numpy as jnp
from jax import lax
from jax.experimental import pallas as pl
from jax.experimental.pallas import tpu as pltpu
from jax.sharding import PartitionSpec as P

LATENT_CHANNELS = 16
C = 384
PROMPT_SAMPLES = 8
BLOCK_FRAMES = 4
LATENT_ROWS = 6
LATENT_COLUMNS = 16


def from_behind(block, axis, distance):
    devices = range(lax.axis_size(axis))
    route = [(i - distance, i) for i in devices if i - distance in devices]
    return lax.ppermute(block, axis, route)


def causal_conv(frames, weight):
    frames_out = frames.shape[0] - 2
    inputs = frames.shape[3]
    padded = jnp.pad(frames, ((0, 0), (1, 1), (1, 1), (0, 0)))
    total = jnp.zeros((frames_out * LATENT_ROWS * LATENT_COLUMNS, weight.shape[2]), jnp.float32)
    for time_tap in range(3):
        for row_tap in range(3):
            for col_tap in range(3):
                window = padded[
                    time_tap : time_tap + frames_out,
                    row_tap : row_tap + LATENT_ROWS,
                    col_tap : col_tap + LATENT_COLUMNS,
                    :,
                ]
                window = window.reshape(frames_out * LATENT_ROWS * LATENT_COLUMNS, inputs)
                tap = 9 * time_tap + 3 * row_tap + col_tap
                total = total + jnp.dot(window, weight[tap], preferred_element_type=jnp.float32)
    return total


def activate(stream, norm_scale_gain):
    values = stream.astype(jnp.float32)
    scale = lax.rsqrt(jnp.mean(values * values, axis=-1, keepdims=True) + 1e-06)
    return jax.nn.silu(values * scale * norm_scale_gain).astype(jnp.bfloat16)


def to_cells(planes):
    return jnp.transpose(
        planes.reshape(planes.shape[0], LATENT_CHANNELS, LATENT_ROWS, LATENT_COLUMNS), (0, 2, 3, 1)
    )


def shards(
    sharded_latents,
    sample_frame_count,
    entry_kernel,
    entry_bias,
    norm_scale_gain,
    residual_kernel,
    residual_bias,
):
    gathered_latents = lax.all_to_all(
        sharded_latents, "tm", split_axis=0, concat_axis=1, tiled=True
    )
    latent_volume = gathered_latents.reshape(
        BLOCK_FRAMES, LATENT_CHANNELS, LATENT_ROWS * LATENT_COLUMNS
    )
    position = lax.axis_index("tm")
    block = position // PROMPT_SAMPLES
    sample = position % PROMPT_SAMPLES
    keep = block > 0
    earlier = from_behind(latent_volume, "tm", PROMPT_SAMPLES)
    earlier = jnp.where(keep, earlier, jnp.zeros_like(earlier))
    frames = to_cells(jnp.concatenate([earlier, latent_volume], axis=0))
    widened = (causal_conv(frames, entry_kernel) + entry_bias).astype(jnp.bfloat16)
    active_all = activate(widened, norm_scale_gain).reshape(
        BLOCK_FRAMES + 2, LATENT_ROWS, LATENT_COLUMNS, C
    )
    behind = jnp.where(keep, active_all[:2], jnp.zeros_like(active_all[:2]))
    extended = jnp.concatenate([behind, active_all[2:]], axis=0)
    stream = widened[2 * LATENT_ROWS * LATENT_COLUMNS :]
    kernel_all = lax.all_gather(residual_kernel, "tm", axis=1, tiled=True)
    branch = causal_conv(extended, kernel_all)
    total = (stream.astype(jnp.float32) + (branch + residual_bias)).reshape(
        BLOCK_FRAMES, LATENT_ROWS, LATENT_COLUMNS, C
    )
    limit = jnp.sum(jnp.where(jnp.arange(PROMPT_SAMPLES) == sample, sample_frame_count, 0))
    frame_index = block * BLOCK_FRAMES + jnp.arange(BLOCK_FRAMES)
    valid = (frame_index < limit)[:, None, None, None]
    return jnp.where(valid, total, jnp.zeros_like(total)).astype(jnp.bfloat16)


MESH = pl.DeviceIdType.MESH
F32, BF16 = jnp.float32, jnp.bfloat16
CELLS = LATENT_ROWS * LATENT_COLUMNS
PLANE = 128
HALF = 64
SLICES = 3
PAIRS = ((8, 7), (6, 5), (4, 3), (2, 1), (0,))
CHUNKS = ((0, 1), (2, 3), (4,))


def section_kernel(
    lat_far, counts, entry_far, entry_bias_far, gain_far, residual_bias_far, taps_far,
    out,
    entry, entry_bias, gain, residual_bias, lat_raw, taps, latq, lat, at, act, kept,
    piece_a, piece_b, piece_c, block_a, block_b, block_c, right, acc, done, got,
    lat_send, lat_recv, z_send, z_recv, y_send, y_recv, c_send, c_recv, o_send, o_recv, own, late,
):
    x = lax.axis_index("groups")
    me = lax.axis_index("tm")
    z, y, c = me // 4, (me // 2) % 2, me % 2
    pieces = (piece_a, piece_b, piece_c)
    blocks = (block_a, block_b, block_c)

    barrier = pltpu.get_barrier_semaphore()

    @pl.when(z < SLICES)
    def _():
        for step in range(1, 16):
            pl.semaphore_signal(barrier, inc=1, device_id={"tm": lax.rem(me + step, 16)}, device_id_type=MESH)
        for step in range(16):
            pl.semaphore_signal(
                barrier, inc=1, device_id={"groups": 1 - x, "tm": lax.rem(me + step, 16)}, device_id_type=MESH
            )

    first_copies = [
        pltpu.make_async_copy(lat_far, lat_raw, own.at[0]),
        pltpu.make_async_copy(taps_far, taps, own.at[1]),
        pltpu.make_async_copy(entry_far, entry, own.at[2]),
        pltpu.make_async_copy(entry_bias_far, entry_bias, own.at[3]),
        pltpu.make_async_copy(gain_far, gain, own.at[4]),
        pltpu.make_async_copy(residual_bias_far, residual_bias, own.at[5]),
    ]
    for copy in first_copies:
        copy.start()
    first_copies[0].wait()
    cell_rows = lat_raw[...].astype(F32)
    quads = [cell_rows[:, CELLS * q : CELLS * q + CELLS] for q in range(4)]
    quads = jnp.concatenate([jnp.concatenate([q, jnp.zeros((16, PLANE - CELLS), F32)], axis=1) for q in quads], axis=0)
    to_ = lax.broadcasted_iota(jnp.int32, (64, 64), 0)
    from_ = lax.broadcasted_iota(jnp.int32, (64, 64), 1)
    pick = from_ == (to_ % 4) * 16 + ((to_ % 16) // 8) * 8 + ((to_ // 4) % 2) * 4 + to_ // 16
    picked = jnp.dot(pick.astype(F32).astype(BF16), quads.astype(BF16), preferred_element_type=F32)
    latq[...] = picked.astype(BF16).reshape(4, 16, PLANE)
    pl.semaphore_wait(barrier, jnp.where(z < SLICES, 23, 24))

    @pl.when(z == SLICES)
    def _():
        for g in range(2):
            for n in range(SLICES):
                pl.semaphore_signal(
                    late, inc=1, device_id={"groups": g, "tm": n * 4 + y * 2 + c}, device_id_type=MESH
                )

    def remote(src, dst, send, recv, device):
        return pltpu.make_async_remote_copy(
            src_ref=src, dst_ref=dst, send_sem=send, recv_sem=recv, device_id=device, device_id_type=MESH
        )

    def columns(n):
        return pl.ds(pl.multiple_of(128 * n, 128), 128)

    def source_of(zz, yy, cc):
        return zz * 4 + yy * 2 + cc

    def lat_copy(to):
        return remote(latq.at[to % 4], lat.at[x, me], lat_send.at[to], lat_recv.at[me], {"tm": to})

    def group_copy(g):
        return remote(lat.at[g], lat.at[g], lat_send.at[12], lat_recv.at[16], {"groups": 1 - x, "tm": me})

    def z_copy(ch, n):
        return remote(
            pieces[ch].at[n], blocks[ch].at[me], z_send.at[ch, n], z_recv.at[ch, z], {"tm": source_of(n, y, c)}
        )

    def z_arrival(ch, zz):
        b = blocks[ch].at[source_of(zz, y, c)]
        return remote(b, b, z_send.at[ch, 0], z_recv.at[ch, zz], {"tm": source_of(zz, y, c)})

    def y_copy(ch, zz, source=None):
        b = blocks[ch].at[source_of(zz, y, c)]
        return remote(
            b if source is None else source, b, y_send.at[ch, zz], y_recv.at[ch, zz], {"tm": source_of(z, 1 - y, c)}
        )

    def y_arrival(ch, zz):
        b = blocks[ch].at[source_of(zz, 1 - y, c)]
        return remote(b, b, y_send.at[ch, zz], y_recv.at[ch, zz], {"tm": source_of(z, 1 - y, c)})

    def c_copy(ch, zz, yy, source=None):
        b = blocks[ch].at[source_of(zz, yy, c)]
        return remote(
            b if source is None else source, b, c_send.at[ch, zz, yy], c_recv.at[ch, zz, yy],
            {"tm": source_of(z, y, 1 - c)},
        )

    def c_arrival(ch, zz, yy):
        b = blocks[ch].at[source_of(zz, yy, 1 - c)]
        return remote(b, b, c_send.at[ch, zz, yy], c_recv.at[ch, zz, yy], {"tm": source_of(z, y, 1 - c)})

    def o_copy(g, h, b):
        return remote(
            done.at[g, h, b], got.at[z, x], o_send.at[g, h, b], o_recv.at[z, x],
            {"groups": g, "tm": source_of(2 * b + h, y, c)},
        )

    def o_arrival(n, xx):
        return remote(
            done.at[0, 0, 0], got.at[n, xx], o_send.at[0, 0, 0], o_recv.at[n, xx],
            {"groups": xx, "tm": source_of(n, y, c)},
        )

    for to in range(12):
        @pl.when(to != me)
        def _():
            lat_copy(to).start()

    first_copies[1].wait()
    keeps = (lax.broadcasted_iota(jnp.int32, (24, 128), 1) < HALF) == (x == 0)

    def halves(low, high, s):
        a = taps[low, :, 128 * s : 128 * s + 128].astype(F32)
        b = taps[high, :, 128 * s : 128 * s + 128].astype(F32)
        still = jnp.where(x == 0, a, b)
        moved = pltpu.roll(jnp.where(x == 0, b, a), HALF, 1)
        return jnp.where(keeps, still, moved).astype(BF16)

    for ch, pairs in enumerate(CHUNKS):
        for s in range(SLICES):
            if ch == 2:
                piece_c[s, 0] = halves(0, 1, s)
                piece_c[s, 1] = halves(2, 2, s)
            else:
                for n, p in enumerate(pairs):
                    low, high = PAIRS[p]
                    for k in range(3):
                        pieces[ch][s, 3 * n + k] = halves(3 * low + k, 3 * high + k, s)
        for n in range(SLICES):
            @pl.when(n != z)
            def _():
                z_copy(ch, n).start()

    @pl.when(z < SLICES)
    def _():
        mine = [pltpu.make_async_copy(latq.at[me % 4], lat.at[x, me], own.at[6])]
        for ch in range(3):
            y_copy(ch, z, pieces[ch].at[z]).start()
            c_copy(ch, z, y, pieces[ch].at[z]).start()
            mine.append(pltpu.make_async_copy(pieces[ch].at[z], blocks[ch].at[me], own.at[7 + ch]))
        for copy in mine:
            copy.start()

        def other(step):
            return SLICES if step == 2 else step + jnp.where(step >= z, 1, 0)

        def forward(ch, *steps):
            for step in steps:
                zz = other(step)
                z_arrival(ch, zz).wait_recv()
                y_copy(ch, zz).start()
                c_copy(ch, zz, y).start()

        def across(ch, *steps):
            for step in steps:
                zz = z if step < 0 else other(step)
                y_arrival(ch, zz).wait_recv()
                c_copy(ch, zz, 1 - y).start()

        def from_sibling(ch):
            for yy in range(2):
                for zz in range(4):
                    c_arrival(ch, zz, yy).wait_recv()

        at[:, 0:2] = jnp.zeros((4, 2, 144, PLANE), BF16)

        def clear(n, carry):
            acc[n // 4, n % 4] = jnp.zeros((10, PLANE, 128), F32)
            return carry

        lax.fori_loop(0, 8, clear, 0)
        for copy in first_copies[2:]:
            copy.wait()
        for copy in mine:
            copy.wait()
        forward(0, 0, 1)
        for source in range(16):
            @pl.when(source != me)
            def _():
                remote(
                    latq.at[0], lat.at[x, source], lat_send.at[0], lat_recv.at[source], {"tm": source}
                ).wait_recv()
        group_copy(x).start()
        target = lax.broadcasted_iota(jnp.int32, (256, 256), 0)
        origin = lax.broadcasted_iota(jnp.int32, (256, 256), 1)
        h_, b_, g_, ch_ = target // 128, (target // 64) % 2, (target // 16) % 4, target % 16
        perm = (origin == (g_ * 4 + ch_ // 4) * 16 + (b_ * 2 + h_) * 4 + ch_ % 4).astype(F32).astype(BF16)
        lane = lax.broadcasted_iota(jnp.int32, (256, PLANE), 1)
        row, column = lane // LATENT_COLUMNS, lane % LATENT_COLUMNS

        def spread(g):
            cells = jnp.dot(perm, lat[g].reshape(256, PLANE), preferred_element_type=F32)
            for j in range(3):
                for k in range(3):
                    offset = (j - 1) * LATENT_COLUMNS + (k - 1)
                    moved = pltpu.roll(cells, (-offset) % PLANE, 1) if offset else cells
                    good = (
                        (row + (j - 1) >= 0)
                        & (row + (j - 1) < LATENT_ROWS)
                        & (column + (k - 1) >= 0)
                        & (column + (k - 1) < LATENT_COLUMNS)
                    )
                    tap = 3 * j + k
                    at[pl.ds(2 * g, 2), 2:, tap * 16 : tap * 16 + 16, :] = (
                        jnp.where(good, moved, 0.0).astype(BF16).reshape(2, 8, 16, PLANE)
                    )

        def inlet(index, carry):
            h, b = index // 2, index % 2
            left = jnp.concatenate([at[h, pl.ds(4 * b + q, 3)].reshape(432, PLANE) for q in range(4)], axis=1)
            wide = lax.dot_general(left, entry[...], (((0,), (0,)), ((), ())), preferred_element_type=F32)
            wide = wide.reshape(4, PLANE, C)[:, :CELLS].reshape(4 * CELLS, C)
            stream = (wide + entry_bias[...][None, :]).astype(BF16)
            kept[index] = stream
            values = stream.astype(F32)
            scale = lax.rsqrt(jnp.mean(values * values, axis=-1, keepdims=True) + 1e-06)
            half_u = values * scale * (0.5 * gain[...])[None, :]
            active = (half_u + half_u * jnp.tanh(half_u)).astype(BF16).astype(F32)
            column = lax.broadcasted_iota(jnp.int32, (4 * CELLS, C), 0) % LATENT_COLUMNS
            before = jnp.where(column == 0, 0.0, pltpu.roll(active, 1, 0))
            behind = jnp.where(column == LATENT_COLUMNS - 1, 0.0, pltpu.roll(active, 4 * CELLS - 1, 0))
            for k, moved in enumerate((before, active, behind)):
                act[h, pl.ds(4 * b, 4), :, k * C : k * C + C] = moved.astype(BF16).reshape(4, CELLS, C)
            return carry

        def prepare_last():
            for n in range(2):
                piece = block_c[:, n].astype(F32).reshape(C, 128).astype(BF16)
                right[2, :C, 128 * n : 128 * n + 128] = piece

        def sweep_last(h):
            left = act[h, :6, :, C : 2 * C].reshape(6 * CELLS, C)
            wide = jnp.dot(left, right[2, :C], preferred_element_type=F32)
            column = lax.broadcasted_iota(jnp.int32, (6 * CELLS, 128), 0) % LATENT_COLUMNS
            before = jnp.where(column == 0, 0.0, pltpu.roll(wide[:, :128], 1, 0))
            behind = jnp.where(column == LATENT_COLUMNS - 1, 0.0, pltpu.roll(wide[:, 128:], 6 * CELLS - 1, 0))
            acc[0, h, 2:8, 32 : 32 + CELLS] += (before + behind).reshape(6, CELLS, 128)
            acc[1, h, 2:8, 32 : 32 + CELLS] += wide[:, :128].reshape(6, CELLS, 128)

        def prepare(ch):
            for n in range(len(CHUNKS[ch])):
                for k in range(3):
                    piece = blocks[ch][:, 3 * n + k].astype(F32).reshape(C, 128).astype(BF16)
                    right[ch, k * C : k * C + C, n * 128 : n * 128 + 128] = piece

        def sweep(h, ch, frames):
            pairs = CHUNKS[ch]
            left = act[h, :frames].reshape(frames * CELLS, 3 * C)
            wide = jnp.dot(left, right[ch, :, : 128 * len(pairs)], preferred_element_type=F32)
            for n, p in enumerate(pairs):
                part = wide[:, 128 * n : 128 * n + 128].reshape(frames, CELLS, 128)
                for side, slot in enumerate(PAIRS[p]):
                    i, j = slot // 3, slot % 3
                    acc[side, h, 2 - i : 2 - i + frames, 16 * (2 - j) : 16 * (2 - j) + CELLS] += part

        def both_groups(step, carry):
            g = jnp.where(step == 0, x, 1 - x)

            @pl.when(step == 1)
            def _():
                group_copy(g).wait_recv()

            spread(g)

            @pl.when(step == 0)
            def _():
                forward(1, 0, 1)

            lax.fori_loop(4 * g, 4 * g + 2, inlet, 0)

            @pl.when(step == 0)
            def _():
                forward(0, 2)
                across(0, -1, 0, 1)
                forward(2, 0, 1)

            @pl.when(step == 1)
            def _():
                forward(2, 2)
                across(0, 2)
                across(2, -1, 0, 1)

            lax.fori_loop(4 * g + 2, 4 * g + 4, inlet, 0)

            @pl.when(step == 0)
            def _():
                forward(1, 2)
                across(1, -1, 0, 1)

            return carry

        lax.fori_loop(0, 2, both_groups, 0)
        across(1, 2)
        from_sibling(0)
        prepare(0)

        def first(h, carry):
            sweep(h, 0, 8)
            return carry

        lax.fori_loop(0, 2, first, 0)
        across(2, 2)
        lax.fori_loop(2, 4, first, 0)
        from_sibling(1)
        prepare(1)
        from_sibling(2)
        prepare_last()
        pl.semaphore_wait(late, 2)
        edge = lax.broadcasted_iota(jnp.int32, (2, CELLS, 128), 2) < HALF
        bias = residual_bias[columns(z)][None, :]
        bias = jnp.where(x == 0, bias, pltpu.roll(jnp.broadcast_to(bias, (8, 128)), HALF, 1)[:1])

        def finish(step, carry):
            g, h = step % 2, 1 - step // 2
            gh = 2 * g + h
            sweep(gh, 1, 7)
            sweep_last(gh)
            for b in (1, 0):
                stream = kept[2 * gh + b, :, columns(z)].astype(F32)
                stream = jnp.where(x == 0, stream, pltpu.roll(stream, HALF, 1))
                even = acc[0, gh, 4 * b : 4 * b + 4, 16 : 16 + CELLS].reshape(4 * CELLS, 128)
                odd = acc[1, gh, 4 * b : 4 * b + 4, 16 : 16 + CELLS].reshape(4 * CELLS, 128)
                total = stream + (even + pltpu.roll(odd, HALF, 1) + bias)
                top = total[: 2 * CELLS].reshape(2, CELLS, 128)
                low = pltpu.roll(total[2 * CELLS :], HALF, 1).reshape(2, CELLS, 128)
                done[g, h, b] = jnp.where(edge, top, low).astype(BF16).reshape(2 * CELLS, 128)

                @pl.when((g != x) | (2 * b + h != z))
                def _():
                    o_copy(g, h, b).start()

            return carry

        lax.fori_loop(0, 4, finish, 0)
        got[z, x] = done[x, z % 2, z // 2]

    for n in range(SLICES):
        for xx in range(2):
            @pl.when((n != z) | (xx != x))
            def _():
                o_arrival(n, xx).wait_recv()
    limit = counts[me % PROMPT_SAMPLES]
    frame = lax.broadcasted_iota(jnp.int32, (2, CELLS, 128), 0) + BLOCK_FRAMES * (me // PROMPT_SAMPLES)
    half = lax.broadcasted_iota(jnp.int32, (2, CELLS, 128), 2) < HALF
    for n in range(SLICES):
        near_half = got[n, 0].astype(F32)
        far_half = got[n, 1].astype(F32)
        top = jnp.where(half, near_half.reshape(2, CELLS, 128), pltpu.roll(far_half, HALF, 1).reshape(2, CELLS, 128))
        low = jnp.where(half, pltpu.roll(near_half, HALF, 1).reshape(2, CELLS, 128), far_half.reshape(2, CELLS, 128))
        for first_frame, values in ((0, top), (2, low)):
            values = jnp.where(frame + first_frame < limit, values, 0.0).astype(BF16)
            out[CELLS * first_frame : CELLS * (first_frame + 2), 128 * n : 128 * n + 128] = values.reshape(2 * CELLS, 128)

    @pl.when(z == SLICES)
    def _():
        for copy in first_copies[2:]:
            copy.wait()

    for n in range(SLICES):
        @pl.when(n != z)
        def _():
            for ch in range(3):
                z_copy(ch, n).wait_send()

    for to in range(12):
        @pl.when(to != me)
        def _():
            lat_copy(to).wait_send()

    @pl.when(z < SLICES)
    def _():
        group_copy(x).wait_send()
        for ch in range(3):
            for zz in range(4):
                y_copy(ch, zz).wait_send()
                for yy in range(2):
                    c_copy(ch, zz, yy).wait_send()
        for g in range(2):
            for h in range(2):
                for b in range(2):
                    @pl.when((g != x) | (2 * b + h != z))
                    def _():
                        o_copy(g, h, b).wait_send()


def sliced_shards(
    sharded_latents,
    sample_frame_count,
    entry_kernel,
    entry_bias,
    norm_scale_gain,
    residual_kernel,
    residual_bias,
):
    vmem = pl.BlockSpec(memory_space=pltpu.VMEM)
    far = pl.BlockSpec(memory_space=pltpu.HBM)
    dma = pltpu.SemaphoreType.DMA
    pairs = (6, 6, 2)
    out = pl.pallas_call(
        section_kernel,
        out_shape=jax.ShapeDtypeStruct((4 * CELLS, C), BF16),
        in_specs=[far, pl.BlockSpec(memory_space=pltpu.SMEM)] + [far] * 5,
        out_specs=vmem,
        scratch_shapes=[
            pltpu.VMEM((27 * LATENT_CHANNELS, C), BF16),
            pltpu.VMEM((C,), F32), pltpu.VMEM((C,), F32), pltpu.VMEM((C,), F32),
            pltpu.VMEM((16, 4 * CELLS), BF16),
            pltpu.VMEM((27, 24, C), BF16),
            pltpu.VMEM((4, 16, PLANE), BF16),
            pltpu.VMEM((2, 16, 16, PLANE), BF16),
            pltpu.VMEM((4, 10, 144, PLANE), BF16),
            pltpu.VMEM((4, 8, CELLS, 3 * C), BF16),
            pltpu.VMEM((8, 4 * CELLS, C), BF16),
        ]
        + [pltpu.VMEM((SLICES, n, 24, 128), BF16) for n in pairs]
        + [pltpu.VMEM((16, n, 24, 128), BF16) for n in pairs]
        + [
            pltpu.VMEM((3, 3 * C, 256), BF16),
            pltpu.VMEM((2, 4, 10, PLANE, 128), F32),
            pltpu.VMEM((2, 2, 2, 2 * CELLS, 128), BF16),
            pltpu.VMEM((SLICES, 2, 2 * CELLS, 128), BF16),
            dma((13,)), dma((17,)), dma((3, 3)), dma((3, 4)), dma((3, 4)), dma((3, 4)),
            dma((3, 4, 2)), dma((3, 4, 2)), dma((2, 2, 2)), dma((3, 2)), dma((10,)), pltpu.SemaphoreType.REGULAR,
        ],
        compiler_params=pltpu.CompilerParams(
            collective_id=0, has_side_effects=True, vmem_limit_bytes=56 * 1024 * 1024
        ),
        cost_estimate=pl.CostEstimate(flops=5_000_000_000, bytes_accessed=2_000_000, transcendentals=600_000),
    )(
        sharded_latents,
        sample_frame_count,
        entry_kernel.reshape(27 * LATENT_CHANNELS, C),
        entry_bias,
        norm_scale_gain,
        residual_bias,
        residual_kernel,
    )
    return out.reshape(4, LATENT_ROWS, LATENT_COLUMNS, C)


def solution(mesh):
    in_specs = (P("groups", "tm"), P("groups"), P(), P(), P(), P(None, "tm", None), P())
    out_specs = P(("groups", "tm"), None, None, None)
    sliced = mesh.shape["groups"] == 2 and mesh.shape["tm"] == 16
    body = sliced_shards if sliced else shards
    return jax.shard_map(body, mesh=mesh, in_specs=in_specs, out_specs=out_specs, check_vma=False)
```

```python
import jax
import jax.numpy as jnp
from jax import lax
from jax.experimental import pallas as pl
from jax.experimental.pallas import tpu as pltpu
from jax.sharding import PartitionSpec as P

LATENT_CHANNELS = 16
C = 384
PROMPT_SAMPLES = 8
BLOCK_FRAMES = 4
LATENT_ROWS = 6
LATENT_COLUMNS = 16


def from_behind(block, axis, distance):
    devices = range(lax.axis_size(axis))
    route = [(i - distance, i) for i in devices if i - distance in devices]
    return lax.ppermute(block, axis, route)


def causal_conv(frames, weight):
    frames_out = frames.shape[0] - 2
    inputs = frames.shape[3]
    padded = jnp.pad(frames, ((0, 0), (1, 1), (1, 1), (0, 0)))
    total = jnp.zeros((frames_out * LATENT_ROWS * LATENT_COLUMNS, weight.shape[2]), jnp.float32)
    for time_tap in range(3):
        for row_tap in range(3):
            for col_tap in range(3):
                window = padded[
                    time_tap : time_tap + frames_out,
                    row_tap : row_tap + LATENT_ROWS,
                    col_tap : col_tap + LATENT_COLUMNS,
                    :,
                ]
                window = window.reshape(frames_out * LATENT_ROWS * LATENT_COLUMNS, inputs)
                tap = 9 * time_tap + 3 * row_tap + col_tap
                total = total + jnp.dot(window, weight[tap], preferred_element_type=jnp.float32)
    return total


def activate(stream, norm_scale_gain):
    values = stream.astype(jnp.float32)
    scale = lax.rsqrt(jnp.mean(values * values, axis=-1, keepdims=True) + 1e-06)
    return jax.nn.silu(values * scale * norm_scale_gain).astype(jnp.bfloat16)


def to_cells(planes):
    return jnp.transpose(
        planes.reshape(planes.shape[0], LATENT_CHANNELS, LATENT_ROWS, LATENT_COLUMNS), (0, 2, 3, 1)
    )


def shards(
    sharded_latents,
    sample_frame_count,
    entry_kernel,
    entry_bias,
    norm_scale_gain,
    residual_kernel,
    residual_bias,
):
    gathered_latents = lax.all_to_all(
        sharded_latents, "tm", split_axis=0, concat_axis=1, tiled=True
    )
    latent_volume = gathered_latents.reshape(
        BLOCK_FRAMES, LATENT_CHANNELS, LATENT_ROWS * LATENT_COLUMNS
    )
    position = lax.axis_index("tm")
    block = position // PROMPT_SAMPLES
    sample = position % PROMPT_SAMPLES
    keep = block > 0
    earlier = from_behind(latent_volume, "tm", PROMPT_SAMPLES)
    earlier = jnp.where(keep, earlier, jnp.zeros_like(earlier))
    frames = to_cells(jnp.concatenate([earlier, latent_volume], axis=0))
    widened = (causal_conv(frames, entry_kernel) + entry_bias).astype(jnp.bfloat16)
    active_all = activate(widened, norm_scale_gain).reshape(
        BLOCK_FRAMES + 2, LATENT_ROWS, LATENT_COLUMNS, C
    )
    behind = jnp.where(keep, active_all[:2], jnp.zeros_like(active_all[:2]))
    extended = jnp.concatenate([behind, active_all[2:]], axis=0)
    stream = widened[2 * LATENT_ROWS * LATENT_COLUMNS :]
    kernel_all = lax.all_gather(residual_kernel, "tm", axis=1, tiled=True)
    branch = causal_conv(extended, kernel_all)
    total = (stream.astype(jnp.float32) + (branch + residual_bias)).reshape(
        BLOCK_FRAMES, LATENT_ROWS, LATENT_COLUMNS, C
    )
    limit = jnp.sum(jnp.where(jnp.arange(PROMPT_SAMPLES) == sample, sample_frame_count, 0))
    frame_index = block * BLOCK_FRAMES + jnp.arange(BLOCK_FRAMES)
    valid = (frame_index < limit)[:, None, None, None]
    return jnp.where(valid, total, jnp.zeros_like(total)).astype(jnp.bfloat16)


MESH = pl.DeviceIdType.MESH
F32, BF16 = jnp.float32, jnp.bfloat16
CELLS = LATENT_ROWS * LATENT_COLUMNS
PLANE = 128
HALF = 64
SLICES = 3
PAIRS = ((8, 7), (6, 5), (4, 3), (2, 1), (0,))
CHUNKS = ((0, 1), (2, 3), (4,))


def section_kernel(
    lat_far, counts_far, entry_far, entry_bias_far, gain_far, residual_bias_far, taps_far,
    out,
    counts, entry, entry_bias, gain, residual_bias, lat_raw, taps, latq, lat, at, act, kept,
    piece_a, piece_b, piece_c, block_a, block_b, block_c, right, acc, done, got,
    lat_send, lat_recv, z_send, z_recv, y_send, y_recv, c_send, c_recv, o_send, o_recv, own, late,
):
    x = lax.axis_index("groups")
    me = lax.axis_index("tm")
    z, y, c = me // 4, (me // 2) % 2, me % 2
    pieces = (piece_a, piece_b, piece_c)
    blocks = (block_a, block_b, block_c)

    barrier = pltpu.get_barrier_semaphore()

    @pl.when(z < SLICES)
    def _():
        for step in range(1, 16):
            pl.semaphore_signal(barrier, inc=1, device_id={"tm": lax.rem(me + step, 16)}, device_id_type=MESH)
        for step in range(16):
            pl.semaphore_signal(
                barrier, inc=1, device_id={"groups": 1 - x, "tm": lax.rem(me + step, 16)}, device_id_type=MESH
            )

    first_copies = [
        pltpu.make_async_copy(lat_far, lat_raw, own.at[0]),
        pltpu.make_async_copy(taps_far, taps, own.at[1]),
        pltpu.make_async_copy(entry_far, entry, own.at[2]),
        pltpu.make_async_copy(entry_bias_far, entry_bias, own.at[3]),
        pltpu.make_async_copy(gain_far, gain, own.at[4]),
        pltpu.make_async_copy(residual_bias_far, residual_bias, own.at[5]),
        pltpu.make_async_copy(counts_far, counts, own.at[10]),
    ]
    for copy in first_copies:
        copy.start()
    first_copies[0].wait()
    cell_rows = lat_raw[...].astype(F32)
    quads = [cell_rows[:, CELLS * q : CELLS * q + CELLS] for q in range(4)]
    quads = jnp.concatenate([jnp.concatenate([q, jnp.zeros((16, PLANE - CELLS), F32)], axis=1) for q in quads], axis=0)
    to_ = lax.broadcasted_iota(jnp.int32, (64, 64), 0)
    from_ = lax.broadcasted_iota(jnp.int32, (64, 64), 1)
    pick = from_ == (to_ % 4) * 16 + ((to_ % 16) // 8) * 8 + ((to_ // 4) % 2) * 4 + to_ // 16
    picked = jnp.dot(pick.astype(F32).astype(BF16), quads.astype(BF16), preferred_element_type=F32)
    latq[...] = picked.astype(BF16).reshape(4, 16, PLANE)
    pl.semaphore_wait(barrier, jnp.where(z < SLICES, 23, 24))

    @pl.when(z == SLICES)
    def _():
        for g in range(2):
            for n in range(SLICES):
                pl.semaphore_signal(
                    late, inc=1, device_id={"groups": g, "tm": n * 4 + y * 2 + c}, device_id_type=MESH
                )

    def remote(src, dst, send, recv, device):
        return pltpu.make_async_remote_copy(
            src_ref=src, dst_ref=dst, send_sem=send, recv_sem=recv, device_id=device, device_id_type=MESH
        )

    def columns(n):
        return pl.ds(pl.multiple_of(128 * n, 128), 128)

    def source_of(zz, yy, cc):
        return zz * 4 + yy * 2 + cc

    def lat_copy(to):
        return remote(latq.at[to % 4], lat.at[x, me], lat_send.at[to], lat_recv.at[me], {"tm": to})

    def group_copy(g):
        return remote(lat.at[g], lat.at[g], lat_send.at[12], lat_recv.at[16], {"groups": 1 - x, "tm": me})

    def z_copy(ch, n):
        return remote(
            pieces[ch].at[n], blocks[ch].at[me], z_send.at[ch, n], z_recv.at[ch, z], {"tm": source_of(n, y, c)}
        )

    def z_arrival(ch, zz):
        b = blocks[ch].at[source_of(zz, y, c)]
        return remote(b, b, z_send.at[ch, 0], z_recv.at[ch, zz], {"tm": source_of(zz, y, c)})

    def y_copy(ch, zz, source=None):
        b = blocks[ch].at[source_of(zz, y, c)]
        return remote(
            b if source is None else source, b, y_send.at[ch, zz], y_recv.at[ch, zz], {"tm": source_of(z, 1 - y, c)}
        )

    def y_arrival(ch, zz):
        b = blocks[ch].at[source_of(zz, 1 - y, c)]
        return remote(b, b, y_send.at[ch, zz], y_recv.at[ch, zz], {"tm": source_of(z, 1 - y, c)})

    def c_copy(ch, zz, yy, source=None):
        b = blocks[ch].at[source_of(zz, yy, c)]
        return remote(
            b if source is None else source, b, c_send.at[ch, zz, yy], c_recv.at[ch, zz, yy],
            {"tm": source_of(z, y, 1 - c)},
        )

    def c_arrival(ch, zz, yy):
        b = blocks[ch].at[source_of(zz, yy, 1 - c)]
        return remote(b, b, c_send.at[ch, zz, yy], c_recv.at[ch, zz, yy], {"tm": source_of(z, y, 1 - c)})

    def o_copy(g, h, b):
        return remote(
            done.at[g, h, b], got.at[z, x], o_send.at[g, h, b], o_recv.at[z, x],
            {"groups": g, "tm": source_of(2 * b + h, y, c)},
        )

    def o_arrival(n, xx):
        return remote(
            done.at[0, 0, 0], got.at[n, xx], o_send.at[0, 0, 0], o_recv.at[n, xx],
            {"groups": xx, "tm": source_of(n, y, c)},
        )

    for to in range(12):
        @pl.when(to != me)
        def _():
            lat_copy(to).start()

    first_copies[1].wait()
    keeps = (lax.broadcasted_iota(jnp.int32, (24, 128), 1) < HALF) == (x == 0)

    def halves(low, high, s):
        a = taps[low, :, 128 * s : 128 * s + 128].astype(F32)
        b = taps[high, :, 128 * s : 128 * s + 128].astype(F32)
        still = jnp.where(x == 0, a, b)
        moved = pltpu.roll(jnp.where(x == 0, b, a), HALF, 1)
        return jnp.where(keeps, still, moved).astype(BF16)

    for ch, pairs in enumerate(CHUNKS):
        for s in range(SLICES):
            if ch == 2:
                piece_c[s, 0] = halves(0, 1, s)
                piece_c[s, 1] = halves(2, 2, s)
            else:
                for n, p in enumerate(pairs):
                    low, high = PAIRS[p]
                    for k in range(3):
                        pieces[ch][s, 3 * n + k] = halves(3 * low + k, 3 * high + k, s)
        for n in range(SLICES):
            @pl.when(n != z)
            def _():
                z_copy(ch, n).start()

        @pl.when(z < SLICES)
        def _():
            y_copy(ch, z, pieces[ch].at[z]).start()
            c_copy(ch, z, y, pieces[ch].at[z]).start()

        if ch < 2:
            for n in range(SLICES):
                @pl.when(z == SLICES)
                def _():
                    z_copy(ch, n).wait_send()

    @pl.when(z < SLICES)
    def _():
        mine = [pltpu.make_async_copy(latq.at[me % 4], lat.at[x, me], own.at[6])]
        for ch in range(3):
            mine.append(pltpu.make_async_copy(pieces[ch].at[z], blocks[ch].at[me], own.at[7 + ch]))
        for copy in mine:
            copy.start()

        def other(step):
            return SLICES if step == 2 else step + jnp.where(step >= z, 1, 0)

        def forward(ch, *steps):
            for step in steps:
                zz = other(step)
                z_arrival(ch, zz).wait_recv()
                y_copy(ch, zz).start()
                c_copy(ch, zz, y).start()

        def across(ch, *steps):
            for step in steps:
                zz = z if step < 0 else other(step)
                y_arrival(ch, zz).wait_recv()
                c_copy(ch, zz, 1 - y).start()

        def from_sibling(ch):
            for yy in range(2):
                for zz in range(4):
                    c_arrival(ch, zz, yy).wait_recv()

        at[:, 0:2] = jnp.zeros((4, 2, 144, PLANE), BF16)

        def clear(n, carry):
            acc[n // 4, n % 4] = jnp.zeros((10, PLANE, 128), F32)
            return carry

        lax.fori_loop(0, 8, clear, 0)
        for copy in first_copies[2:]:
            copy.wait()
        for copy in mine:
            copy.wait()
        forward(0, 0, 1)
        for source in range(16):
            @pl.when(source != me)
            def _():
                remote(
                    latq.at[0], lat.at[x, source], lat_send.at[0], lat_recv.at[source], {"tm": source}
                ).wait_recv()
        group_copy(x).start()
        target = lax.broadcasted_iota(jnp.int32, (256, 256), 0)
        origin = lax.broadcasted_iota(jnp.int32, (256, 256), 1)
        h_, b_, g_, ch_ = target // 128, (target // 64) % 2, (target // 16) % 4, target % 16
        perm = (origin == (g_ * 4 + ch_ // 4) * 16 + (b_ * 2 + h_) * 4 + ch_ % 4).astype(F32).astype(BF16)
        lane = lax.broadcasted_iota(jnp.int32, (256, PLANE), 1)
        row, column = lane // LATENT_COLUMNS, lane % LATENT_COLUMNS

        def spread(g):
            cells = jnp.dot(perm, lat[g].reshape(256, PLANE), preferred_element_type=F32)
            for j in range(3):
                for k in range(3):
                    offset = (j - 1) * LATENT_COLUMNS + (k - 1)
                    moved = pltpu.roll(cells, (-offset) % PLANE, 1) if offset else cells
                    good = (
                        (row + (j - 1) >= 0)
                        & (row + (j - 1) < LATENT_ROWS)
                        & (column + (k - 1) >= 0)
                        & (column + (k - 1) < LATENT_COLUMNS)
                    )
                    tap = 3 * j + k
                    at[pl.ds(2 * g, 2), 2:, tap * 16 : tap * 16 + 16, :] = (
                        jnp.where(good, moved, 0.0).astype(BF16).reshape(2, 8, 16, PLANE)
                    )

        def inlet(index, carry):
            h, b = index // 2, index % 2
            left = jnp.concatenate([at[h, pl.ds(4 * b + q, 3)].reshape(432, PLANE) for q in range(4)], axis=1)
            wide = lax.dot_general(left, entry[...], (((0,), (0,)), ((), ())), preferred_element_type=F32)
            wide = wide.reshape(4, PLANE, C)[:, :CELLS].reshape(4 * CELLS, C)
            stream = (wide + entry_bias[...][None, :]).astype(BF16)
            kept[index] = stream
            values = stream.astype(F32)
            scale = lax.rsqrt(jnp.mean(values * values, axis=-1, keepdims=True) + 1e-06)
            half_u = values * scale * (0.5 * gain[...])[None, :]
            active = (half_u + half_u * jnp.tanh(half_u)).astype(BF16).astype(F32)
            column = lax.broadcasted_iota(jnp.int32, (4 * CELLS, C), 0) % LATENT_COLUMNS
            before = jnp.where(column == 0, 0.0, pltpu.roll(active, 1, 0))
            behind = jnp.where(column == LATENT_COLUMNS - 1, 0.0, pltpu.roll(active, 4 * CELLS - 1, 0))
            for k, moved in enumerate((before, active, behind)):
                act[h, pl.ds(4 * b, 4), :, k * C : k * C + C] = moved.astype(BF16).reshape(4, CELLS, C)
            return carry

        def prepare_last():
            for n in range(2):
                piece = block_c[:, n].astype(F32).reshape(C, 128).astype(BF16)
                right[2, :C, 128 * n : 128 * n + 128] = piece

        def sweep_last(h):
            left = act[h, :6, :, C : 2 * C].reshape(6 * CELLS, C)
            wide = jnp.dot(left, right[2, :C], preferred_element_type=F32)
            column = lax.broadcasted_iota(jnp.int32, (6 * CELLS, 128), 0) % LATENT_COLUMNS
            before = jnp.where(column == 0, 0.0, pltpu.roll(wide[:, :128], 1, 0))
            behind = jnp.where(column == LATENT_COLUMNS - 1, 0.0, pltpu.roll(wide[:, 128:], 6 * CELLS - 1, 0))
            acc[0, h, 2:8, 32 : 32 + CELLS] += (before + behind).reshape(6, CELLS, 128)
            acc[1, h, 2:8, 32 : 32 + CELLS] += wide[:, :128].reshape(6, CELLS, 128)

        def prepare(ch):
            for n in range(len(CHUNKS[ch])):
                for k in range(3):
                    piece = blocks[ch][:, 3 * n + k].astype(F32).reshape(C, 128).astype(BF16)
                    right[ch, k * C : k * C + C, n * 128 : n * 128 + 128] = piece

        def sweep(h, ch, frames):
            pairs = CHUNKS[ch]
            left = act[h, :frames].reshape(frames * CELLS, 3 * C)
            wide = jnp.dot(left, right[ch, :, : 128 * len(pairs)], preferred_element_type=F32)
            for n, p in enumerate(pairs):
                part = wide[:, 128 * n : 128 * n + 128].reshape(frames, CELLS, 128)
                for side, slot in enumerate(PAIRS[p]):
                    i, j = slot // 3, slot % 3
                    acc[side, h, 2 - i : 2 - i + frames, 16 * (2 - j) : 16 * (2 - j) + CELLS] += part

        def both_groups(step, carry):
            g = jnp.where(step == 0, x, 1 - x)

            @pl.when(step == 1)
            def _():
                group_copy(g).wait_recv()

            spread(g)

            @pl.when(step == 0)
            def _():
                forward(1, 0, 1)

            lax.fori_loop(4 * g, 4 * g + 2, inlet, 0)

            @pl.when(step == 0)
            def _():
                forward(0, 2)
                across(0, -1, 0, 1)
                forward(2, 0, 1)

            @pl.when(step == 1)
            def _():
                forward(2, 2)
                across(0, 2)
                across(2, -1, 0, 1)

            lax.fori_loop(4 * g + 2, 4 * g + 4, inlet, 0)

            @pl.when(step == 0)
            def _():
                forward(1, 2)
                across(1, -1, 0, 1)

            return carry

        lax.fori_loop(0, 2, both_groups, 0)
        across(1, 2)
        from_sibling(0)
        prepare(0)

        def first(step, carry):
            sweep(2 * step + 1, 0, 8)
            return carry

        lax.fori_loop(0, 1, first, 0)
        across(2, 2)
        from_sibling(1)
        prepare(1)
        from_sibling(2)
        prepare_last()
        pl.semaphore_wait(late, 2)
        edge = lax.broadcasted_iota(jnp.int32, (2, CELLS, 128), 2) < HALF
        bias = residual_bias[columns(z)][None, :]
        bias = jnp.where(x == 0, bias, pltpu.roll(jnp.broadcast_to(bias, (8, 128)), HALF, 1)[:1])

        def finish(step, carry):
            g, h = step % 2, 1 - step // 2
            gh = 2 * g + h

            @pl.when(step >= 1)
            def _():
                sweep(gh, 0, 8)

            sweep(gh, 1, 7)
            sweep_last(gh)
            for b in (1, 0):
                stream = kept[2 * gh + b, :, columns(z)].astype(F32)
                stream = jnp.where(x == 0, stream, pltpu.roll(stream, HALF, 1))
                even = acc[0, gh, 4 * b : 4 * b + 4, 16 : 16 + CELLS].reshape(4 * CELLS, 128)
                odd = acc[1, gh, 4 * b : 4 * b + 4, 16 : 16 + CELLS].reshape(4 * CELLS, 128)
                total = stream + (even + pltpu.roll(odd, HALF, 1) + bias)
                top = total[: 2 * CELLS].reshape(2, CELLS, 128)
                low = pltpu.roll(total[2 * CELLS :], HALF, 1).reshape(2, CELLS, 128)
                done[g, h, b] = jnp.where(edge, top, low).astype(BF16).reshape(2 * CELLS, 128)

                @pl.when((g != x) | (2 * b + h != z))
                def _():
                    o_copy(g, h, b).start()

            return carry

        lax.fori_loop(0, 4, finish, 0)
        got[z, x] = done[x, z % 2, z // 2]

    for n in range(SLICES):
        for xx in range(2):
            @pl.when((n != z) | (xx != x))
            def _():
                o_arrival(n, xx).wait_recv()
    @pl.when(z == SLICES)
    def _():
        for copy in first_copies[2:]:
            copy.wait()

    limit = counts[me % PROMPT_SAMPLES]
    frame = lax.broadcasted_iota(jnp.int32, (2, CELLS, 128), 0) + BLOCK_FRAMES * (me // PROMPT_SAMPLES)
    half = lax.broadcasted_iota(jnp.int32, (2, CELLS, 128), 2) < HALF
    for n in range(SLICES):
        near_half = got[n, 0].astype(F32)
        far_half = got[n, 1].astype(F32)
        top = jnp.where(half, near_half.reshape(2, CELLS, 128), pltpu.roll(far_half, HALF, 1).reshape(2, CELLS, 128))
        low = jnp.where(half, pltpu.roll(near_half, HALF, 1).reshape(2, CELLS, 128), far_half.reshape(2, CELLS, 128))
        for first_frame, values in ((0, top), (2, low)):
            values = jnp.where(frame + first_frame < limit, values, 0.0).astype(BF16)
            out[CELLS * first_frame : CELLS * (first_frame + 2), 128 * n : 128 * n + 128] = values.reshape(2 * CELLS, 128)

    for n in range(SLICES):
        @pl.when(n != z)
        def _():
            z_copy(2, n).wait_send()

            @pl.when(z < SLICES)
            def _():
                for ch in range(2):
                    z_copy(ch, n).wait_send()

    for to in range(12):
        @pl.when(to != me)
        def _():
            lat_copy(to).wait_send()

    @pl.when(z < SLICES)
    def _():
        group_copy(x).wait_send()
        for ch in range(3):
            for zz in range(4):
                y_copy(ch, zz).wait_send()
                for yy in range(2):
                    c_copy(ch, zz, yy).wait_send()
        for g in range(2):
            for h in range(2):
                for b in range(2):
                    @pl.when((g != x) | (2 * b + h != z))
                    def _():
                        o_copy(g, h, b).wait_send()


def sliced_shards(
    sharded_latents,
    sample_frame_count,
    entry_kernel,
    entry_bias,
    norm_scale_gain,
    residual_kernel,
    residual_bias,
):
    vmem = pl.BlockSpec(memory_space=pltpu.VMEM)
    far = pl.BlockSpec(memory_space=pltpu.HBM)
    dma = pltpu.SemaphoreType.DMA
    pairs = (6, 6, 2)
    out = pl.pallas_call(
        section_kernel,
        out_shape=jax.ShapeDtypeStruct((4 * CELLS, C), BF16),
        in_specs=[far] * 7,
        out_specs=vmem,
        scratch_shapes=[
            pltpu.SMEM((PROMPT_SAMPLES,), jnp.int32),
            pltpu.VMEM((27 * LATENT_CHANNELS, C), BF16),
            pltpu.VMEM((C,), F32), pltpu.VMEM((C,), F32), pltpu.VMEM((C,), F32),
            pltpu.VMEM((16, 4 * CELLS), BF16),
            pltpu.VMEM((27, 24, C), BF16),
            pltpu.VMEM((4, 16, PLANE), BF16),
            pltpu.VMEM((2, 16, 16, PLANE), BF16),
            pltpu.VMEM((4, 10, 144, PLANE), BF16),
            pltpu.VMEM((4, 8, CELLS, 3 * C), BF16),
            pltpu.VMEM((8, 4 * CELLS, C), BF16),
        ]
        + [pltpu.VMEM((SLICES, n, 24, 128), BF16) for n in pairs]
        + [pltpu.VMEM((16, n, 24, 128), BF16) for n in pairs]
        + [
            pltpu.VMEM((3, 3 * C, 256), BF16),
            pltpu.VMEM((2, 4, 10, PLANE, 128), F32),
            pltpu.VMEM((2, 2, 2, 2 * CELLS, 128), BF16),
            pltpu.VMEM((SLICES, 2, 2 * CELLS, 128), BF16),
            dma((13,)), dma((17,)), dma((3, 3)), dma((3, 4)), dma((3, 4)), dma((3, 4)),
            dma((3, 4, 2)), dma((3, 4, 2)), dma((2, 2, 2)), dma((3, 2)), dma((11,)), pltpu.SemaphoreType.REGULAR,
        ],
        compiler_params=pltpu.CompilerParams(
            collective_id=0, has_side_effects=True, vmem_limit_bytes=56 * 1024 * 1024
        ),
        cost_estimate=pl.CostEstimate(flops=5_000_000_000, bytes_accessed=2_000_000, transcendentals=600_000),
    )(
        sharded_latents,
        sample_frame_count,
        entry_kernel.reshape(27 * LATENT_CHANNELS, C),
        entry_bias,
        norm_scale_gain,
        residual_bias,
        residual_kernel,
    )
    return out.reshape(4, LATENT_ROWS, LATENT_COLUMNS, C)


def solution(mesh):
    in_specs = (P("groups", "tm"), P("groups"), P(), P(), P(), P(None, "tm", None), P())
    out_specs = P(("groups", "tm"), None, None, None)
    sliced = mesh.shape["groups"] == 2 and mesh.shape["tm"] == 16
    body = sliced_shards if sliced else shards
    return jax.shard_map(body, mesh=mesh, in_specs=in_specs, out_specs=out_specs, check_vma=False)
```

```python
import jax
import jax.numpy as jnp
from jax import lax
from jax.experimental import pallas as pl
from jax.experimental.pallas import tpu as pltpu
from jax.sharding import PartitionSpec as P

LATENT_CHANNELS = 16
C = 384
PROMPT_SAMPLES = 8
BLOCK_FRAMES = 4
LATENT_ROWS = 6
LATENT_COLUMNS = 16


def from_behind(block, axis, distance):
    devices = range(lax.axis_size(axis))
    route = [(i - distance, i) for i in devices if i - distance in devices]
    return lax.ppermute(block, axis, route)


def causal_conv(frames, weight):
    frames_out = frames.shape[0] - 2
    inputs = frames.shape[3]
    padded = jnp.pad(frames, ((0, 0), (1, 1), (1, 1), (0, 0)))
    total = jnp.zeros((frames_out * LATENT_ROWS * LATENT_COLUMNS, weight.shape[2]), jnp.float32)
    for time_tap in range(3):
        for row_tap in range(3):
            for col_tap in range(3):
                window = padded[
                    time_tap : time_tap + frames_out,
                    row_tap : row_tap + LATENT_ROWS,
                    col_tap : col_tap + LATENT_COLUMNS,
                    :,
                ]
                window = window.reshape(frames_out * LATENT_ROWS * LATENT_COLUMNS, inputs)
                tap = 9 * time_tap + 3 * row_tap + col_tap
                total = total + jnp.dot(window, weight[tap], preferred_element_type=jnp.float32)
    return total


def activate(stream, norm_scale_gain):
    values = stream.astype(jnp.float32)
    scale = lax.rsqrt(jnp.mean(values * values, axis=-1, keepdims=True) + 1e-06)
    return jax.nn.silu(values * scale * norm_scale_gain).astype(jnp.bfloat16)


def to_cells(planes):
    return jnp.transpose(
        planes.reshape(planes.shape[0], LATENT_CHANNELS, LATENT_ROWS, LATENT_COLUMNS), (0, 2, 3, 1)
    )


def shards(
    sharded_latents,
    sample_frame_count,
    entry_kernel,
    entry_bias,
    norm_scale_gain,
    residual_kernel,
    residual_bias,
):
    gathered_latents = lax.all_to_all(
        sharded_latents, "tm", split_axis=0, concat_axis=1, tiled=True
    )
    latent_volume = gathered_latents.reshape(
        BLOCK_FRAMES, LATENT_CHANNELS, LATENT_ROWS * LATENT_COLUMNS
    )
    position = lax.axis_index("tm")
    block = position // PROMPT_SAMPLES
    sample = position % PROMPT_SAMPLES
    keep = block > 0
    earlier = from_behind(latent_volume, "tm", PROMPT_SAMPLES)
    earlier = jnp.where(keep, earlier, jnp.zeros_like(earlier))
    frames = to_cells(jnp.concatenate([earlier, latent_volume], axis=0))
    widened = (causal_conv(frames, entry_kernel) + entry_bias).astype(jnp.bfloat16)
    active_all = activate(widened, norm_scale_gain).reshape(
        BLOCK_FRAMES + 2, LATENT_ROWS, LATENT_COLUMNS, C
    )
    behind = jnp.where(keep, active_all[:2], jnp.zeros_like(active_all[:2]))
    extended = jnp.concatenate([behind, active_all[2:]], axis=0)
    stream = widened[2 * LATENT_ROWS * LATENT_COLUMNS :]
    kernel_all = lax.all_gather(residual_kernel, "tm", axis=1, tiled=True)
    branch = causal_conv(extended, kernel_all)
    total = (stream.astype(jnp.float32) + (branch + residual_bias)).reshape(
        BLOCK_FRAMES, LATENT_ROWS, LATENT_COLUMNS, C
    )
    limit = jnp.sum(jnp.where(jnp.arange(PROMPT_SAMPLES) == sample, sample_frame_count, 0))
    frame_index = block * BLOCK_FRAMES + jnp.arange(BLOCK_FRAMES)
    valid = (frame_index < limit)[:, None, None, None]
    return jnp.where(valid, total, jnp.zeros_like(total)).astype(jnp.bfloat16)


MESH = pl.DeviceIdType.MESH
F32, BF16 = jnp.float32, jnp.bfloat16
CELLS = LATENT_ROWS * LATENT_COLUMNS
PLANE = 128
HALF = 64
SLICES = 3
PAIRS = ((8, 7), (6, 5), (4, 3), (2, 1), (0,))
CHUNKS = ((0, 1), (2, 3))


def section_kernel(
    lat_far, counts_far, entry_far, entry_bias_far, gain_far, residual_bias_far, taps_far,
    out,
    counts, entry, entry_bias, gain, residual_bias, lat_raw, taps, latq, lat, at, act, kept,
    piece_a, piece_b, block_a, block_b, right, acc, done, got,
    lat_send, lat_recv, z_send, z_recv, y_send, y_recv, c_send, c_recv, o_send, o_recv, own, late,
):
    x = lax.axis_index("groups")
    me = lax.axis_index("tm")
    z, y, c = me // 4, (me // 2) % 2, me % 2
    pieces = (piece_a, piece_b)
    blocks = (block_a, block_b)

    barrier = pltpu.get_barrier_semaphore()

    @pl.when(z < SLICES)
    def _():
        for step in range(1, 16):
            pl.semaphore_signal(barrier, inc=1, device_id={"tm": lax.rem(me + step, 16)}, device_id_type=MESH)
        for step in range(16):
            pl.semaphore_signal(
                barrier, inc=1, device_id={"groups": 1 - x, "tm": lax.rem(me + step, 16)}, device_id_type=MESH
            )

    first_copies = [
        pltpu.make_async_copy(lat_far, lat_raw, own.at[0]),
        pltpu.make_async_copy(taps_far, taps, own.at[1]),
        pltpu.make_async_copy(entry_far, entry, own.at[2]),
        pltpu.make_async_copy(entry_bias_far, entry_bias, own.at[3]),
        pltpu.make_async_copy(gain_far, gain, own.at[4]),
        pltpu.make_async_copy(residual_bias_far, residual_bias, own.at[5]),
        pltpu.make_async_copy(counts_far, counts, own.at[10]),
    ]
    for copy in first_copies:
        copy.start()
    first_copies[0].wait()
    cell_rows = lat_raw[...].astype(F32)
    quads = [cell_rows[:, CELLS * q : CELLS * q + CELLS] for q in range(4)]
    quads = jnp.concatenate([jnp.concatenate([q, jnp.zeros((16, PLANE - CELLS), F32)], axis=1) for q in quads], axis=0)
    to_ = lax.broadcasted_iota(jnp.int32, (64, 64), 0)
    from_ = lax.broadcasted_iota(jnp.int32, (64, 64), 1)
    pick = from_ == (to_ % 4) * 16 + ((to_ % 16) // 8) * 8 + ((to_ // 4) % 2) * 4 + to_ // 16
    picked = jnp.dot(pick.astype(F32).astype(BF16), quads.astype(BF16), preferred_element_type=F32)
    latq[...] = picked.astype(BF16).reshape(4, 16, PLANE)
    pl.semaphore_wait(barrier, jnp.where(z < SLICES, 23, 24))

    @pl.when(z == SLICES)
    def _():
        for g in range(2):
            for n in range(SLICES):
                pl.semaphore_signal(
                    late, inc=1, device_id={"groups": g, "tm": n * 4 + y * 2 + c}, device_id_type=MESH
                )

    def remote(src, dst, send, recv, device):
        return pltpu.make_async_remote_copy(
            src_ref=src, dst_ref=dst, send_sem=send, recv_sem=recv, device_id=device, device_id_type=MESH
        )

    def columns(n):
        return pl.ds(pl.multiple_of(128 * n, 128), 128)

    def source_of(zz, yy, cc):
        return zz * 4 + yy * 2 + cc

    def lat_copy(to):
        return remote(latq.at[to % 4], lat.at[x, me], lat_send.at[to], lat_recv.at[me], {"tm": to})

    def group_copy(g):
        return remote(lat.at[g], lat.at[g], lat_send.at[12], lat_recv.at[16], {"groups": 1 - x, "tm": me})

    def z_copy(ch, n):
        return remote(
            pieces[ch].at[n], blocks[ch].at[me], z_send.at[ch, n], z_recv.at[ch, z], {"tm": source_of(n, y, c)}
        )

    def z_arrival(ch, zz):
        b = blocks[ch].at[source_of(zz, y, c)]
        return remote(b, b, z_send.at[ch, 0], z_recv.at[ch, zz], {"tm": source_of(zz, y, c)})

    def y_copy(ch, zz, source=None):
        b = blocks[ch].at[source_of(zz, y, c)]
        return remote(
            b if source is None else source, b, y_send.at[ch, zz], y_recv.at[ch, zz], {"tm": source_of(z, 1 - y, c)}
        )

    def y_arrival(ch, zz):
        b = blocks[ch].at[source_of(zz, 1 - y, c)]
        return remote(b, b, y_send.at[ch, zz], y_recv.at[ch, zz], {"tm": source_of(z, 1 - y, c)})

    def c_copy(ch, zz, yy, source=None):
        b = blocks[ch].at[source_of(zz, yy, c)]
        return remote(
            b if source is None else source, b, c_send.at[ch, zz, yy], c_recv.at[ch, zz, yy],
            {"tm": source_of(z, y, 1 - c)},
        )

    def c_arrival(ch, zz, yy):
        b = blocks[ch].at[source_of(zz, yy, 1 - c)]
        return remote(b, b, c_send.at[ch, zz, yy], c_recv.at[ch, zz, yy], {"tm": source_of(z, y, 1 - c)})

    def o_copy(g, h, b):
        return remote(
            done.at[g, h, b], got.at[z, x], o_send.at[g, h, b], o_recv.at[z, x],
            {"groups": g, "tm": source_of(2 * b + h, y, c)},
        )

    def o_arrival(n, xx):
        return remote(
            done.at[0, 0, 0], got.at[n, xx], o_send.at[0, 0, 0], o_recv.at[n, xx],
            {"groups": xx, "tm": source_of(n, y, c)},
        )

    for to in range(12):
        @pl.when(to != me)
        def _():
            lat_copy(to).start()

    first_copies[1].wait()
    keeps = (lax.broadcasted_iota(jnp.int32, (24, 128), 1) < HALF) == (x == 0)

    def halves(low, high, s):
        a = taps[low, :, 128 * s : 128 * s + 128].astype(F32)
        b = taps[high, :, 128 * s : 128 * s + 128].astype(F32)
        still = jnp.where(x == 0, a, b)
        moved = pltpu.roll(jnp.where(x == 0, b, a), HALF, 1)
        return jnp.where(keeps, still, moved).astype(BF16)

    for ch, pairs in enumerate(CHUNKS):
        for s in range(SLICES):
            if ch == 1:
                piece_b[s, 6] = halves(0, 1, s)
                piece_b[s, 7] = halves(2, 2, s)
            for n, p in enumerate(pairs):
                low, high = PAIRS[p]
                for k in range(3):
                    pieces[ch][s, 3 * n + k] = halves(3 * low + k, 3 * high + k, s)
        for n in range(SLICES):
            @pl.when(n != z)
            def _():
                z_copy(ch, n).start()

        @pl.when(z < SLICES)
        def _():
            y_copy(ch, z, pieces[ch].at[z]).start()
            c_copy(ch, z, y, pieces[ch].at[z]).start()

        if ch < 1:
            for n in range(SLICES):
                @pl.when(z == SLICES)
                def _():
                    z_copy(ch, n).wait_send()

    @pl.when(z < SLICES)
    def _():
        mine = [pltpu.make_async_copy(latq.at[me % 4], lat.at[x, me], own.at[6])]
        for ch in range(2):
            mine.append(pltpu.make_async_copy(pieces[ch].at[z], blocks[ch].at[me], own.at[7 + ch]))
        for copy in mine:
            copy.start()

        def other(step):
            return SLICES if step == 2 else step + jnp.where(step >= z, 1, 0)

        def forward(ch, *steps):
            for step in steps:
                zz = other(step)
                z_arrival(ch, zz).wait_recv()
                y_copy(ch, zz).start()
                c_copy(ch, zz, y).start()

        def across(ch, *steps):
            for step in steps:
                zz = z if step < 0 else other(step)
                y_arrival(ch, zz).wait_recv()
                c_copy(ch, zz, 1 - y).start()

        def from_sibling(ch):
            for yy in range(2):
                for zz in range(4):
                    c_arrival(ch, zz, yy).wait_recv()

        at[:, 0:2] = jnp.zeros((4, 2, 144, PLANE), BF16)

        def clear(n, carry):
            acc[n // 4, n % 4] = jnp.zeros((10, PLANE, 128), F32)
            return carry

        lax.fori_loop(0, 8, clear, 0)
        for copy in first_copies[2:]:
            copy.wait()
        for copy in mine:
            copy.wait()
        forward(0, 0, 1)
        for source in range(16):
            @pl.when(source != me)
            def _():
                remote(
                    latq.at[0], lat.at[x, source], lat_send.at[0], lat_recv.at[source], {"tm": source}
                ).wait_recv()
        group_copy(x).start()
        target = lax.broadcasted_iota(jnp.int32, (256, 256), 0)
        origin = lax.broadcasted_iota(jnp.int32, (256, 256), 1)
        h_, b_, g_, ch_ = target // 128, (target // 64) % 2, (target // 16) % 4, target % 16
        perm = (origin == (g_ * 4 + ch_ // 4) * 16 + (b_ * 2 + h_) * 4 + ch_ % 4).astype(F32).astype(BF16)
        lane = lax.broadcasted_iota(jnp.int32, (256, PLANE), 1)
        row, column = lane // LATENT_COLUMNS, lane % LATENT_COLUMNS

        def spread(g):
            cells = jnp.dot(perm, lat[g].reshape(256, PLANE), preferred_element_type=F32)
            for j in range(3):
                for k in range(3):
                    offset = (j - 1) * LATENT_COLUMNS + (k - 1)
                    moved = pltpu.roll(cells, (-offset) % PLANE, 1) if offset else cells
                    good = (
                        (row + (j - 1) >= 0)
                        & (row + (j - 1) < LATENT_ROWS)
                        & (column + (k - 1) >= 0)
                        & (column + (k - 1) < LATENT_COLUMNS)
                    )
                    tap = 3 * j + k
                    at[pl.ds(2 * g, 2), 2:, tap * 16 : tap * 16 + 16, :] = (
                        jnp.where(good, moved, 0.0).astype(BF16).reshape(2, 8, 16, PLANE)
                    )

        def inlet(index, carry):
            h, b = index // 2, index % 2
            left = jnp.concatenate([at[h, pl.ds(4 * b + q, 3)].reshape(432, PLANE) for q in range(4)], axis=1)
            wide = lax.dot_general(left, entry[...], (((0,), (0,)), ((), ())), preferred_element_type=F32)
            wide = wide.reshape(4, PLANE, C)[:, :CELLS].reshape(4 * CELLS, C)
            stream = (wide + entry_bias[...][None, :]).astype(BF16)
            kept[index] = stream
            values = stream.astype(F32)
            scale = lax.rsqrt(jnp.mean(values * values, axis=-1, keepdims=True) + 1e-06)
            half_u = values * scale * (0.5 * gain[...])[None, :]
            active = (half_u + half_u * jnp.tanh(half_u)).astype(BF16).astype(F32)
            column = lax.broadcasted_iota(jnp.int32, (4 * CELLS, C), 0) % LATENT_COLUMNS
            before = jnp.where(column == 0, 0.0, pltpu.roll(active, 1, 0))
            behind = jnp.where(column == LATENT_COLUMNS - 1, 0.0, pltpu.roll(active, 4 * CELLS - 1, 0))
            for k, moved in enumerate((before, active, behind)):
                act[h, pl.ds(4 * b, 4), :, k * C : k * C + C] = moved.astype(BF16).reshape(4, CELLS, C)
            return carry

        def prepare_last():
            for n in range(2):
                piece = block_b[:, 6 + n].astype(F32).reshape(C, 128).astype(BF16)
                right[2, :C, 128 * n : 128 * n + 128] = piece

        def sweep_last(h):
            left = act[h, :6, :, C : 2 * C].reshape(6 * CELLS, C)
            wide = jnp.dot(left, right[2, :C], preferred_element_type=F32)
            column = lax.broadcasted_iota(jnp.int32, (6 * CELLS, 128), 0) % LATENT_COLUMNS
            before = jnp.where(column == 0, 0.0, pltpu.roll(wide[:, :128], 1, 0))
            behind = jnp.where(column == LATENT_COLUMNS - 1, 0.0, pltpu.roll(wide[:, 128:], 6 * CELLS - 1, 0))
            acc[0, h, 2:8, 32 : 32 + CELLS] += (before + behind).reshape(6, CELLS, 128)
            acc[1, h, 2:8, 32 : 32 + CELLS] += wide[:, :128].reshape(6, CELLS, 128)

        def prepare(ch):
            for n in range(len(CHUNKS[ch])):
                for k in range(3):
                    piece = blocks[ch][:, 3 * n + k].astype(F32).reshape(C, 128).astype(BF16)
                    right[ch, k * C : k * C + C, n * 128 : n * 128 + 128] = piece

        def sweep(h, ch, frames):
            pairs = CHUNKS[ch]
            left = act[h, :frames].reshape(frames * CELLS, 3 * C)
            wide = jnp.dot(left, right[ch, :, : 128 * len(pairs)], preferred_element_type=F32)
            for n, p in enumerate(pairs):
                part = wide[:, 128 * n : 128 * n + 128].reshape(frames, CELLS, 128)
                for side, slot in enumerate(PAIRS[p]):
                    i, j = slot // 3, slot % 3
                    acc[side, h, 2 - i : 2 - i + frames, 16 * (2 - j) : 16 * (2 - j) + CELLS] += part

        def both_groups(step, carry):
            g = jnp.where(step == 0, x, 1 - x)

            @pl.when(step == 1)
            def _():
                group_copy(g).wait_recv()

            spread(g)

            @pl.when(step == 0)
            def _():
                forward(1, 0, 1)

            lax.fori_loop(4 * g, 4 * g + 2, inlet, 0)

            @pl.when(step == 0)
            def _():
                forward(0, 2)
                across(0, -1, 0, 1)

            @pl.when(step == 1)
            def _():
                across(0, 2)

            lax.fori_loop(4 * g + 2, 4 * g + 4, inlet, 0)

            @pl.when(step == 0)
            def _():
                forward(1, 2)
                across(1, -1, 0, 1)

            return carry

        lax.fori_loop(0, 2, both_groups, 0)
        across(1, 2)
        from_sibling(0)
        prepare(0)

        def first(step, carry):
            sweep(2 * step + 1, 0, 8)
            return carry

        lax.fori_loop(0, 1, first, 0)
        from_sibling(1)
        prepare(1)
        prepare_last()
        pl.semaphore_wait(late, 2)
        edge = lax.broadcasted_iota(jnp.int32, (2, CELLS, 128), 2) < HALF
        bias = residual_bias[columns(z)][None, :]
        bias = jnp.where(x == 0, bias, pltpu.roll(jnp.broadcast_to(bias, (8, 128)), HALF, 1)[:1])

        def finish(step, carry):
            g, h = step % 2, 1 - step // 2
            gh = 2 * g + h

            @pl.when(step >= 1)
            def _():
                sweep(gh, 0, 8)

            sweep(gh, 1, 7)
            sweep_last(gh)
            for b in (1, 0):
                stream = kept[2 * gh + b, :, columns(z)].astype(F32)
                stream = jnp.where(x == 0, stream, pltpu.roll(stream, HALF, 1))
                even = acc[0, gh, 4 * b : 4 * b + 4, 16 : 16 + CELLS].reshape(4 * CELLS, 128)
                odd = acc[1, gh, 4 * b : 4 * b + 4, 16 : 16 + CELLS].reshape(4 * CELLS, 128)
                total = stream + (even + pltpu.roll(odd, HALF, 1) + bias)
                top = total[: 2 * CELLS].reshape(2, CELLS, 128)
                low = pltpu.roll(total[2 * CELLS :], HALF, 1).reshape(2, CELLS, 128)
                done[g, h, b] = jnp.where(edge, top, low).astype(BF16).reshape(2 * CELLS, 128)

                @pl.when((g != x) | (2 * b + h != z))
                def _():
                    o_copy(g, h, b).start()

            return carry

        lax.fori_loop(0, 4, finish, 0)
        got[z, x] = done[x, z % 2, z // 2]

    for n in range(SLICES):
        for xx in range(2):
            @pl.when((n != z) | (xx != x))
            def _():
                o_arrival(n, xx).wait_recv()
    @pl.when(z == SLICES)
    def _():
        for copy in first_copies[2:]:
            copy.wait()

    limit = counts[me % PROMPT_SAMPLES]
    frame = lax.broadcasted_iota(jnp.int32, (2, CELLS, 128), 0) + BLOCK_FRAMES * (me // PROMPT_SAMPLES)
    half = lax.broadcasted_iota(jnp.int32, (2, CELLS, 128), 2) < HALF
    for n in range(SLICES):
        near_half = got[n, 0].astype(F32)
        far_half = got[n, 1].astype(F32)
        top = jnp.where(half, near_half.reshape(2, CELLS, 128), pltpu.roll(far_half, HALF, 1).reshape(2, CELLS, 128))
        low = jnp.where(half, pltpu.roll(near_half, HALF, 1).reshape(2, CELLS, 128), far_half.reshape(2, CELLS, 128))
        for first_frame, values in ((0, top), (2, low)):
            values = jnp.where(frame + first_frame < limit, values, 0.0).astype(BF16)
            out[CELLS * first_frame : CELLS * (first_frame + 2), 128 * n : 128 * n + 128] = values.reshape(2 * CELLS, 128)

    for n in range(SLICES):
        @pl.when(n != z)
        def _():
            z_copy(1, n).wait_send()

            @pl.when(z < SLICES)
            def _():
                z_copy(0, n).wait_send()

    for to in range(12):
        @pl.when(to != me)
        def _():
            lat_copy(to).wait_send()

    @pl.when(z < SLICES)
    def _():
        group_copy(x).wait_send()
        for ch in range(2):
            for zz in range(4):
                y_copy(ch, zz).wait_send()
                for yy in range(2):
                    c_copy(ch, zz, yy).wait_send()
        for g in range(2):
            for h in range(2):
                for b in range(2):
                    @pl.when((g != x) | (2 * b + h != z))
                    def _():
                        o_copy(g, h, b).wait_send()


def sliced_shards(
    sharded_latents,
    sample_frame_count,
    entry_kernel,
    entry_bias,
    norm_scale_gain,
    residual_kernel,
    residual_bias,
):
    vmem = pl.BlockSpec(memory_space=pltpu.VMEM)
    far = pl.BlockSpec(memory_space=pltpu.HBM)
    dma = pltpu.SemaphoreType.DMA
    pairs = (6, 8)
    out = pl.pallas_call(
        section_kernel,
        out_shape=jax.ShapeDtypeStruct((4 * CELLS, C), BF16),
        in_specs=[far] * 7,
        out_specs=vmem,
        scratch_shapes=[
            pltpu.SMEM((PROMPT_SAMPLES,), jnp.int32),
            pltpu.VMEM((27 * LATENT_CHANNELS, C), BF16),
            pltpu.VMEM((C,), F32), pltpu.VMEM((C,), F32), pltpu.VMEM((C,), F32),
            pltpu.VMEM((16, 4 * CELLS), BF16),
            pltpu.VMEM((27, 24, C), BF16),
            pltpu.VMEM((4, 16, PLANE), BF16),
            pltpu.VMEM((2, 16, 16, PLANE), BF16),
            pltpu.VMEM((4, 10, 144, PLANE), BF16),
            pltpu.VMEM((4, 8, CELLS, 3 * C), BF16),
            pltpu.VMEM((8, 4 * CELLS, C), BF16),
        ]
        + [pltpu.VMEM((SLICES, n, 24, 128), BF16) for n in pairs]
        + [pltpu.VMEM((16, n, 24, 128), BF16) for n in pairs]
        + [
            pltpu.VMEM((3, 3 * C, 256), BF16),
            pltpu.VMEM((2, 4, 10, PLANE, 128), F32),
            pltpu.VMEM((2, 2, 2, 2 * CELLS, 128), BF16),
            pltpu.VMEM((SLICES, 2, 2 * CELLS, 128), BF16),
            dma((13,)), dma((17,)), dma((3, 3)), dma((3, 4)), dma((3, 4)), dma((3, 4)),
            dma((3, 4, 2)), dma((3, 4, 2)), dma((2, 2, 2)), dma((3, 2)), dma((11,)), pltpu.SemaphoreType.REGULAR,
        ],
        compiler_params=pltpu.CompilerParams(
            collective_id=0, has_side_effects=True, vmem_limit_bytes=56 * 1024 * 1024
        ),
        cost_estimate=pl.CostEstimate(flops=5_000_000_000, bytes_accessed=2_000_000, transcendentals=600_000),
    )(
        sharded_latents,
        sample_frame_count,
        entry_kernel.reshape(27 * LATENT_CHANNELS, C),
        entry_bias,
        norm_scale_gain,
        residual_bias,
        residual_kernel,
    )
    return out.reshape(4, LATENT_ROWS, LATENT_COLUMNS, C)


def solution(mesh):
    in_specs = (P("groups", "tm"), P("groups"), P(), P(), P(), P(None, "tm", None), P())
    out_specs = P(("groups", "tm"), None, None, None)
    sliced = mesh.shape["groups"] == 2 and mesh.shape["tm"] == 16
    body = sliced_shards if sliced else shards
    return jax.shard_map(body, mesh=mesh, in_specs=in_specs, out_specs=out_specs, check_vma=False)
```

```python
import jax
import jax.numpy as jnp
from jax import lax
from jax.experimental import pallas as pl
from jax.experimental.pallas import tpu as pltpu
from jax.sharding import PartitionSpec as P

LATENT_CHANNELS = 16
C = 384
PROMPT_SAMPLES = 8
BLOCK_FRAMES = 4
LATENT_ROWS = 6
LATENT_COLUMNS = 16


def from_behind(block, axis, distance):
    devices = range(lax.axis_size(axis))
    route = [(i - distance, i) for i in devices if i - distance in devices]
    return lax.ppermute(block, axis, route)


def causal_conv(frames, weight):
    frames_out = frames.shape[0] - 2
    inputs = frames.shape[3]
    padded = jnp.pad(frames, ((0, 0), (1, 1), (1, 1), (0, 0)))
    total = jnp.zeros((frames_out * LATENT_ROWS * LATENT_COLUMNS, weight.shape[2]), jnp.float32)
    for time_tap in range(3):
        for row_tap in range(3):
            for col_tap in range(3):
                window = padded[
                    time_tap : time_tap + frames_out,
                    row_tap : row_tap + LATENT_ROWS,
                    col_tap : col_tap + LATENT_COLUMNS,
                    :,
                ]
                window = window.reshape(frames_out * LATENT_ROWS * LATENT_COLUMNS, inputs)
                tap = 9 * time_tap + 3 * row_tap + col_tap
                total = total + jnp.dot(window, weight[tap], preferred_element_type=jnp.float32)
    return total


def activate(stream, norm_scale_gain):
    values = stream.astype(jnp.float32)
    scale = lax.rsqrt(jnp.mean(values * values, axis=-1, keepdims=True) + 1e-06)
    return jax.nn.silu(values * scale * norm_scale_gain).astype(jnp.bfloat16)


def to_cells(planes):
    return jnp.transpose(
        planes.reshape(planes.shape[0], LATENT_CHANNELS, LATENT_ROWS, LATENT_COLUMNS), (0, 2, 3, 1)
    )


def shards(
    sharded_latents,
    sample_frame_count,
    entry_kernel,
    entry_bias,
    norm_scale_gain,
    residual_kernel,
    residual_bias,
):
    gathered_latents = lax.all_to_all(
        sharded_latents, "tm", split_axis=0, concat_axis=1, tiled=True
    )
    latent_volume = gathered_latents.reshape(
        BLOCK_FRAMES, LATENT_CHANNELS, LATENT_ROWS * LATENT_COLUMNS
    )
    position = lax.axis_index("tm")
    block = position // PROMPT_SAMPLES
    sample = position % PROMPT_SAMPLES
    keep = block > 0
    earlier = from_behind(latent_volume, "tm", PROMPT_SAMPLES)
    earlier = jnp.where(keep, earlier, jnp.zeros_like(earlier))
    frames = to_cells(jnp.concatenate([earlier, latent_volume], axis=0))
    widened = (causal_conv(frames, entry_kernel) + entry_bias).astype(jnp.bfloat16)
    active_all = activate(widened, norm_scale_gain).reshape(
        BLOCK_FRAMES + 2, LATENT_ROWS, LATENT_COLUMNS, C
    )
    behind = jnp.where(keep, active_all[:2], jnp.zeros_like(active_all[:2]))
    extended = jnp.concatenate([behind, active_all[2:]], axis=0)
    stream = widened[2 * LATENT_ROWS * LATENT_COLUMNS :]
    kernel_all = lax.all_gather(residual_kernel, "tm", axis=1, tiled=True)
    branch = causal_conv(extended, kernel_all)
    total = (stream.astype(jnp.float32) + (branch + residual_bias)).reshape(
        BLOCK_FRAMES, LATENT_ROWS, LATENT_COLUMNS, C
    )
    limit = jnp.sum(jnp.where(jnp.arange(PROMPT_SAMPLES) == sample, sample_frame_count, 0))
    frame_index = block * BLOCK_FRAMES + jnp.arange(BLOCK_FRAMES)
    valid = (frame_index < limit)[:, None, None, None]
    return jnp.where(valid, total, jnp.zeros_like(total)).astype(jnp.bfloat16)


MESH = pl.DeviceIdType.MESH
F32, BF16 = jnp.float32, jnp.bfloat16
CELLS = LATENT_ROWS * LATENT_COLUMNS
PLANE = 128
HALF = 64
SLICES = 3
PAIRS = ((8, 7), (6, 5), (4, 3), (2, 1), (0,))
CHUNKS = ((0, 1), (2, 3))


def section_kernel(
    lat_far, counts_far, entry_far, entry_bias_far, gain_far, residual_bias_far, taps_far,
    out,
    counts, entry, entry_bias, gain, residual_bias, lat_raw, taps, latq, lat, at, act, kept,
    piece_a, piece_b, block_a, block_b, right, acc, done, got,
    lat_send, lat_recv, z_send, z_recv, y_send, y_recv, c_send, c_recv, o_send, o_recv, own, late,
):
    x = lax.axis_index("groups")
    me = lax.axis_index("tm")
    z, y, c = me // 4, (me // 2) % 2, me % 2
    pieces = (piece_a, piece_b)
    blocks = (block_a, block_b)

    barrier = pltpu.get_barrier_semaphore()

    @pl.when(z < SLICES)
    def _():
        for step in range(1, 16):
            pl.semaphore_signal(barrier, inc=1, device_id={"tm": lax.rem(me + step, 16)}, device_id_type=MESH)
        for step in range(16):
            pl.semaphore_signal(
                barrier, inc=1, device_id={"groups": 1 - x, "tm": lax.rem(me + step, 16)}, device_id_type=MESH
            )

    first_copies = [
        pltpu.make_async_copy(lat_far, lat_raw, own.at[0]),
        pltpu.make_async_copy(taps_far, taps, own.at[1]),
        pltpu.make_async_copy(entry_far, entry, own.at[2]),
        pltpu.make_async_copy(entry_bias_far, entry_bias, own.at[3]),
        pltpu.make_async_copy(gain_far, gain, own.at[4]),
        pltpu.make_async_copy(residual_bias_far, residual_bias, own.at[5]),
        pltpu.make_async_copy(counts_far, counts, own.at[10]),
    ]
    for copy in first_copies:
        copy.start()
    first_copies[0].wait()
    cell_rows = lat_raw[...].astype(F32)
    quads = [cell_rows[:, CELLS * q : CELLS * q + CELLS] for q in range(4)]
    quads = jnp.concatenate([jnp.concatenate([q, jnp.zeros((16, PLANE - CELLS), F32)], axis=1) for q in quads], axis=0)
    to_ = lax.broadcasted_iota(jnp.int32, (64, 64), 0)
    from_ = lax.broadcasted_iota(jnp.int32, (64, 64), 1)
    pick = from_ == (to_ % 4) * 16 + ((to_ % 16) // 8) * 8 + ((to_ // 4) % 2) * 4 + to_ // 16
    picked = jnp.dot(pick.astype(F32).astype(BF16), quads.astype(BF16), preferred_element_type=F32)
    latq[...] = picked.astype(BF16).reshape(4, 16, PLANE)
    pl.semaphore_wait(barrier, jnp.where(z < SLICES, 23, 24))

    @pl.when(z == SLICES)
    def _():
        for g in range(2):
            for n in range(SLICES):
                pl.semaphore_signal(
                    late, inc=1, device_id={"groups": g, "tm": n * 4 + y * 2 + c}, device_id_type=MESH
                )

    def remote(src, dst, send, recv, device):
        return pltpu.make_async_remote_copy(
            src_ref=src, dst_ref=dst, send_sem=send, recv_sem=recv, device_id=device, device_id_type=MESH
        )

    def columns(n):
        return pl.ds(pl.multiple_of(128 * n, 128), 128)

    def source_of(zz, yy, cc):
        return zz * 4 + yy * 2 + cc

    def lat_copy(to):
        return remote(latq.at[to % 4], lat.at[x, me], lat_send.at[to], lat_recv.at[me], {"tm": to})

    def group_copy(g):
        return remote(lat.at[g], lat.at[g], lat_send.at[12], lat_recv.at[16], {"groups": 1 - x, "tm": me})

    def z_copy(ch, n):
        return remote(
            pieces[ch].at[n], blocks[ch].at[me], z_send.at[ch, n], z_recv.at[ch, z], {"tm": source_of(n, y, c)}
        )

    def z_arrival(ch, zz):
        b = blocks[ch].at[source_of(zz, y, c)]
        return remote(b, b, z_send.at[ch, 0], z_recv.at[ch, zz], {"tm": source_of(zz, y, c)})

    def y_copy(ch, zz, source=None):
        b = blocks[ch].at[source_of(zz, y, c)]
        return remote(
            b if source is None else source, b, y_send.at[ch, zz], y_recv.at[ch, zz], {"tm": source_of(z, 1 - y, c)}
        )

    def y_arrival(ch, zz):
        b = blocks[ch].at[source_of(zz, 1 - y, c)]
        return remote(b, b, y_send.at[ch, zz], y_recv.at[ch, zz], {"tm": source_of(z, 1 - y, c)})

    def c_copy(ch, zz, yy, source=None):
        b = blocks[ch].at[source_of(zz, yy, c)]
        return remote(
            b if source is None else source, b, c_send.at[ch, zz, yy], c_recv.at[ch, zz, yy],
            {"tm": source_of(z, y, 1 - c)},
        )

    def c_arrival(ch, zz, yy):
        b = blocks[ch].at[source_of(zz, yy, 1 - c)]
        return remote(b, b, c_send.at[ch, zz, yy], c_recv.at[ch, zz, yy], {"tm": source_of(z, y, 1 - c)})

    def o_copy(g, h, b):
        return remote(
            done.at[g, h, b], got.at[z, x], o_send.at[g, h, b], o_recv.at[z, x],
            {"groups": g, "tm": source_of(2 * b + h, y, c)},
        )

    def o_arrival(n, xx):
        return remote(
            done.at[0, 0, 0], got.at[n, xx], o_send.at[0, 0, 0], o_recv.at[n, xx],
            {"groups": xx, "tm": source_of(n, y, c)},
        )

    for to in range(12):
        @pl.when(to != me)
        def _():
            lat_copy(to).start()

    first_copies[1].wait()
    keeps = (lax.broadcasted_iota(jnp.int32, (24, 128), 1) < HALF) == (x == 0)

    def halves(low, high, s):
        a = taps[low, :, 128 * s : 128 * s + 128].astype(F32)
        b = taps[high, :, 128 * s : 128 * s + 128].astype(F32)
        still = jnp.where(x == 0, a, b)
        moved = pltpu.roll(jnp.where(x == 0, b, a), HALF, 1)
        return jnp.where(keeps, still, moved).astype(BF16)

    for ch, pairs in enumerate(CHUNKS):
        for s in range(SLICES):
            if ch == 1:
                piece_b[s, 6] = halves(0, 1, s)
                piece_b[s, 7] = halves(2, 2, s)
            for n, p in enumerate(pairs):
                low, high = PAIRS[p]
                for k in range(3):
                    pieces[ch][s, 3 * n + k] = halves(3 * low + k, 3 * high + k, s)
        for n in range(SLICES):
            @pl.when(n != z)
            def _():
                z_copy(ch, n).start()

        @pl.when(z < SLICES)
        def _():
            y_copy(ch, z, pieces[ch].at[z]).start()
            c_copy(ch, z, y, pieces[ch].at[z]).start()

        if ch < 1:
            for n in range(SLICES):
                @pl.when(z == SLICES)
                def _():
                    z_copy(ch, n).wait_send()

    @pl.when(z < SLICES)
    def _():
        mine = [pltpu.make_async_copy(latq.at[me % 4], lat.at[x, me], own.at[6])]
        for ch in range(2):
            mine.append(pltpu.make_async_copy(pieces[ch].at[z], blocks[ch].at[me], own.at[7 + ch]))
        for copy in mine:
            copy.start()

        def other(step):
            return SLICES if step == 2 else step + jnp.where(step >= z, 1, 0)

        def forward(ch, *steps):
            for step in steps:
                zz = other(step)
                z_arrival(ch, zz).wait_recv()
                y_copy(ch, zz).start()
                c_copy(ch, zz, y).start()

        def across(ch, *steps):
            for step in steps:
                zz = z if step < 0 else other(step)
                y_arrival(ch, zz).wait_recv()
                c_copy(ch, zz, 1 - y).start()

        def from_sibling(ch):
            for yy in range(2):
                for zz in range(4):
                    c_arrival(ch, zz, yy).wait_recv()

        at[:, 0:2] = jnp.zeros((4, 2, 144, PLANE), BF16)

        def clear(n, carry):
            acc[n // 4, n % 4] = jnp.zeros((10, PLANE, 128), F32)
            return carry

        lax.fori_loop(0, 8, clear, 0)
        for copy in first_copies[2:]:
            copy.wait()
        for copy in mine:
            copy.wait()
        forward(0, 0, 1)
        for source in range(16):
            @pl.when(source != me)
            def _():
                remote(
                    latq.at[0], lat.at[x, source], lat_send.at[0], lat_recv.at[source], {"tm": source}
                ).wait_recv()
        group_copy(x).start()
        target = lax.broadcasted_iota(jnp.int32, (256, 256), 0)
        origin = lax.broadcasted_iota(jnp.int32, (256, 256), 1)
        h_, b_, g_, ch_ = target // 128, (target // 64) % 2, (target // 16) % 4, target % 16
        perm = (origin == (g_ * 4 + ch_ // 4) * 16 + (b_ * 2 + h_) * 4 + ch_ % 4).astype(F32).astype(BF16)
        lane = lax.broadcasted_iota(jnp.int32, (256, PLANE), 1)
        row, column = lane // LATENT_COLUMNS, lane % LATENT_COLUMNS

        def spread(g):
            cells = jnp.dot(perm, lat[g].reshape(256, PLANE), preferred_element_type=F32)
            for j in range(3):
                for k in range(3):
                    offset = (j - 1) * LATENT_COLUMNS + (k - 1)
                    moved = pltpu.roll(cells, (-offset) % PLANE, 1) if offset else cells
                    good = (
                        (row + (j - 1) >= 0)
                        & (row + (j - 1) < LATENT_ROWS)
                        & (column + (k - 1) >= 0)
                        & (column + (k - 1) < LATENT_COLUMNS)
                    )
                    tap = 3 * j + k
                    at[pl.ds(2 * g, 2), 2:, tap * 16 : tap * 16 + 16, :] = (
                        jnp.where(good, moved, 0.0).astype(BF16).reshape(2, 8, 16, PLANE)
                    )

        def inlet(index, carry):
            h, b = index // 2, index % 2
            left = jnp.concatenate([at[h, pl.ds(4 * b + q, 3)].reshape(432, PLANE) for q in range(4)], axis=1)
            wide = lax.dot_general(left, entry[...], (((0,), (0,)), ((), ())), preferred_element_type=F32)
            wide = wide.reshape(4, PLANE, C)[:, :CELLS].reshape(4 * CELLS, C)
            stream = (wide + entry_bias[...][None, :]).astype(BF16)
            kept[index] = stream
            values = stream.astype(F32)
            scale = lax.rsqrt(jnp.mean(values * values, axis=-1, keepdims=True) + 1e-06)
            half_u = values * scale * (0.5 * gain[...])[None, :]
            active = (half_u + half_u * jnp.tanh(half_u)).astype(BF16).astype(F32)
            column = lax.broadcasted_iota(jnp.int32, (4 * CELLS, C), 0) % LATENT_COLUMNS
            before = jnp.where(column == 0, 0.0, pltpu.roll(active, 1, 0))
            behind = jnp.where(column == LATENT_COLUMNS - 1, 0.0, pltpu.roll(active, 4 * CELLS - 1, 0))
            for k, moved in enumerate((before, active, behind)):
                act[h, pl.ds(4 * b, 4), :, k * C : k * C + C] = moved.astype(BF16).reshape(4, CELLS, C)
            return carry

        def prepare_last():
            for n in range(2):
                piece = block_b[:, 6 + n].astype(F32).reshape(C, 128).astype(BF16)
                right[2, :C, 128 * n : 128 * n + 128] = piece

        def sweep_last(h):
            left = act[h, :6, :, C : 2 * C].reshape(6 * CELLS, C)
            wide = jnp.dot(left, right[2, :C], preferred_element_type=F32)
            column = lax.broadcasted_iota(jnp.int32, (6 * CELLS, 128), 0) % LATENT_COLUMNS
            before = jnp.where(column == 0, 0.0, pltpu.roll(wide[:, :128], 1, 0))
            behind = jnp.where(column == LATENT_COLUMNS - 1, 0.0, pltpu.roll(wide[:, 128:], 6 * CELLS - 1, 0))
            acc[0, h, 2:8, 32 : 32 + CELLS] += (before + behind).reshape(6, CELLS, 128)
            acc[1, h, 2:8, 32 : 32 + CELLS] += wide[:, :128].reshape(6, CELLS, 128)

        def prepare(ch):
            for n in range(len(CHUNKS[ch])):
                for k in range(3):
                    piece = blocks[ch][:, 3 * n + k].astype(F32).reshape(C, 128).astype(BF16)
                    right[ch, k * C : k * C + C, n * 128 : n * 128 + 128] = piece

        def sweep(h, ch, frames):
            pairs = CHUNKS[ch]
            left = act[h, :frames].reshape(frames * CELLS, 3 * C)
            wide = jnp.dot(left, right[ch, :, : 128 * len(pairs)], preferred_element_type=F32)
            for n, p in enumerate(pairs):
                part = wide[:, 128 * n : 128 * n + 128].reshape(frames, CELLS, 128)
                for side, slot in enumerate(PAIRS[p]):
                    i, j = slot // 3, slot % 3
                    acc[side, h, 2 - i : 2 - i + frames, 16 * (2 - j) : 16 * (2 - j) + CELLS] += part

        def both_groups(step, carry):
            g = jnp.where(step == 0, x, 1 - x)

            @pl.when(step == 1)
            def _():
                group_copy(g).wait_recv()

            spread(g)

            @pl.when(step == 0)
            def _():
                forward(1, 0, 1)

            lax.fori_loop(4 * g, 4 * g + 2, inlet, 0)

            @pl.when(step == 0)
            def _():
                forward(0, 2)
                across(0, -1, 0, 1)

            @pl.when(step == 1)
            def _():
                across(0, 2)
                across(1, 0, 1)

            lax.fori_loop(4 * g + 2, 4 * g + 4, inlet, 0)

            @pl.when(step == 0)
            def _():
                forward(1, 2)
                across(1, -1)

            return carry

        lax.fori_loop(0, 2, both_groups, 0)
        across(1, 2)
        from_sibling(0)
        prepare(0)

        def first(step, carry):
            sweep(2 * step + 1, 0, 8)
            return carry

        lax.fori_loop(0, 2, first, 0)
        from_sibling(1)
        prepare(1)
        prepare_last()
        pl.semaphore_wait(late, 2)
        edge = lax.broadcasted_iota(jnp.int32, (2, CELLS, 128), 2) < HALF
        bias = residual_bias[columns(z)][None, :]
        bias = jnp.where(x == 0, bias, pltpu.roll(jnp.broadcast_to(bias, (8, 128)), HALF, 1)[:1])

        def finish(step, carry):
            g, h = step % 2, 1 - step // 2
            gh = 2 * g + h

            @pl.when(step >= 2)
            def _():
                sweep(gh, 0, 8)

            sweep(gh, 1, 7)
            sweep_last(gh)
            for b in (1, 0):
                stream = kept[2 * gh + b, :, columns(z)].astype(F32)
                stream = jnp.where(x == 0, stream, pltpu.roll(stream, HALF, 1))
                even = acc[0, gh, 4 * b : 4 * b + 4, 16 : 16 + CELLS].reshape(4 * CELLS, 128)
                odd = acc[1, gh, 4 * b : 4 * b + 4, 16 : 16 + CELLS].reshape(4 * CELLS, 128)
                total = stream + (even + pltpu.roll(odd, HALF, 1) + bias)
                top = total[: 2 * CELLS].reshape(2, CELLS, 128)
                low = pltpu.roll(total[2 * CELLS :], HALF, 1).reshape(2, CELLS, 128)
                done[g, h, b] = jnp.where(edge, top, low).astype(BF16).reshape(2 * CELLS, 128)

                @pl.when((g != x) | (2 * b + h != z))
                def _():
                    o_copy(g, h, b).start()

            return carry

        lax.fori_loop(0, 4, finish, 0)
        got[z, x] = done[x, z % 2, z // 2]

    for n in range(SLICES):
        for xx in range(2):
            @pl.when((n != z) | (xx != x))
            def _():
                o_arrival(n, xx).wait_recv()
    @pl.when(z == SLICES)
    def _():
        for copy in first_copies[2:]:
            copy.wait()

    limit = counts[me % PROMPT_SAMPLES]
    frame = lax.broadcasted_iota(jnp.int32, (2, CELLS, 128), 0) + BLOCK_FRAMES * (me // PROMPT_SAMPLES)
    half = lax.broadcasted_iota(jnp.int32, (2, CELLS, 128), 2) < HALF
    for n in range(SLICES):
        near_half = got[n, 0].astype(F32)
        far_half = got[n, 1].astype(F32)
        top = jnp.where(half, near_half.reshape(2, CELLS, 128), pltpu.roll(far_half, HALF, 1).reshape(2, CELLS, 128))
        low = jnp.where(half, pltpu.roll(near_half, HALF, 1).reshape(2, CELLS, 128), far_half.reshape(2, CELLS, 128))
        for first_frame, values in ((0, top), (2, low)):
            values = jnp.where(frame + first_frame < limit, values, 0.0).astype(BF16)
            out[CELLS * first_frame : CELLS * (first_frame + 2), 128 * n : 128 * n + 128] = values.reshape(2 * CELLS, 128)

    for n in range(SLICES):
        @pl.when(n != z)
        def _():
            z_copy(1, n).wait_send()

            @pl.when(z < SLICES)
            def _():
                z_copy(0, n).wait_send()

    for to in range(12):
        @pl.when(to != me)
        def _():
            lat_copy(to).wait_send()

    @pl.when(z < SLICES)
    def _():
        group_copy(x).wait_send()
        for ch in range(2):
            for zz in range(4):
                y_copy(ch, zz).wait_send()
                for yy in range(2):
                    c_copy(ch, zz, yy).wait_send()
        for g in range(2):
            for h in range(2):
                for b in range(2):
                    @pl.when((g != x) | (2 * b + h != z))
                    def _():
                        o_copy(g, h, b).wait_send()


def sliced_shards(
    sharded_latents,
    sample_frame_count,
    entry_kernel,
    entry_bias,
    norm_scale_gain,
    residual_kernel,
    residual_bias,
):
    vmem = pl.BlockSpec(memory_space=pltpu.VMEM)
    far = pl.BlockSpec(memory_space=pltpu.HBM)
    dma = pltpu.SemaphoreType.DMA
    pairs = (6, 8)
    out = pl.pallas_call(
        section_kernel,
        out_shape=jax.ShapeDtypeStruct((4 * CELLS, C), BF16),
        in_specs=[far] * 7,
        out_specs=vmem,
        scratch_shapes=[
            pltpu.SMEM((PROMPT_SAMPLES,), jnp.int32),
            pltpu.VMEM((27 * LATENT_CHANNELS, C), BF16),
            pltpu.VMEM((C,), F32), pltpu.VMEM((C,), F32), pltpu.VMEM((C,), F32),
            pltpu.VMEM((16, 4 * CELLS), BF16),
            pltpu.VMEM((27, 24, C), BF16),
            pltpu.VMEM((4, 16, PLANE), BF16),
            pltpu.VMEM((2, 16, 16, PLANE), BF16),
            pltpu.VMEM((4, 10, 144, PLANE), BF16),
            pltpu.VMEM((4, 8, CELLS, 3 * C), BF16),
            pltpu.VMEM((8, 4 * CELLS, C), BF16),
        ]
        + [pltpu.VMEM((SLICES, n, 24, 128), BF16) for n in pairs]
        + [pltpu.VMEM((16, n, 24, 128), BF16) for n in pairs]
        + [
            pltpu.VMEM((3, 3 * C, 256), BF16),
            pltpu.VMEM((2, 4, 10, PLANE, 128), F32),
            pltpu.VMEM((2, 2, 2, 2 * CELLS, 128), BF16),
            pltpu.VMEM((SLICES, 2, 2 * CELLS, 128), BF16),
            dma((13,)), dma((17,)), dma((3, 3)), dma((3, 4)), dma((3, 4)), dma((3, 4)),
            dma((3, 4, 2)), dma((3, 4, 2)), dma((2, 2, 2)), dma((3, 2)), dma((11,)), pltpu.SemaphoreType.REGULAR,
        ],
        compiler_params=pltpu.CompilerParams(
            collective_id=0, has_side_effects=True, vmem_limit_bytes=56 * 1024 * 1024
        ),
        cost_estimate=pl.CostEstimate(flops=5_000_000_000, bytes_accessed=2_000_000, transcendentals=600_000),
    )(
        sharded_latents,
        sample_frame_count,
        entry_kernel.reshape(27 * LATENT_CHANNELS, C),
        entry_bias,
        norm_scale_gain,
        residual_bias,
        residual_kernel,
    )
    return out.reshape(4, LATENT_ROWS, LATENT_COLUMNS, C)


def solution(mesh):
    in_specs = (P("groups", "tm"), P("groups"), P(), P(), P(), P(None, "tm", None), P())
    out_specs = P(("groups", "tm"), None, None, None)
    sliced = mesh.shape["groups"] == 2 and mesh.shape["tm"] == 16
    body = sliced_shards if sliced else shards
    return jax.shard_map(body, mesh=mesh, in_specs=in_specs, out_specs=out_specs, check_vma=False)
```

```python
import jax
import jax.numpy as jnp
from jax import lax
from jax.experimental import pallas as pl
from jax.experimental.pallas import tpu as pltpu
from jax.sharding import PartitionSpec as P

LATENT_CHANNELS = 16
C = 384
PROMPT_SAMPLES = 8
BLOCK_FRAMES = 4
LATENT_ROWS = 6
LATENT_COLUMNS = 16


def from_behind(block, axis, distance):
    devices = range(lax.axis_size(axis))
    route = [(i - distance, i) for i in devices if i - distance in devices]
    return lax.ppermute(block, axis, route)


def causal_conv(frames, weight):
    frames_out = frames.shape[0] - 2
    inputs = frames.shape[3]
    padded = jnp.pad(frames, ((0, 0), (1, 1), (1, 1), (0, 0)))
    total = jnp.zeros((frames_out * LATENT_ROWS * LATENT_COLUMNS, weight.shape[2]), jnp.float32)
    for time_tap in range(3):
        for row_tap in range(3):
            for col_tap in range(3):
                window = padded[
                    time_tap : time_tap + frames_out,
                    row_tap : row_tap + LATENT_ROWS,
                    col_tap : col_tap + LATENT_COLUMNS,
                    :,
                ]
                window = window.reshape(frames_out * LATENT_ROWS * LATENT_COLUMNS, inputs)
                tap = 9 * time_tap + 3 * row_tap + col_tap
                total = total + jnp.dot(window, weight[tap], preferred_element_type=jnp.float32)
    return total


def activate(stream, norm_scale_gain):
    values = stream.astype(jnp.float32)
    scale = lax.rsqrt(jnp.mean(values * values, axis=-1, keepdims=True) + 1e-06)
    return jax.nn.silu(values * scale * norm_scale_gain).astype(jnp.bfloat16)


def to_cells(planes):
    return jnp.transpose(
        planes.reshape(planes.shape[0], LATENT_CHANNELS, LATENT_ROWS, LATENT_COLUMNS), (0, 2, 3, 1)
    )


def shards(
    sharded_latents,
    sample_frame_count,
    entry_kernel,
    entry_bias,
    norm_scale_gain,
    residual_kernel,
    residual_bias,
):
    gathered_latents = lax.all_to_all(
        sharded_latents, "tm", split_axis=0, concat_axis=1, tiled=True
    )
    latent_volume = gathered_latents.reshape(
        BLOCK_FRAMES, LATENT_CHANNELS, LATENT_ROWS * LATENT_COLUMNS
    )
    position = lax.axis_index("tm")
    block = position // PROMPT_SAMPLES
    sample = position % PROMPT_SAMPLES
    keep = block > 0
    earlier = from_behind(latent_volume, "tm", PROMPT_SAMPLES)
    earlier = jnp.where(keep, earlier, jnp.zeros_like(earlier))
    frames = to_cells(jnp.concatenate([earlier, latent_volume], axis=0))
    widened = (causal_conv(frames, entry_kernel) + entry_bias).astype(jnp.bfloat16)
    active_all = activate(widened, norm_scale_gain).reshape(
        BLOCK_FRAMES + 2, LATENT_ROWS, LATENT_COLUMNS, C
    )
    behind = jnp.where(keep, active_all[:2], jnp.zeros_like(active_all[:2]))
    extended = jnp.concatenate([behind, active_all[2:]], axis=0)
    stream = widened[2 * LATENT_ROWS * LATENT_COLUMNS :]
    kernel_all = lax.all_gather(residual_kernel, "tm", axis=1, tiled=True)
    branch = causal_conv(extended, kernel_all)
    total = (stream.astype(jnp.float32) + (branch + residual_bias)).reshape(
        BLOCK_FRAMES, LATENT_ROWS, LATENT_COLUMNS, C
    )
    limit = jnp.sum(jnp.where(jnp.arange(PROMPT_SAMPLES) == sample, sample_frame_count, 0))
    frame_index = block * BLOCK_FRAMES + jnp.arange(BLOCK_FRAMES)
    valid = (frame_index < limit)[:, None, None, None]
    return jnp.where(valid, total, jnp.zeros_like(total)).astype(jnp.bfloat16)


MESH = pl.DeviceIdType.MESH
F32, BF16 = jnp.float32, jnp.bfloat16
CELLS = LATENT_ROWS * LATENT_COLUMNS
PLANE = 128
HALF = 64
SLICES = 3
PAIRS = ((8, 7), (6, 5), (4, 3), (2, 1), (0,))
CHUNKS = ((0, 1), (2, 3))


def section_kernel(
    lat_far, counts_far, entry_far, entry_bias_far, gain_far, residual_bias_far, taps_far,
    out,
    counts, entry, entry_bias, gain, residual_bias, lat_raw, taps, latq, lat, at, act, kept,
    piece_a, piece_b, block_a, block_b, right, acc, done, got,
    lat_send, lat_recv, z_send, z_recv, y_send, y_recv, c_send, c_recv, o_send, o_recv, own, late,
):
    x = lax.axis_index("groups")
    me = lax.axis_index("tm")
    z, y, c = me // 4, (me // 2) % 2, me % 2
    pieces = (piece_a, piece_b)
    blocks = (block_a, block_b)

    barrier = pltpu.get_barrier_semaphore()

    @pl.when(z < SLICES)
    def _():
        for step in range(1, 16):
            pl.semaphore_signal(barrier, inc=1, device_id={"tm": lax.rem(me + step, 16)}, device_id_type=MESH)
        for step in range(16):
            pl.semaphore_signal(
                barrier, inc=1, device_id={"groups": 1 - x, "tm": lax.rem(me + step, 16)}, device_id_type=MESH
            )

    first_copies = [
        pltpu.make_async_copy(lat_far, lat_raw, own.at[0]),
        pltpu.make_async_copy(taps_far, taps, own.at[1]),
        pltpu.make_async_copy(entry_far, entry, own.at[2]),
        pltpu.make_async_copy(entry_bias_far, entry_bias, own.at[3]),
        pltpu.make_async_copy(gain_far, gain, own.at[4]),
        pltpu.make_async_copy(residual_bias_far, residual_bias, own.at[5]),
        pltpu.make_async_copy(counts_far, counts, own.at[10]),
    ]
    for copy in first_copies:
        copy.start()
    first_copies[0].wait()
    cell_rows = lat_raw[...].astype(F32)
    quads = [cell_rows[:, CELLS * q : CELLS * q + CELLS] for q in range(4)]
    quads = jnp.concatenate([jnp.concatenate([q, jnp.zeros((16, PLANE - CELLS), F32)], axis=1) for q in quads], axis=0)
    to_ = lax.broadcasted_iota(jnp.int32, (64, 64), 0)
    from_ = lax.broadcasted_iota(jnp.int32, (64, 64), 1)
    pick = from_ == (to_ % 4) * 16 + ((to_ % 16) // 8) * 8 + ((to_ // 4) % 2) * 4 + to_ // 16
    picked = jnp.dot(pick.astype(F32).astype(BF16), quads.astype(BF16), preferred_element_type=F32)
    latq[...] = picked.astype(BF16).reshape(4, 16, PLANE)
    pl.semaphore_wait(barrier, jnp.where(z < SLICES, 23, 24))

    @pl.when(z == SLICES)
    def _():
        for g in range(2):
            for n in range(SLICES):
                pl.semaphore_signal(
                    late, inc=1, device_id={"groups": g, "tm": n * 4 + y * 2 + c}, device_id_type=MESH
                )

    def remote(src, dst, send, recv, device):
        return pltpu.make_async_remote_copy(
            src_ref=src, dst_ref=dst, send_sem=send, recv_sem=recv, device_id=device, device_id_type=MESH
        )

    def columns(n):
        return pl.ds(pl.multiple_of(128 * n, 128), 128)

    def source_of(zz, yy, cc):
        return zz * 4 + yy * 2 + cc

    def lat_copy(to):
        return remote(latq.at[to % 4], lat.at[x, me], lat_send.at[to], lat_recv.at[me], {"tm": to})

    def group_copy(g):
        return remote(lat.at[g], lat.at[g], lat_send.at[12], lat_recv.at[16], {"groups": 1 - x, "tm": me})

    def z_copy(ch, n):
        return remote(
            pieces[ch].at[n], blocks[ch].at[me], z_send.at[ch, n], z_recv.at[ch, z], {"tm": source_of(n, y, c)}
        )

    def z_arrival(ch, zz):
        b = blocks[ch].at[source_of(zz, y, c)]
        return remote(b, b, z_send.at[ch, 0], z_recv.at[ch, zz], {"tm": source_of(zz, y, c)})

    def y_copy(ch, zz, source=None):
        b = blocks[ch].at[source_of(zz, y, c)]
        return remote(
            b if source is None else source, b, y_send.at[ch, zz], y_recv.at[ch, zz], {"tm": source_of(z, 1 - y, c)}
        )

    def y_arrival(ch, zz):
        b = blocks[ch].at[source_of(zz, 1 - y, c)]
        return remote(b, b, y_send.at[ch, zz], y_recv.at[ch, zz], {"tm": source_of(z, 1 - y, c)})

    def c_copy(ch, zz, yy, source=None):
        b = blocks[ch].at[source_of(zz, yy, c)]
        return remote(
            b if source is None else source, b, c_send.at[ch, zz, yy], c_recv.at[ch, zz, yy],
            {"tm": source_of(z, y, 1 - c)},
        )

    def c_arrival(ch, zz, yy):
        b = blocks[ch].at[source_of(zz, yy, 1 - c)]
        return remote(b, b, c_send.at[ch, zz, yy], c_recv.at[ch, zz, yy], {"tm": source_of(z, y, 1 - c)})

    def o_copy(g, h, b):
        return remote(
            done.at[g, h, b], got.at[z, x], o_send.at[g, h, b], o_recv.at[z, x],
            {"groups": g, "tm": source_of(2 * b + h, y, c)},
        )

    def o_arrival(n, xx):
        return remote(
            done.at[0, 0, 0], got.at[n, xx], o_send.at[0, 0, 0], o_recv.at[n, xx],
            {"groups": xx, "tm": source_of(n, y, c)},
        )

    for to in range(12):
        @pl.when(to != me)
        def _():
            lat_copy(to).start()

    first_copies[1].wait()
    keeps = (lax.broadcasted_iota(jnp.int32, (24, 128), 1) < HALF) == (x == 0)

    def halves(low, high, s):
        a = taps[low, :, 128 * s : 128 * s + 128].astype(F32)
        b = taps[high, :, 128 * s : 128 * s + 128].astype(F32)
        still = jnp.where(x == 0, a, b)
        moved = pltpu.roll(jnp.where(x == 0, b, a), HALF, 1)
        return jnp.where(keeps, still, moved).astype(BF16)

    for ch, pairs in enumerate(CHUNKS):
        for s in range(SLICES):
            if ch == 1:
                piece_b[s, 6] = halves(0, 1, s)
                piece_b[s, 7] = halves(2, 2, s)
            for n, p in enumerate(pairs):
                low, high = PAIRS[p]
                for k in range(3):
                    pieces[ch][s, 3 * n + k] = halves(3 * low + k, 3 * high + k, s)
        for n in range(SLICES):
            @pl.when(n != z)
            def _():
                z_copy(ch, n).start()

        @pl.when(z < SLICES)
        def _():
            y_copy(ch, z, pieces[ch].at[z]).start()
            c_copy(ch, z, y, pieces[ch].at[z]).start()

        if ch < 1:
            for n in range(SLICES):
                @pl.when(z == SLICES)
                def _():
                    z_copy(ch, n).wait_send()

    @pl.when(z < SLICES)
    def _():
        mine = [pltpu.make_async_copy(latq.at[me % 4], lat.at[x, me], own.at[6])]
        for ch in range(2):
            mine.append(pltpu.make_async_copy(pieces[ch].at[z], blocks[ch].at[me], own.at[7 + ch]))
        for copy in mine:
            copy.start()

        def other(step):
            return SLICES if step == 2 else step + jnp.where(step >= z, 1, 0)

        def forward(ch, *steps):
            for step in steps:
                zz = other(step)
                z_arrival(ch, zz).wait_recv()
                y_copy(ch, zz).start()
                c_copy(ch, zz, y).start()

        def across(ch, *steps):
            for step in steps:
                zz = z if step < 0 else other(step)
                y_arrival(ch, zz).wait_recv()
                c_copy(ch, zz, 1 - y).start()

        def from_sibling(ch):
            for yy in range(2):
                for zz in range(4):
                    c_arrival(ch, zz, yy).wait_recv()

        at[:, 0:2] = jnp.zeros((4, 2, 144, PLANE), BF16)

        def clear(n, carry):
            acc[n // 4, n % 4] = jnp.zeros((10, PLANE, 128), F32)
            return carry

        lax.fori_loop(0, 8, clear, 0)
        for copy in first_copies[2:]:
            copy.wait()
        for copy in mine:
            copy.wait()
        for source in range(16):
            @pl.when(source != me)
            def _():
                remote(
                    latq.at[0], lat.at[x, source], lat_send.at[0], lat_recv.at[source], {"tm": source}
                ).wait_recv()
        group_copy(x).start()
        forward(0, 0, 1)
        target = lax.broadcasted_iota(jnp.int32, (256, 256), 0)
        origin = lax.broadcasted_iota(jnp.int32, (256, 256), 1)
        h_, b_, g_, ch_ = target // 128, (target // 64) % 2, (target // 16) % 4, target % 16
        perm = (origin == (g_ * 4 + ch_ // 4) * 16 + (b_ * 2 + h_) * 4 + ch_ % 4).astype(F32).astype(BF16)
        lane = lax.broadcasted_iota(jnp.int32, (256, PLANE), 1)
        row, column = lane // LATENT_COLUMNS, lane % LATENT_COLUMNS

        def spread(g):
            cells = jnp.dot(perm, lat[g].reshape(256, PLANE), preferred_element_type=F32)
            for j in range(3):
                for k in range(3):
                    offset = (j - 1) * LATENT_COLUMNS + (k - 1)
                    moved = pltpu.roll(cells, (-offset) % PLANE, 1) if offset else cells
                    good = (
                        (row + (j - 1) >= 0)
                        & (row + (j - 1) < LATENT_ROWS)
                        & (column + (k - 1) >= 0)
                        & (column + (k - 1) < LATENT_COLUMNS)
                    )
                    tap = 3 * j + k
                    at[pl.ds(2 * g, 2), 2:, tap * 16 : tap * 16 + 16, :] = (
                        jnp.where(good, moved, 0.0).astype(BF16).reshape(2, 8, 16, PLANE)
                    )

        def inlet(index, carry):
            h, b = index // 2, index % 2
            left = jnp.concatenate([at[h, pl.ds(4 * b + q, 3)].reshape(432, PLANE) for q in range(4)], axis=1)
            wide = lax.dot_general(left, entry[...], (((0,), (0,)), ((), ())), preferred_element_type=F32)
            wide = wide.reshape(4, PLANE, C)[:, :CELLS].reshape(4 * CELLS, C)
            stream = (wide + entry_bias[...][None, :]).astype(BF16)
            kept[index] = stream
            values = stream.astype(F32)
            scale = lax.rsqrt(jnp.mean(values * values, axis=-1, keepdims=True) + 1e-06)
            half_u = values * scale * (0.5 * gain[...])[None, :]
            active = (half_u + half_u * jnp.tanh(half_u)).astype(BF16).astype(F32)
            column = lax.broadcasted_iota(jnp.int32, (4 * CELLS, C), 0) % LATENT_COLUMNS
            before = jnp.where(column == 0, 0.0, pltpu.roll(active, 1, 0))
            behind = jnp.where(column == LATENT_COLUMNS - 1, 0.0, pltpu.roll(active, 4 * CELLS - 1, 0))
            for k, moved in enumerate((before, active, behind)):
                act[h, pl.ds(4 * b, 4), :, k * C : k * C + C] = moved.astype(BF16).reshape(4, CELLS, C)
            return carry

        def prepare_last():
            for n in range(2):
                piece = block_b[:, 6 + n].astype(F32).reshape(C, 128).astype(BF16)
                right[2, :C, 128 * n : 128 * n + 128] = piece

        def sweep_last(h):
            left = act[h, :6, :, C : 2 * C].reshape(6 * CELLS, C)
            wide = jnp.dot(left, right[2, :C], preferred_element_type=F32)
            column = lax.broadcasted_iota(jnp.int32, (6 * CELLS, 128), 0) % LATENT_COLUMNS
            before = jnp.where(column == 0, 0.0, pltpu.roll(wide[:, :128], 1, 0))
            behind = jnp.where(column == LATENT_COLUMNS - 1, 0.0, pltpu.roll(wide[:, 128:], 6 * CELLS - 1, 0))
            acc[0, h, 2:8, 32 : 32 + CELLS] += (before + behind).reshape(6, CELLS, 128)
            acc[1, h, 2:8, 32 : 32 + CELLS] += wide[:, :128].reshape(6, CELLS, 128)

        def prepare(ch):
            for n in range(len(CHUNKS[ch])):
                for k in range(3):
                    piece = blocks[ch][:, 3 * n + k].astype(F32).reshape(C, 128).astype(BF16)
                    right[ch, k * C : k * C + C, n * 128 : n * 128 + 128] = piece

        def sweep(h, ch, frames):
            pairs = CHUNKS[ch]
            left = act[h, :frames].reshape(frames * CELLS, 3 * C)
            wide = jnp.dot(left, right[ch, :, : 128 * len(pairs)], preferred_element_type=F32)
            for n, p in enumerate(pairs):
                part = wide[:, 128 * n : 128 * n + 128].reshape(frames, CELLS, 128)
                for side, slot in enumerate(PAIRS[p]):
                    i, j = slot // 3, slot % 3
                    acc[side, h, 2 - i : 2 - i + frames, 16 * (2 - j) : 16 * (2 - j) + CELLS] += part

        def both_groups(step, carry):
            g = jnp.where(step == 0, x, 1 - x)

            @pl.when(step == 1)
            def _():
                group_copy(g).wait_recv()

            spread(g)

            @pl.when(step == 0)
            def _():
                forward(1, 0, 1)

            lax.fori_loop(4 * g, 4 * g + 2, inlet, 0)

            @pl.when(step == 0)
            def _():
                forward(0, 2)
                across(0, -1, 0, 1)

            @pl.when(step == 1)
            def _():
                across(0, 2)
                across(1, 0, 1)

            lax.fori_loop(4 * g + 2, 4 * g + 4, inlet, 0)

            @pl.when(step == 0)
            def _():
                forward(1, 2)
                across(1, -1)

            return carry

        lax.fori_loop(0, 2, both_groups, 0)
        across(1, 2)
        from_sibling(0)
        prepare(0)

        def first(step, carry):
            sweep(2 * step + 1, 0, 8)
            return carry

        lax.fori_loop(0, 2, first, 0)
        from_sibling(1)
        prepare(1)
        prepare_last()
        pl.semaphore_wait(late, 2)
        edge = lax.broadcasted_iota(jnp.int32, (2, CELLS, 128), 2) < HALF
        bias = residual_bias[columns(z)][None, :]
        bias = jnp.where(x == 0, bias, pltpu.roll(jnp.broadcast_to(bias, (8, 128)), HALF, 1)[:1])

        def finish(step, carry):
            g, h = step % 2, 1 - step // 2
            gh = 2 * g + h

            @pl.when(step >= 2)
            def _():
                sweep(gh, 0, 8)

            sweep(gh, 1, 7)
            sweep_last(gh)
            for b in (1, 0):
                stream = kept[2 * gh + b, :, columns(z)].astype(F32)
                stream = jnp.where(x == 0, stream, pltpu.roll(stream, HALF, 1))
                even = acc[0, gh, 4 * b : 4 * b + 4, 16 : 16 + CELLS].reshape(4 * CELLS, 128)
                odd = acc[1, gh, 4 * b : 4 * b + 4, 16 : 16 + CELLS].reshape(4 * CELLS, 128)
                total = stream + (even + pltpu.roll(odd, HALF, 1) + bias)
                top = total[: 2 * CELLS].reshape(2, CELLS, 128)
                low = pltpu.roll(total[2 * CELLS :], HALF, 1).reshape(2, CELLS, 128)
                done[g, h, b] = jnp.where(edge, top, low).astype(BF16).reshape(2 * CELLS, 128)

                @pl.when((g != x) | (2 * b + h != z))
                def _():
                    o_copy(g, h, b).start()

            return carry

        lax.fori_loop(0, 4, finish, 0)
        got[z, x] = done[x, z % 2, z // 2]

    for n in range(SLICES):
        for xx in range(2):
            @pl.when((n != z) | (xx != x))
            def _():
                o_arrival(n, xx).wait_recv()
    @pl.when(z == SLICES)
    def _():
        for copy in first_copies[2:]:
            copy.wait()

    limit = counts[me % PROMPT_SAMPLES]
    frame = lax.broadcasted_iota(jnp.int32, (2, CELLS, 128), 0) + BLOCK_FRAMES * (me // PROMPT_SAMPLES)
    half = lax.broadcasted_iota(jnp.int32, (2, CELLS, 128), 2) < HALF
    for n in range(SLICES):
        near_half = got[n, 0].astype(F32)
        far_half = got[n, 1].astype(F32)
        top = jnp.where(half, near_half.reshape(2, CELLS, 128), pltpu.roll(far_half, HALF, 1).reshape(2, CELLS, 128))
        low = jnp.where(half, pltpu.roll(near_half, HALF, 1).reshape(2, CELLS, 128), far_half.reshape(2, CELLS, 128))
        for first_frame, values in ((0, top), (2, low)):
            values = jnp.where(frame + first_frame < limit, values, 0.0).astype(BF16)
            out[CELLS * first_frame : CELLS * (first_frame + 2), 128 * n : 128 * n + 128] = values.reshape(2 * CELLS, 128)

    for n in range(SLICES):
        @pl.when(n != z)
        def _():
            z_copy(1, n).wait_send()

            @pl.when(z < SLICES)
            def _():
                z_copy(0, n).wait_send()

    for to in range(12):
        @pl.when(to != me)
        def _():
            lat_copy(to).wait_send()

    @pl.when(z < SLICES)
    def _():
        group_copy(x).wait_send()
        for ch in range(2):
            for zz in range(4):
                y_copy(ch, zz).wait_send()
                for yy in range(2):
                    c_copy(ch, zz, yy).wait_send()
        for g in range(2):
            for h in range(2):
                for b in range(2):
                    @pl.when((g != x) | (2 * b + h != z))
                    def _():
                        o_copy(g, h, b).wait_send()


def sliced_shards(
    sharded_latents,
    sample_frame_count,
    entry_kernel,
    entry_bias,
    norm_scale_gain,
    residual_kernel,
    residual_bias,
):
    vmem = pl.BlockSpec(memory_space=pltpu.VMEM)
    far = pl.BlockSpec(memory_space=pltpu.HBM)
    dma = pltpu.SemaphoreType.DMA
    pairs = (6, 8)
    out = pl.pallas_call(
        section_kernel,
        out_shape=jax.ShapeDtypeStruct((4 * CELLS, C), BF16),
        in_specs=[far] * 7,
        out_specs=vmem,
        scratch_shapes=[
            pltpu.SMEM((PROMPT_SAMPLES,), jnp.int32),
            pltpu.VMEM((27 * LATENT_CHANNELS, C), BF16),
            pltpu.VMEM((C,), F32), pltpu.VMEM((C,), F32), pltpu.VMEM((C,), F32),
            pltpu.VMEM((16, 4 * CELLS), BF16),
            pltpu.VMEM((27, 24, C), BF16),
            pltpu.VMEM((4, 16, PLANE), BF16),
            pltpu.VMEM((2, 16, 16, PLANE), BF16),
            pltpu.VMEM((4, 10, 144, PLANE), BF16),
            pltpu.VMEM((4, 8, CELLS, 3 * C), BF16),
            pltpu.VMEM((8, 4 * CELLS, C), BF16),
        ]
        + [pltpu.VMEM((SLICES, n, 24, 128), BF16) for n in pairs]
        + [pltpu.VMEM((16, n, 24, 128), BF16) for n in pairs]
        + [
            pltpu.VMEM((3, 3 * C, 256), BF16),
            pltpu.VMEM((2, 4, 10, PLANE, 128), F32),
            pltpu.VMEM((2, 2, 2, 2 * CELLS, 128), BF16),
            pltpu.VMEM((SLICES, 2, 2 * CELLS, 128), BF16),
            dma((13,)), dma((17,)), dma((3, 3)), dma((3, 4)), dma((3, 4)), dma((3, 4)),
            dma((3, 4, 2)), dma((3, 4, 2)), dma((2, 2, 2)), dma((3, 2)), dma((11,)), pltpu.SemaphoreType.REGULAR,
        ],
        compiler_params=pltpu.CompilerParams(
            collective_id=0, has_side_effects=True, vmem_limit_bytes=56 * 1024 * 1024
        ),
        cost_estimate=pl.CostEstimate(flops=5_000_000_000, bytes_accessed=2_000_000, transcendentals=600_000),
    )(
        sharded_latents,
        sample_frame_count,
        entry_kernel.reshape(27 * LATENT_CHANNELS, C),
        entry_bias,
        norm_scale_gain,
        residual_bias,
        residual_kernel,
    )
    return out.reshape(4, LATENT_ROWS, LATENT_COLUMNS, C)


def solution(mesh):
    in_specs = (P("groups", "tm"), P("groups"), P(), P(), P(), P(None, "tm", None), P())
    out_specs = P(("groups", "tm"), None, None, None)
    sliced = mesh.shape["groups"] == 2 and mesh.shape["tm"] == 16
    body = sliced_shards if sliced else shards
    return jax.shard_map(body, mesh=mesh, in_specs=in_specs, out_specs=out_specs, check_vma=False)
```

```python
import jax
import jax.numpy as jnp
from jax import lax
from jax.experimental import pallas as pl
from jax.experimental.pallas import tpu as pltpu
from jax.sharding import PartitionSpec as P

LATENT_CHANNELS = 16
C = 384
PROMPT_SAMPLES = 8
BLOCK_FRAMES = 4
LATENT_ROWS = 6
LATENT_COLUMNS = 16


def from_behind(block, axis, distance):
    devices = range(lax.axis_size(axis))
    route = [(i - distance, i) for i in devices if i - distance in devices]
    return lax.ppermute(block, axis, route)


def causal_conv(frames, weight):
    frames_out = frames.shape[0] - 2
    inputs = frames.shape[3]
    padded = jnp.pad(frames, ((0, 0), (1, 1), (1, 1), (0, 0)))
    total = jnp.zeros((frames_out * LATENT_ROWS * LATENT_COLUMNS, weight.shape[2]), jnp.float32)
    for time_tap in range(3):
        for row_tap in range(3):
            for col_tap in range(3):
                window = padded[
                    time_tap : time_tap + frames_out,
                    row_tap : row_tap + LATENT_ROWS,
                    col_tap : col_tap + LATENT_COLUMNS,
                    :,
                ]
                window = window.reshape(frames_out * LATENT_ROWS * LATENT_COLUMNS, inputs)
                tap = 9 * time_tap + 3 * row_tap + col_tap
                total = total + jnp.dot(window, weight[tap], preferred_element_type=jnp.float32)
    return total


def activate(stream, norm_scale_gain):
    values = stream.astype(jnp.float32)
    scale = lax.rsqrt(jnp.mean(values * values, axis=-1, keepdims=True) + 1e-06)
    return jax.nn.silu(values * scale * norm_scale_gain).astype(jnp.bfloat16)


def to_cells(planes):
    return jnp.transpose(
        planes.reshape(planes.shape[0], LATENT_CHANNELS, LATENT_ROWS, LATENT_COLUMNS), (0, 2, 3, 1)
    )


def shards(
    sharded_latents,
    sample_frame_count,
    entry_kernel,
    entry_bias,
    norm_scale_gain,
    residual_kernel,
    residual_bias,
):
    gathered_latents = lax.all_to_all(
        sharded_latents, "tm", split_axis=0, concat_axis=1, tiled=True
    )
    latent_volume = gathered_latents.reshape(
        BLOCK_FRAMES, LATENT_CHANNELS, LATENT_ROWS * LATENT_COLUMNS
    )
    position = lax.axis_index("tm")
    block = position // PROMPT_SAMPLES
    sample = position % PROMPT_SAMPLES
    keep = block > 0
    earlier = from_behind(latent_volume, "tm", PROMPT_SAMPLES)
    earlier = jnp.where(keep, earlier, jnp.zeros_like(earlier))
    frames = to_cells(jnp.concatenate([earlier, latent_volume], axis=0))
    widened = (causal_conv(frames, entry_kernel) + entry_bias).astype(jnp.bfloat16)
    active_all = activate(widened, norm_scale_gain).reshape(
        BLOCK_FRAMES + 2, LATENT_ROWS, LATENT_COLUMNS, C
    )
    behind = jnp.where(keep, active_all[:2], jnp.zeros_like(active_all[:2]))
    extended = jnp.concatenate([behind, active_all[2:]], axis=0)
    stream = widened[2 * LATENT_ROWS * LATENT_COLUMNS :]
    kernel_all = lax.all_gather(residual_kernel, "tm", axis=1, tiled=True)
    branch = causal_conv(extended, kernel_all)
    total = (stream.astype(jnp.float32) + (branch + residual_bias)).reshape(
        BLOCK_FRAMES, LATENT_ROWS, LATENT_COLUMNS, C
    )
    limit = jnp.sum(jnp.where(jnp.arange(PROMPT_SAMPLES) == sample, sample_frame_count, 0))
    frame_index = block * BLOCK_FRAMES + jnp.arange(BLOCK_FRAMES)
    valid = (frame_index < limit)[:, None, None, None]
    return jnp.where(valid, total, jnp.zeros_like(total)).astype(jnp.bfloat16)


MESH = pl.DeviceIdType.MESH
F32, BF16 = jnp.float32, jnp.bfloat16
CELLS = LATENT_ROWS * LATENT_COLUMNS
PLANE = 128
HALF = 64
SLICES = 3
PAIRS = ((8, 7), (6, 5), (4, 3), (2, 1), (0,))
CHUNKS = ((0, 1), (2, 3))


def section_kernel(
    lat_far, counts_far, entry_far, entry_bias_far, gain_far, residual_bias_far, taps_far,
    out,
    counts, entry, entry_bias, gain, residual_bias, lat_raw, taps, latq, lat, at, act, kept,
    piece_a, piece_b, block_a, block_b, right, acc, done, got,
    lat_send, lat_recv, z_send, z_recv, y_send, y_recv, c_send, c_recv, o_send, o_recv, own, late,
):
    x = lax.axis_index("groups")
    me = lax.axis_index("tm")
    z, y, c = me // 4, (me // 2) % 2, me % 2
    pieces = (piece_a, piece_b)
    blocks = (block_a, block_b)

    barrier = pltpu.get_barrier_semaphore()

    @pl.when(z < SLICES)
    def _():
        for step in range(1, 16):
            pl.semaphore_signal(barrier, inc=1, device_id={"tm": lax.rem(me + step, 16)}, device_id_type=MESH)
        for step in range(16):
            pl.semaphore_signal(
                barrier, inc=1, device_id={"groups": 1 - x, "tm": lax.rem(me + step, 16)}, device_id_type=MESH
            )

    first_copies = [
        pltpu.make_async_copy(lat_far, lat_raw, own.at[0]),
        pltpu.make_async_copy(taps_far, taps, own.at[1]),
        pltpu.make_async_copy(entry_far, entry, own.at[2]),
        pltpu.make_async_copy(entry_bias_far, entry_bias, own.at[3]),
        pltpu.make_async_copy(gain_far, gain, own.at[4]),
        pltpu.make_async_copy(residual_bias_far, residual_bias, own.at[5]),
        pltpu.make_async_copy(counts_far, counts, own.at[10]),
    ]
    for copy in first_copies:
        copy.start()
    first_copies[0].wait()
    cell_rows = lat_raw[...].astype(F32)
    quads = [cell_rows[:, CELLS * q : CELLS * q + CELLS] for q in range(4)]
    quads = jnp.concatenate([jnp.concatenate([q, jnp.zeros((16, PLANE - CELLS), F32)], axis=1) for q in quads], axis=0)
    to_ = lax.broadcasted_iota(jnp.int32, (64, 64), 0)
    from_ = lax.broadcasted_iota(jnp.int32, (64, 64), 1)
    pick = from_ == (to_ % 4) * 16 + ((to_ % 16) // 8) * 8 + ((to_ // 4) % 2) * 4 + to_ // 16
    picked = jnp.dot(pick.astype(F32).astype(BF16), quads.astype(BF16), preferred_element_type=F32)
    latq[...] = picked.astype(BF16).reshape(4, 16, PLANE)
    pl.semaphore_wait(barrier, jnp.where(z < SLICES, 23, 24))

    @pl.when(z == SLICES)
    def _():
        for g in range(2):
            for n in range(SLICES):
                pl.semaphore_signal(
                    late, inc=1, device_id={"groups": g, "tm": n * 4 + y * 2 + c}, device_id_type=MESH
                )

    def remote(src, dst, send, recv, device):
        return pltpu.make_async_remote_copy(
            src_ref=src, dst_ref=dst, send_sem=send, recv_sem=recv, device_id=device, device_id_type=MESH
        )

    def columns(n):
        return pl.ds(pl.multiple_of(128 * n, 128), 128)

    def source_of(zz, yy, cc):
        return zz * 4 + yy * 2 + cc

    def lat_copy(to):
        return remote(latq.at[to % 4], lat.at[x, me], lat_send.at[to], lat_recv.at[me], {"tm": to})

    def group_copy(g):
        return remote(lat.at[g], lat.at[g], lat_send.at[12], lat_recv.at[16], {"groups": 1 - x, "tm": me})

    def z_copy(ch, n):
        return remote(
            pieces[ch].at[n], blocks[ch].at[me], z_send.at[ch, n], z_recv.at[ch, z], {"tm": source_of(n, y, c)}
        )

    def z_arrival(ch, zz):
        b = blocks[ch].at[source_of(zz, y, c)]
        return remote(b, b, z_send.at[ch, 0], z_recv.at[ch, zz], {"tm": source_of(zz, y, c)})

    def y_copy(ch, zz, source=None):
        b = blocks[ch].at[source_of(zz, y, c)]
        return remote(
            b if source is None else source, b, y_send.at[ch, zz], y_recv.at[ch, zz], {"tm": source_of(z, 1 - y, c)}
        )

    def y_arrival(ch, zz):
        b = blocks[ch].at[source_of(zz, 1 - y, c)]
        return remote(b, b, y_send.at[ch, zz], y_recv.at[ch, zz], {"tm": source_of(z, 1 - y, c)})

    def c_copy(ch, zz, yy, source=None):
        b = blocks[ch].at[source_of(zz, yy, c)]
        return remote(
            b if source is None else source, b, c_send.at[ch, zz, yy], c_recv.at[ch, zz, yy],
            {"tm": source_of(z, y, 1 - c)},
        )

    def c_arrival(ch, zz, yy):
        b = blocks[ch].at[source_of(zz, yy, 1 - c)]
        return remote(b, b, c_send.at[ch, zz, yy], c_recv.at[ch, zz, yy], {"tm": source_of(z, y, 1 - c)})

    def o_copy(g, h, b):
        return remote(
            done.at[g, h, b], got.at[z, x], o_send.at[g, h, b], o_recv.at[z, x],
            {"groups": g, "tm": source_of(2 * b + h, y, c)},
        )

    def o_arrival(n, xx):
        return remote(
            done.at[0, 0, 0], got.at[n, xx], o_send.at[0, 0, 0], o_recv.at[n, xx],
            {"groups": xx, "tm": source_of(n, y, c)},
        )

    for to in range(12):
        @pl.when(to != me)
        def _():
            lat_copy(to).start()

    first_copies[1].wait()
    keeps = (lax.broadcasted_iota(jnp.int32, (24, 128), 1) < HALF) == (x == 0)

    def halves(low, high, s):
        a = taps[low, :, 128 * s : 128 * s + 128].astype(F32)
        b = taps[high, :, 128 * s : 128 * s + 128].astype(F32)
        still = jnp.where(x == 0, a, b)
        moved = pltpu.roll(jnp.where(x == 0, b, a), HALF, 1)
        return jnp.where(keeps, still, moved).astype(BF16)

    for ch, pairs in enumerate(CHUNKS):
        for s in range(SLICES):
            if ch == 1:
                piece_b[s, 6] = halves(0, 1, s)
                piece_b[s, 7] = halves(2, 2, s)
            for n, p in enumerate(pairs):
                low, high = PAIRS[p]
                for k in range(3):
                    pieces[ch][s, 3 * n + k] = halves(3 * low + k, 3 * high + k, s)

            @pl.when(s != z)
            def _():
                z_copy(ch, s).start()

        @pl.when(z < SLICES)
        def _():
            y_copy(ch, z, pieces[ch].at[z]).start()
            c_copy(ch, z, y, pieces[ch].at[z]).start()

        if ch < 1:
            for n in range(SLICES):
                @pl.when(z == SLICES)
                def _():
                    z_copy(ch, n).wait_send()

    @pl.when(z < SLICES)
    def _():
        mine = [pltpu.make_async_copy(latq.at[me % 4], lat.at[x, me], own.at[6])]
        for ch in range(2):
            mine.append(pltpu.make_async_copy(pieces[ch].at[z], blocks[ch].at[me], own.at[7 + ch]))
        for copy in mine:
            copy.start()

        def other(step):
            return SLICES if step == 2 else step + jnp.where(step >= z, 1, 0)

        def forward(ch, *steps):
            for step in steps:
                zz = other(step)
                z_arrival(ch, zz).wait_recv()
                y_copy(ch, zz).start()
                c_copy(ch, zz, y).start()

        def across(ch, *steps):
            for step in steps:
                zz = z if step < 0 else other(step)
                y_arrival(ch, zz).wait_recv()
                c_copy(ch, zz, 1 - y).start()

        def from_sibling(ch):
            for yy in range(2):
                for zz in range(4):
                    c_arrival(ch, zz, yy).wait_recv()

        at[:, 0:2] = jnp.zeros((4, 2, 144, PLANE), BF16)

        def clear(n, carry):
            acc[n // 4, n % 4] = jnp.zeros((10, PLANE, 128), F32)
            return carry

        lax.fori_loop(0, 8, clear, 0)
        for copy in first_copies[2:]:
            copy.wait()
        for copy in mine:
            copy.wait()
        for source in range(16):
            @pl.when(source != me)
            def _():
                remote(
                    latq.at[0], lat.at[x, source], lat_send.at[0], lat_recv.at[source], {"tm": source}
                ).wait_recv()
        group_copy(x).start()
        forward(0, 0, 1)
        target = lax.broadcasted_iota(jnp.int32, (256, 256), 0)
        origin = lax.broadcasted_iota(jnp.int32, (256, 256), 1)
        h_, b_, g_, ch_ = target // 128, (target // 64) % 2, (target // 16) % 4, target % 16
        perm = (origin == (g_ * 4 + ch_ // 4) * 16 + (b_ * 2 + h_) * 4 + ch_ % 4).astype(F32).astype(BF16)
        lane = lax.broadcasted_iota(jnp.int32, (256, PLANE), 1)
        row, column = lane // LATENT_COLUMNS, lane % LATENT_COLUMNS

        def spread(g):
            cells = jnp.dot(perm, lat[g].reshape(256, PLANE), preferred_element_type=F32)
            for j in range(3):
                for k in range(3):
                    offset = (j - 1) * LATENT_COLUMNS + (k - 1)
                    moved = pltpu.roll(cells, (-offset) % PLANE, 1) if offset else cells
                    good = (
                        (row + (j - 1) >= 0)
                        & (row + (j - 1) < LATENT_ROWS)
                        & (column + (k - 1) >= 0)
                        & (column + (k - 1) < LATENT_COLUMNS)
                    )
                    tap = 3 * j + k
                    at[pl.ds(2 * g, 2), 2:, tap * 16 : tap * 16 + 16, :] = (
                        jnp.where(good, moved, 0.0).astype(BF16).reshape(2, 8, 16, PLANE)
                    )

        def inlet(index, carry):
            h, b = index // 2, index % 2
            left = jnp.concatenate([at[h, pl.ds(4 * b + q, 3)].reshape(432, PLANE) for q in range(4)], axis=1)
            wide = lax.dot_general(left, entry[...], (((0,), (0,)), ((), ())), preferred_element_type=F32)
            wide = wide.reshape(4, PLANE, C)[:, :CELLS].reshape(4 * CELLS, C)
            stream = (wide + entry_bias[...][None, :]).astype(BF16)
            kept[index] = stream
            values = stream.astype(F32)
            scale = lax.rsqrt(jnp.mean(values * values, axis=-1, keepdims=True) + 1e-06)
            half_u = values * scale * (0.5 * gain[...])[None, :]
            active = (half_u + half_u * jnp.tanh(half_u)).astype(BF16).astype(F32)
            column = lax.broadcasted_iota(jnp.int32, (4 * CELLS, C), 0) % LATENT_COLUMNS
            before = jnp.where(column == 0, 0.0, pltpu.roll(active, 1, 0))
            behind = jnp.where(column == LATENT_COLUMNS - 1, 0.0, pltpu.roll(active, 4 * CELLS - 1, 0))
            for k, moved in enumerate((before, active, behind)):
                act[h, pl.ds(4 * b, 4), :, k * C : k * C + C] = moved.astype(BF16).reshape(4, CELLS, C)
            return carry

        def prepare_last():
            for n in range(2):
                piece = block_b[:, 6 + n].astype(F32).reshape(C, 128).astype(BF16)
                right[2, :C, 128 * n : 128 * n + 128] = piece

        def sweep_last(h):
            left = act[h, :6, :, C : 2 * C].reshape(6 * CELLS, C)
            wide = jnp.dot(left, right[2, :C], preferred_element_type=F32)
            column = lax.broadcasted_iota(jnp.int32, (6 * CELLS, 128), 0) % LATENT_COLUMNS
            before = jnp.where(column == 0, 0.0, pltpu.roll(wide[:, :128], 1, 0))
            behind = jnp.where(column == LATENT_COLUMNS - 1, 0.0, pltpu.roll(wide[:, 128:], 6 * CELLS - 1, 0))
            acc[0, h, 2:8, 32 : 32 + CELLS] += (before + behind).reshape(6, CELLS, 128)
            acc[1, h, 2:8, 32 : 32 + CELLS] += wide[:, :128].reshape(6, CELLS, 128)

        def prepare(ch):
            for n in range(len(CHUNKS[ch])):
                for k in range(3):
                    piece = blocks[ch][:, 3 * n + k].astype(F32).reshape(C, 128).astype(BF16)
                    right[ch, k * C : k * C + C, n * 128 : n * 128 + 128] = piece

        def sweep(h, ch, frames):
            pairs = CHUNKS[ch]
            left = act[h, :frames].reshape(frames * CELLS, 3 * C)
            wide = jnp.dot(left, right[ch, :, : 128 * len(pairs)], preferred_element_type=F32)
            for n, p in enumerate(pairs):
                part = wide[:, 128 * n : 128 * n + 128].reshape(frames, CELLS, 128)
                for side, slot in enumerate(PAIRS[p]):
                    i, j = slot // 3, slot % 3
                    acc[side, h, 2 - i : 2 - i + frames, 16 * (2 - j) : 16 * (2 - j) + CELLS] += part

        def both_groups(step, carry):
            g = jnp.where(step == 0, x, 1 - x)

            @pl.when(step == 1)
            def _():
                group_copy(g).wait_recv()

            spread(g)

            @pl.when(step == 0)
            def _():
                forward(1, 0, 1)

            lax.fori_loop(4 * g, 4 * g + 2, inlet, 0)

            @pl.when(step == 0)
            def _():
                forward(0, 2)
                across(0, -1, 0, 1)

            @pl.when(step == 1)
            def _():
                across(0, 2)
                across(1, 0, 1)

            lax.fori_loop(4 * g + 2, 4 * g + 4, inlet, 0)

            @pl.when(step == 0)
            def _():
                forward(1, 2)
                across(1, -1)

            return carry

        lax.fori_loop(0, 2, both_groups, 0)
        across(1, 2)
        from_sibling(0)
        prepare(0)

        def first(step, carry):
            sweep(2 * step + 1, 0, 8)
            return carry

        lax.fori_loop(0, 2, first, 0)
        from_sibling(1)
        prepare(1)
        prepare_last()
        pl.semaphore_wait(late, 2)
        edge = lax.broadcasted_iota(jnp.int32, (2, CELLS, 128), 2) < HALF
        bias = residual_bias[columns(z)][None, :]
        bias = jnp.where(x == 0, bias, pltpu.roll(jnp.broadcast_to(bias, (8, 128)), HALF, 1)[:1])

        def finish(step, carry):
            g, h = step % 2, 1 - step // 2
            gh = 2 * g + h

            @pl.when(step >= 2)
            def _():
                sweep(gh, 0, 8)

            sweep(gh, 1, 7)
            sweep_last(gh)
            for b in (1, 0):
                stream = kept[2 * gh + b, :, columns(z)].astype(F32)
                stream = jnp.where(x == 0, stream, pltpu.roll(stream, HALF, 1))
                even = acc[0, gh, 4 * b : 4 * b + 4, 16 : 16 + CELLS].reshape(4 * CELLS, 128)
                odd = acc[1, gh, 4 * b : 4 * b + 4, 16 : 16 + CELLS].reshape(4 * CELLS, 128)
                total = stream + (even + pltpu.roll(odd, HALF, 1) + bias)
                top = total[: 2 * CELLS].reshape(2, CELLS, 128)
                low = pltpu.roll(total[2 * CELLS :], HALF, 1).reshape(2, CELLS, 128)
                done[g, h, b] = jnp.where(edge, top, low).astype(BF16).reshape(2 * CELLS, 128)

                @pl.when((g != x) | (2 * b + h != z))
                def _():
                    o_copy(g, h, b).start()

            return carry

        lax.fori_loop(0, 4, finish, 0)
        got[z, x] = done[x, z % 2, z // 2]

    for n in range(SLICES):
        for xx in range(2):
            @pl.when((n != z) | (xx != x))
            def _():
                o_arrival(n, xx).wait_recv()
    @pl.when(z == SLICES)
    def _():
        for copy in first_copies[2:]:
            copy.wait()

    limit = counts[me % PROMPT_SAMPLES]
    frame = lax.broadcasted_iota(jnp.int32, (2, CELLS, 128), 0) + BLOCK_FRAMES * (me // PROMPT_SAMPLES)
    half = lax.broadcasted_iota(jnp.int32, (2, CELLS, 128), 2) < HALF
    for n in range(SLICES):
        near_half = got[n, 0].astype(F32)
        far_half = got[n, 1].astype(F32)
        top = jnp.where(half, near_half.reshape(2, CELLS, 128), pltpu.roll(far_half, HALF, 1).reshape(2, CELLS, 128))
        low = jnp.where(half, pltpu.roll(near_half, HALF, 1).reshape(2, CELLS, 128), far_half.reshape(2, CELLS, 128))
        for first_frame, values in ((0, top), (2, low)):
            values = jnp.where(frame + first_frame < limit, values, 0.0).astype(BF16)
            out[CELLS * first_frame : CELLS * (first_frame + 2), 128 * n : 128 * n + 128] = values.reshape(2 * CELLS, 128)

    for n in range(SLICES):
        @pl.when(n != z)
        def _():
            z_copy(1, n).wait_send()

            @pl.when(z < SLICES)
            def _():
                z_copy(0, n).wait_send()

    for to in range(12):
        @pl.when(to != me)
        def _():
            lat_copy(to).wait_send()

    @pl.when(z < SLICES)
    def _():
        group_copy(x).wait_send()
        for ch in range(2):
            for zz in range(4):
                y_copy(ch, zz).wait_send()
                for yy in range(2):
                    c_copy(ch, zz, yy).wait_send()
        for g in range(2):
            for h in range(2):
                for b in range(2):
                    @pl.when((g != x) | (2 * b + h != z))
                    def _():
                        o_copy(g, h, b).wait_send()


def sliced_shards(
    sharded_latents,
    sample_frame_count,
    entry_kernel,
    entry_bias,
    norm_scale_gain,
    residual_kernel,
    residual_bias,
):
    vmem = pl.BlockSpec(memory_space=pltpu.VMEM)
    far = pl.BlockSpec(memory_space=pltpu.HBM)
    dma = pltpu.SemaphoreType.DMA
    pairs = (6, 8)
    out = pl.pallas_call(
        section_kernel,
        out_shape=jax.ShapeDtypeStruct((4 * CELLS, C), BF16),
        in_specs=[far] * 7,
        out_specs=vmem,
        scratch_shapes=[
            pltpu.SMEM((PROMPT_SAMPLES,), jnp.int32),
            pltpu.VMEM((27 * LATENT_CHANNELS, C), BF16),
            pltpu.VMEM((C,), F32), pltpu.VMEM((C,), F32), pltpu.VMEM((C,), F32),
            pltpu.VMEM((16, 4 * CELLS), BF16),
            pltpu.VMEM((27, 24, C), BF16),
            pltpu.VMEM((4, 16, PLANE), BF16),
            pltpu.VMEM((2, 16, 16, PLANE), BF16),
            pltpu.VMEM((4, 10, 144, PLANE), BF16),
            pltpu.VMEM((4, 8, CELLS, 3 * C), BF16),
            pltpu.VMEM((8, 4 * CELLS, C), BF16),
        ]
        + [pltpu.VMEM((SLICES, n, 24, 128), BF16) for n in pairs]
        + [pltpu.VMEM((16, n, 24, 128), BF16) for n in pairs]
        + [
            pltpu.VMEM((3, 3 * C, 256), BF16),
            pltpu.VMEM((2, 4, 10, PLANE, 128), F32),
            pltpu.VMEM((2, 2, 2, 2 * CELLS, 128), BF16),
            pltpu.VMEM((SLICES, 2, 2 * CELLS, 128), BF16),
            dma((13,)), dma((17,)), dma((3, 3)), dma((3, 4)), dma((3, 4)), dma((3, 4)),
            dma((3, 4, 2)), dma((3, 4, 2)), dma((2, 2, 2)), dma((3, 2)), dma((11,)), pltpu.SemaphoreType.REGULAR,
        ],
        compiler_params=pltpu.CompilerParams(
            collective_id=0, has_side_effects=True, vmem_limit_bytes=56 * 1024 * 1024
        ),
        cost_estimate=pl.CostEstimate(flops=5_000_000_000, bytes_accessed=2_000_000, transcendentals=600_000),
    )(
        sharded_latents,
        sample_frame_count,
        entry_kernel.reshape(27 * LATENT_CHANNELS, C),
        entry_bias,
        norm_scale_gain,
        residual_bias,
        residual_kernel,
    )
    return out.reshape(4, LATENT_ROWS, LATENT_COLUMNS, C)


def solution(mesh):
    in_specs = (P("groups", "tm"), P("groups"), P(), P(), P(), P(None, "tm", None), P())
    out_specs = P(("groups", "tm"), None, None, None)
    sliced = mesh.shape["groups"] == 2 and mesh.shape["tm"] == 16
    body = sliced_shards if sliced else shards
    return jax.shard_map(body, mesh=mesh, in_specs=in_specs, out_specs=out_specs, check_vma=False)
```
